32 devices in a mesh: blk: 32 (over z, y, x, core).
Axes of the slice: x: 2, y: 2, z: 4, core: 2. Of those that a mesh axis runs over, the one named last changes fastest.
Arguments:
- right_side: float32 [4096, 128], P('blk')
- kernel_tiles: float32 [32, 17, 128, 128], P('blk'), as said below
- route_pairs: int32 [17, 2], replicated, may hold values from 0 to 10, as said below
Outputs:
- solution: float32 [4096, 128], P('blk')
- residual: float32 [4096, 128], P('blk')
The draws below stay inside these ranges and needn't reach their ends.
Inputs may be any that keep to these rules, and one draw needn't show every extreme that they name: For every row t, cover[route_pairs[t,1]] - cover[route_pairs[t,0]] is congruent to t modulo 32, with cover as in the reference program. kernel_tiles makes K symmetric with a positive diagonal of about 1 to 16 inside the diagonal tiles; K is positive definite.
All inputs are finite; a program needn't handle non-finite values.
Results may differ from the reference program's by a relative error of at most 0.0003.
Values sent between devices are 32-bit elements; how exact they have to be, the bound alone decides.
No kernel may reach another device: no remote copies, remote signals or barrier semaphores. Data moves between devices by JAX's collectives and lax.ppermute only.
A program may use at most 128 MiB of HBM per device.

```python
import math
import jax
import jax.numpy as jnp
import numpy as np
from jax import lax

B = 128
R = 128
ITERS = 1
NB = 32
N = 4096
NT = 17
SPAN = 8


def draw_right_side(key, part):
    rows = jnp.arange(N, dtype=jnp.int32) // B
    factor = 0.6 + 1.2 * rows.astype(jnp.float32) / (NB - 1)
    values = jnp.clip(jax.random.normal(key, (N, R), jnp.float32), -6.0, 6.0)
    return values * factor[:, None]


def draw_kernel_tiles(key, part):
    entry_scale = 0.52 / math.sqrt(N)
    first_key = jax.random.fold_in(key, 11)
    second_key = jax.random.fold_in(key, 12)
    entries = jax.random.uniform(first_key, (NB, NT, B, B), jnp.float32, -entry_scale, entry_scale)
    ridge = jnp.exp(jax.random.uniform(second_key, (NB, B), jnp.float32, 0.0, math.log(4.0)))
    center = entries[:, 0]
    center = 0.5 * (center + jnp.swapaxes(center, 1, 2)) + ridge[:, :, None] * jnp.eye(B, dtype=jnp.float32)[None]
    upper = entries[:, NT - 1]
    flipped = jnp.swapaxes(jnp.roll(upper, NB // 2, axis=0), 1, 2)
    owner_ids = jnp.arange(NB, dtype=jnp.int32)[:, None, None]
    far_tile = jnp.where(owner_ids >= NB // 2, flipped, upper)
    return entries.at[:, 0].set(center).at[:, NT - 1].set(far_tile)


def draw_route_pairs(key, part):
    cover_set = np.array([k for k in range(SPAN)] + [k * SPAN for k in range(1, NB // SPAN)], dtype=np.int64)
    cover_len = cover_set.shape[0]
    distance = (cover_set[None, :] - cover_set[:, None]) % NB
    distances = jnp.array(distance.reshape(-1), dtype=jnp.int32)
    scores = jax.random.randint(key, (NT, cover_len * cover_len), 0, 1 << 20) * (cover_len * cover_len)
    scores = scores + jnp.arange(cover_len * cover_len, dtype=jnp.int32)[None, :]
    usable = distances[None, :] == jnp.arange(NT, dtype=jnp.int32)[:, None]
    scores = jnp.where(usable, scores, -1)
    _, chosen = lax.top_k(scores, 1)
    chosen = chosen[:, 0].astype(jnp.int32)
    return jnp.stack([chosen // cover_len, chosen % cover_len], axis=1).astype(jnp.int32)


def setup_inputs(seed: int = 0) -> dict:
    key_of = jax.random.split(jax.random.key(seed), 4)
    return {
        "right_side": draw_right_side(jax.random.fold_in(key_of[3], 71), 0),
        "kernel_tiles": draw_kernel_tiles(jax.random.fold_in(key_of[3], 71), 0),
        "route_pairs": draw_route_pairs(jax.random.fold_in(key_of[3], 71), 0),
    }


def cover_offsets():
    return [k for k in range(SPAN)] + [k * SPAN for k in range(1, NB // SPAN)]


def apply_kernel(kernel_tiles, route_pairs, vector):
    cover_set = jnp.array(cover_offsets(), dtype=jnp.int32)
    row_off = cover_set[route_pairs[:, 0]]
    col_off = cover_set[route_pairs[:, 1]]
    slot_ids = jnp.arange(NT, dtype=jnp.int32)
    mirror = ((slot_ids > 0) & (slot_ids < NT - 1)).astype(vector.dtype)

    def visit_owner(summed, entry_pair):
        tile_set, owner_id = entry_pair
        row_blk = ((owner_id + row_off) % NB).astype(jnp.int32)
        col_blk = ((owner_id + col_off) % NB).astype(jnp.int32)
        by_row = jnp.einsum("tij,tjr->tir", tile_set, vector[col_blk], precision=lax.Precision.HIGHEST)
        by_col = jnp.einsum("tji,tjr->tir", tile_set, vector[row_blk], precision=lax.Precision.HIGHEST)
        by_col = by_col * mirror[:, None, None]
        summed = summed.at[row_blk].add(by_row).at[col_blk].add(by_col)
        return summed, None

    summed, _ = lax.scan(visit_owner, jnp.zeros_like(vector), (kernel_tiles, jnp.arange(NB, dtype=jnp.int32)))
    return summed


def reference(right_side, kernel_tiles, route_pairs):
    rhs_blocks = right_side.reshape(NB, B, R)
    solution = jnp.zeros_like(rhs_blocks)
    residual = rhs_blocks
    direction = rhs_blocks
    norm_now = jnp.sum(residual * residual, axis=(0, 1))
    for step in range(ITERS):
        image = apply_kernel(kernel_tiles, route_pairs, direction)
        step_len = norm_now / jnp.sum(direction * image, axis=(0, 1))
        solution = solution + step_len * direction
        residual = residual - step_len * image
        norm_next = jnp.sum(residual * residual, axis=(0, 1))
        direction = residual + (norm_next / norm_now) * direction
        norm_now = norm_next
    return solution.reshape(N, R), residual.reshape(N, R)
```

```python
import functools

import jax
import jax.numpy as jnp
from jax import lax
from jax.experimental import pallas as pl
from jax.experimental.pallas import tpu as pltpu
from jax.sharding import PartitionSpec as P

EXTRA = 8
VMEM_BYTES = 32 * 1024 * 1024


def shifted(value, steps):
    count = lax.axis_size("blk")
    pairs = [(source, (source + steps) % count) for source in range(count)]
    return lax.ppermute(value, "blk", pairs)


def within_plane(value, window, chips_ahead):
    count = lax.axis_size("blk")
    pairs = []
    for source in range(count):
        plane, place = divmod(source, window)
        pairs.append((source, plane * window + (place + 2 * chips_ahead) % window))
    return lax.ppermute(value, "blk", pairs)


def core_partner(value):
    count = lax.axis_size("blk")
    return lax.ppermute(value, "blk", [(source, source ^ 1) for source in range(count)])


def split_two(values):
    high = values.astype(jnp.bfloat16)
    low = (values - high.astype(jnp.float32)).astype(jnp.bfloat16)
    return high, low


def product_kernel(planes, chips, pairs_ref, core_ref, own_ref, *refs):
    window = 2 * chips
    far = refs[: planes - 1]
    even = refs[planes - 1 : planes + chips - 2]
    odd_ref, tiles_ref = refs[planes + chips - 2 : planes + chips]
    outs = refs[planes + chips :]
    message_ref, kept_ref = outs[:2]
    far_out = outs[2:planes]
    whole, parts, total = outs[planes:]
    rows, cols = own_ref.shape
    core = core_ref[0]

    def put(place, values):
        whole[place] = values
        high, low = split_two(values)
        parts[place, :, :cols] = high
        parts[place, :, cols:] = low

    put(0, own_ref[...])
    for k in range(1, planes):
        put(window - 1 + k, far[k - 1][...])
    for m in range(1, chips):
        put(2 * m, even[m - 1][...])
        put(2 * m + 1 - 2 * core, odd_ref[(m - 1) * rows : m * rows, :])
    put(jnp.where(core == 0, 1, window - 1), odd_ref[(chips - 1) * rows : chips * rows, :])

    total[...] = jnp.zeros_like(total)
    slots = tiles_ref.shape[0]

    def product(tile, place):
        high, low = split_two(tile)
        both = jnp.dot(high, parts[place], preferred_element_type=jnp.float32)
        rest = jnp.dot(low, parts[place, :, :cols], preferred_element_type=jnp.float32)
        return both[:, :cols] + (both[:, cols:] + rest)

    def visit(t, mirrored):
        row_place, col_place = pairs_ref[t, 0], pairs_ref[t, 1]
        tile = tiles_ref[t]
        total[row_place] += product(tile, col_place)
        if mirrored:
            total[col_place] += product(tile.T, row_place)

    visit(0, False)
    if slots <= 32:
        for t in range(1, slots - 1):
            visit(t, True)
    else:
        lax.fori_loop(1, slots - 1, lambda t, c: (visit(t, True), c)[1], 0)
    visit(slots - 1, False)

    dots = jnp.zeros((1, cols), jnp.float32)
    for place in range(whole.shape[0]):
        dots = dots + jnp.sum(whole[place] * total[place], axis=0, keepdims=True)
    own = own_ref[...]
    norm = jnp.sum(own * own, axis=0, keepdims=True)
    for m in range(1, chips):
        message_ref[(m - 1) * rows : m * rows, :] = total[2 * m + 1 - 2 * core]
    message_ref[(chips - 1) * rows : chips * rows, :] = total[jnp.where(core == 0, 1, window - 1)]
    message_ref[chips * rows :, :] = jnp.concatenate([norm, dots, jnp.zeros((EXTRA - 2, cols), jnp.float32)], axis=0)
    for m in range(chips):
        kept_ref[m] = total[2 * m]
    kept_ref[chips] = total[window]
    for k in range(2, planes):
        far_out[k - 2][...] = total[window - 1 + k]


def pair_kernel(chips, core_ref, sent_ref, kept_ref, got_ref, *outs):
    messages = outs[: chips - 1]
    near_ref, next_ref, sums_ref = outs[chips - 1 :]
    rows = kept_ref.shape[1]
    core = core_ref[0]
    sums = sent_ref[chips * rows :, :] + got_ref[chips * rows :, :]
    for m in range(1, chips):
        messages[m - 1][:rows, :] = kept_ref[m] + got_ref[(m - 1) * rows : m * rows, :]
        messages[m - 1][rows:, :] = sums
    spare = got_ref[(chips - 1) * rows : chips * rows, :]
    near_ref[...] = kept_ref[0] + jnp.where(core == 1, spare, 0.0)
    next_ref[...] = kept_ref[chips] + jnp.where(core == 0, spare, 0.0)
    sums_ref[...] = sums


def plane_kernel(planes, chips, chip_ref, near_ref, next_ref, sums_ref, *refs):
    got = refs[: chips - 1]
    far = refs[chips - 1 : chips + planes - 3]
    near_out = refs[chips + planes - 3]
    messages = refs[chips + planes - 2 : chips + 2 * planes - 3]
    sums_out = refs[chips + 2 * planes - 3]
    rows = near_ref.shape[0]
    chip = chip_ref[0]
    near, ahead, sums = near_ref[...], next_ref[...], sums_ref[...]
    for m in range(1, chips):
        block = got[m - 1][:rows, :]
        near = near + jnp.where(chip >= m, block, 0.0)
        ahead = ahead + jnp.where(chip >= m, 0.0, block)
        sums = sums + got[m - 1][rows:, :]
    near_out[...] = near
    sums_out[...] = sums
    messages[0][:rows, :] = ahead
    for k in range(2, planes):
        messages[k - 1][:rows, :] = far[k - 2][...]
    for k in range(1, planes):
        messages[k - 1][rows:, :] = sums


def final_kernel(planes, right_ref, near_ref, sums_ref, *refs):
    got = refs[: planes - 1]
    solution_ref, residual_ref = refs[planes - 1 :]
    rows = near_ref.shape[0]
    image, sums = near_ref[...], sums_ref[...]
    for k in range(1, planes):
        image = image + got[k - 1][:rows, :]
        sums = sums + got[k - 1][rows:, :]
    step_len = sums[0:1, :] / sums[1:2, :]
    right = right_ref[...]
    solution_ref[...] = step_len * right
    residual_ref[...] = right - step_len * image


def call(kernel, smem, operands, outs, scratch=()):
    vmem = pl.BlockSpec(memory_space=pltpu.VMEM)
    return pl.pallas_call(
        kernel,
        in_specs=[pl.BlockSpec(memory_space=pltpu.SMEM)] * len(smem) + [vmem] * len(operands),
        out_specs=[vmem] * len(outs),
        out_shape=[jax.ShapeDtypeStruct(shape, jnp.float32) for shape in outs],
        scratch_shapes=list(scratch),
        compiler_params=pltpu.CompilerParams(vmem_limit_bytes=VMEM_BYTES),
    )(*smem, *operands)


def per_device(right_side, kernel_tiles, route_pairs):
    count = lax.axis_size("blk")
    window = max(8, min(16, count // 8))
    planes, chips = count // window, window // 2
    rows, cols = right_side.shape
    cover_len = window + planes - 1
    place = lax.axis_index("blk")
    core = (place % 2).astype(jnp.int32)
    chip = (place % window // 2).astype(jnp.int32)

    far = [shifted(right_side, -k * window) for k in range(1, planes)]
    even = []
    for m in range(1, chips):
        sent = jnp.where(chip >= m, right_side, far[0])
        even.append(within_plane(sent, window, -m))
    odd = core_partner(jnp.concatenate(even + [jnp.where(core == 0, far[0], right_side)], axis=0))

    block, marked = (rows, cols), (rows + EXTRA, cols)
    sent, kept, *far_out = call(
        functools.partial(product_kernel, planes, chips),
        (route_pairs, core[None]),
        (right_side, *far, *even, odd, kernel_tiles[0]),
        [(chips * rows + EXTRA, cols), (chips + 1, rows, cols)] + [block] * (planes - 2),
        (
            pltpu.VMEM((cover_len, rows, cols), jnp.float32),
            pltpu.VMEM((cover_len, rows, 2 * cols), jnp.bfloat16),
            pltpu.VMEM((cover_len, rows, cols), jnp.float32),
        ),
    )
    got = core_partner(sent)
    *messages, near, ahead, sums = call(
        functools.partial(pair_kernel, chips),
        (core[None],),
        (sent, kept, got),
        [marked] * (chips - 1) + [block, block, (EXTRA, cols)],
    )
    got = [within_plane(messages[m - 1], window, m) for m in range(1, chips)]
    near, *messages, sums = call(
        functools.partial(plane_kernel, planes, chips),
        (chip[None],),
        (near, ahead, sums, *got, *far_out),
        [block] + [marked] * (planes - 1) + [(EXTRA, cols)],
    )
    got = [shifted(messages[k - 1], k * window) for k in range(1, planes)]
    solution, residual = call(
        functools.partial(final_kernel, planes),
        (),
        (right_side, near, sums, *got),
        [block, block],
    )
    return solution, residual


def solution(mesh):
    return jax.shard_map(
        per_device,
        mesh=mesh,
        in_specs=(P("blk", None), P("blk", None, None, None), P()),
        out_specs=(P("blk", None), P("blk", None)),
        check_vma=False,
    )
```

```python
import functools

import jax
import jax.numpy as jnp
from jax import lax
from jax.experimental import pallas as pl
from jax.experimental.pallas import tpu as pltpu
from jax.sharding import PartitionSpec as P

EXTRA = 8
VMEM_BYTES = 48 * 1024 * 1024


def split_two(values):
    high = values.astype(jnp.bfloat16)
    low = (values - high.astype(jnp.float32)).astype(jnp.bfloat16)
    return high, low


def product_kernel(cover, pairs_ref, place_ref, blocks_ref, tiles_ref, out_ref, parts):
    count, marked, cols = out_ref.shape
    rows = marked - EXTRA
    place = place_ref[0]
    slots = tiles_ref.shape[0]

    def at(offset):
        return lax.rem(place + offset, count)

    def block_of(position):
        window = len(cover) - (count // (cover[-1] - cover[-2])) + 1
        offset = jnp.where(position < window, position, (position - window + 1) * window)
        return at(offset)

    out_ref[...] = jnp.zeros_like(out_ref)
    for position, offset in enumerate(cover):
        high, low = split_two(blocks_ref[at(offset)])
        parts[position, :, :cols] = high
        parts[position, :, cols:] = low

    def product(tile, position):
        high, low = split_two(tile)
        both = jnp.dot(high, parts[position], preferred_element_type=jnp.float32)
        rest = jnp.dot(low, parts[position, :, :cols], preferred_element_type=jnp.float32)
        return both[:, :cols] + (both[:, cols:] + rest)

    def visit(t, mirrored):
        row_place, col_place = pairs_ref[0, t], pairs_ref[1, t]
        tile = tiles_ref[t]
        out_ref[block_of(row_place), :rows, :] += product(tile, col_place)
        if mirrored:
            out_ref[block_of(col_place), :rows, :] += product(tile.T, row_place)

    visit(0, False)
    if slots <= 32:
        for t in range(1, slots - 1):
            visit(t, True)
    else:
        lax.fori_loop(1, slots - 1, lambda t, c: (visit(t, True), c)[1], 0)
    visit(slots - 1, False)

    dots = jnp.zeros((1, cols), jnp.float32)
    for offset in cover:
        block = at(offset)
        dots = dots + jnp.sum(blocks_ref[block] * out_ref[block, :rows, :], axis=0, keepdims=True)
    own = blocks_ref[place]
    norm = jnp.sum(own * own, axis=0, keepdims=True)
    sums = jnp.concatenate([norm, dots, jnp.zeros((EXTRA - 2, cols), jnp.float32)], axis=0)
    for block in range(count):
        out_ref[block, rows:, :] = sums


def final_kernel(right_ref, image_ref, solution_ref, residual_ref):
    rows = right_ref.shape[0]
    step_len = image_ref[rows : rows + 1, :] / image_ref[rows + 1 : rows + 2, :]
    right = right_ref[...]
    solution_ref[...] = step_len * right
    residual_ref[...] = right - step_len * image_ref[:rows, :]


def call(kernel, smem, operands, outs, scratch=()):
    vmem = pl.BlockSpec(memory_space=pltpu.VMEM)
    return pl.pallas_call(
        kernel,
        in_specs=[pl.BlockSpec(memory_space=pltpu.SMEM)] * len(smem) + [vmem] * len(operands),
        out_specs=[vmem] * len(outs),
        out_shape=[jax.ShapeDtypeStruct(shape, jnp.float32) for shape in outs],
        scratch_shapes=list(scratch),
        compiler_params=pltpu.CompilerParams(vmem_limit_bytes=VMEM_BYTES),
    )(*smem, *operands)


def per_device(right_side, kernel_tiles, route_pairs):
    count = lax.axis_size("blk")
    window = max(8, min(16, count // 8))
    cover = list(range(window)) + [k * window for k in range(1, count // window)]
    rows, cols = right_side.shape
    place = lax.axis_index("blk").astype(jnp.int32)
    blocks = lax.all_gather(right_side, "blk")
    (partial,) = call(
        functools.partial(product_kernel, cover),
        (route_pairs.T, place[None]),
        (blocks, kernel_tiles[0]),
        [(count, rows + EXTRA, cols)],
        (pltpu.VMEM((len(cover), rows, 2 * cols), jnp.bfloat16),),
    )
    image = lax.psum_scatter(partial, "blk", scatter_dimension=0)
    solution, residual = call(final_kernel, (), (right_side, image), [(rows, cols), (rows, cols)])
    return solution, residual


def solution(mesh):
    return jax.shard_map(
        per_device,
        mesh=mesh,
        in_specs=(P("blk", None), P("blk", None, None, None), P()),
        out_specs=(P("blk", None), P("blk", None)),
        check_vma=False,
    )
```

```python
import functools

import jax
import jax.numpy as jnp
from jax import lax
from jax.experimental import pallas as pl
from jax.experimental.pallas import tpu as pltpu
from jax.sharding import PartitionSpec as P

EXTRA = 8
VMEM_BYTES = 48 * 1024 * 1024


def core_partner(value):
    count = lax.axis_size("blk")
    return lax.ppermute(value, "blk", [(source, source ^ 1) for source in range(count)])


def exchange_in_plane(value, window):
    count = lax.axis_size("blk")
    groups = [
        [plane * window + 2 * chip + core for chip in range(window // 2)]
        for plane in range(count // window)
        for core in range(2)
    ]
    return lax.all_to_all(value, "blk", 0, 0, axis_index_groups=groups)


def exchange_planes(value, window):
    count = lax.axis_size("blk")
    groups = [[plane * window + place for plane in range(count // window)] for place in range(window)]
    return lax.all_to_all(value, "blk", 0, 0, axis_index_groups=groups)


def split_two(values):
    high = values.astype(jnp.bfloat16)
    low = (values - high.astype(jnp.float32)).astype(jnp.bfloat16)
    return high, low


def around(start, steps, count):
    return lax.rem(start + steps, count)


def split_kernel(tiles_ref, straight_ref, turned_ref):
    slots = tiles_ref.shape[0]

    def visit(t):
        tile = tiles_ref[t]
        straight_ref[t, 0], straight_ref[t, 1] = split_two(tile)
        turned_ref[t, 0], turned_ref[t, 1] = split_two(tile.T)

    if slots <= 32:
        for t in range(slots):
            visit(t)
    else:
        lax.fori_loop(0, slots, lambda t, c: (visit(t), c)[1], 0)


def product_kernel(
    planes, chips, pairs_ref, where_ref, own_ref, far_ref, even_ref, odd_ref, straight_ref, turned_ref,
    message_ref, kept_ref, far_out, whole, parts, total,
):
    window = 2 * chips
    rows, cols = own_ref.shape
    plane, chip, core = where_ref[0], where_ref[1], where_ref[2]
    spare = jnp.where(core == 0, 1, window - 1)

    def put(place, values):
        whole[place] = values
        high, low = split_two(values)
        parts[place, :, :cols] = high
        parts[place, :, cols:] = low

    put(0, own_ref[...])
    for k in range(1, planes):
        put(window - 1 + k, far_ref[around(plane, k, planes)])
    for m in range(1, chips):
        source = around(chip, m, chips)
        put(2 * m, even_ref[source])
        put(2 * m + 1 - 2 * core, odd_ref[source])
    put(spare, odd_ref[chip])

    total[...] = jnp.zeros_like(total)
    slots = straight_ref.shape[0]

    def product(split_ref, t, place):
        both = jnp.dot(split_ref[t, 0], parts[place], preferred_element_type=jnp.float32)
        rest = jnp.dot(split_ref[t, 1], parts[place, :, :cols], preferred_element_type=jnp.float32)
        return both[:, :cols] + (both[:, cols:] + rest)

    def visit(t, mirrored):
        row_place, col_place = pairs_ref[0, t], pairs_ref[1, t]
        total[row_place] += product(straight_ref, t, col_place)
        if mirrored:
            total[col_place] += product(turned_ref, t, row_place)

    visit(0, False)
    if slots <= 32:
        for t in range(1, slots - 1):
            visit(t, True)
    else:
        lax.fori_loop(1, slots - 1, lambda t, c: (visit(t, True), c)[1], 0)
    visit(slots - 1, False)

    dots = jnp.zeros((1, cols), jnp.float32)
    for place in range(whole.shape[0]):
        dots = dots + jnp.sum(whole[place] * total[place], axis=0, keepdims=True)
    own = own_ref[...]
    norm = jnp.sum(own * own, axis=0, keepdims=True)
    sums = jnp.concatenate([norm, dots, jnp.zeros((EXTRA - 2, cols), jnp.float32)], axis=0)
    for m in range(1, chips):
        message_ref[around(chip, m, chips), :rows, :] = total[2 * m + 1 - 2 * core]
    message_ref[chip, :rows, :] = total[spare]
    for m in range(chips):
        message_ref[m, rows:, :] = sums
        kept_ref[m] = total[2 * m]
    kept_ref[chips] = total[window]
    for k in range(2, planes):
        far_out[k - 2] = total[window - 1 + k]


def pair_kernel(chips, where_ref, sent_ref, kept_ref, got_ref, message_ref, ahead_ref):
    rows = kept_ref.shape[1]
    chip, core = where_ref[1], where_ref[2]
    sums = sent_ref[0, rows:, :] + got_ref[0, rows:, :]
    for m in range(1, chips):
        target = around(chip, m, chips)
        message_ref[target, :rows, :] = kept_ref[m] + got_ref[target, :rows, :]
    spare = got_ref[chip, :rows, :]
    message_ref[chip, :rows, :] = kept_ref[0] + jnp.where(core == 1, spare, 0.0)
    ahead_ref[...] = kept_ref[chips] + jnp.where(core == 0, spare, 0.0)
    for m in range(chips):
        message_ref[m, rows:, :] = sums


def plane_kernel(planes, chips, where_ref, ahead_ref, got_ref, far_ref, message_ref):
    rows, cols = ahead_ref.shape
    plane, chip = where_ref[0], where_ref[1]
    near, ahead, sums = got_ref[chip, :rows, :], ahead_ref[...], got_ref[chip, rows:, :]
    for m in range(1, chips):
        source = around(chip, m, chips)
        block = got_ref[source, :rows, :]
        near = near + jnp.where(source < chip, block, 0.0)
        ahead = ahead + jnp.where(source < chip, 0.0, block)
        sums = sums + got_ref[source, rows:, :]
    message_ref[plane, :rows, :] = near
    message_ref[around(plane, 1, planes), :rows, :] = ahead
    for k in range(2, planes):
        message_ref[around(plane, k, planes), :rows, :] = far_ref[k - 2]
    for k in range(planes):
        message_ref[k, rows:, :] = sums


def final_kernel(right_ref, got_ref, solution_ref, residual_ref):
    rows = right_ref.shape[0]
    both = got_ref[0]
    for k in range(1, got_ref.shape[0]):
        both = both + got_ref[k]
    step_len = both[rows : rows + 1, :] / both[rows + 1 : rows + 2, :]
    right = right_ref[...]
    solution_ref[...] = step_len * right
    residual_ref[...] = right - step_len * both[:rows, :]


def call(kernel, smem, operands, outs, scratch=()):
    vmem = pl.BlockSpec(memory_space=pltpu.VMEM)
    return pl.pallas_call(
        kernel,
        in_specs=[pl.BlockSpec(memory_space=pltpu.SMEM)] * len(smem) + [vmem] * len(operands),
        out_specs=[vmem] * len(outs),
        out_shape=[jax.ShapeDtypeStruct(shape, kind) for shape, kind in outs],
        scratch_shapes=list(scratch),
        compiler_params=pltpu.CompilerParams(vmem_limit_bytes=VMEM_BYTES),
    )(*smem, *operands)


def per_device(right_side, kernel_tiles, route_pairs):
    count = lax.axis_size("blk")
    window = max(8, min(16, count // 8))
    planes, chips = count // window, window // 2
    rows, cols = right_side.shape
    slots = kernel_tiles.shape[1]
    cover_len = window + planes - 1
    place = lax.axis_index("blk").astype(jnp.int32)
    plane, chip, core = place // window, place % window // 2, place % 2
    where = jnp.stack([plane, chip, core])
    single = jnp.float32

    straight, turned = call(
        split_kernel, (), (kernel_tiles[0],), [((slots, 2, rows, cols), jnp.bfloat16), ((slots, 2, cols, rows), jnp.bfloat16)]
    )
    far = exchange_planes(jnp.broadcast_to(right_side, (planes, rows, cols)), window)
    ahead = lax.dynamic_index_in_dim(far, (plane + 1) % planes, 0, keepdims=False)
    slot = jnp.arange(chips, dtype=jnp.int32)[:, None, None]
    spare = jnp.where(core == 0, ahead, right_side)
    even = exchange_in_plane(
        jnp.where(slot < chip, right_side, jnp.where(slot > chip, ahead, spare)), window
    )
    odd = core_partner(even)

    sent, kept, far_out = call(
        functools.partial(product_kernel, planes, chips),
        (route_pairs.T, where),
        (right_side, far, even, odd, straight, turned),
        [
            ((chips, rows + EXTRA, cols), single),
            ((chips + 1, rows, cols), single),
            ((planes - 2, rows, cols), single),
        ],
        (
            pltpu.VMEM((cover_len, rows, cols), single),
            pltpu.VMEM((cover_len, rows, 2 * cols), jnp.bfloat16),
            pltpu.VMEM((cover_len, rows, cols), single),
        ),
    )
    got = core_partner(sent)
    message, ahead = call(
        functools.partial(pair_kernel, chips),
        (where,),
        (sent, kept, got),
        [((chips, rows + EXTRA, cols), single), ((rows, cols), single)],
    )
    got = exchange_in_plane(message, window)
    (message,) = call(
        functools.partial(plane_kernel, planes, chips),
        (where,),
        (ahead, got, far_out),
        [((planes, rows + EXTRA, cols), single)],
    )
    got = exchange_planes(message, window)
    return call(final_kernel, (), (right_side, got), [((rows, cols), single), ((rows, cols), single)])


def solution(mesh):
    def run(*args):
        return tuple(per_device(*args))

    return jax.shard_map(
        run,
        mesh=mesh,
        in_specs=(P("blk", None), P("blk", None, None, None), P()),
        out_specs=(P("blk", None), P("blk", None)),
        check_vma=False,
    )
```

```python
import functools

import jax
import jax.numpy as jnp
from jax import lax
from jax.experimental import pallas as pl
from jax.experimental.pallas import tpu as pltpu
from jax.sharding import PartitionSpec as P

EXTRA = 8
VMEM_BYTES = 48 * 1024 * 1024


def shifted(value, steps):
    count = lax.axis_size("blk")
    pairs = [(source, (source + steps) % count) for source in range(count)]
    return lax.ppermute(value, "blk", pairs)


def chip_partner(value, mask):
    count = lax.axis_size("blk")
    return lax.ppermute(value, "blk", [(source, source ^ (2 * mask)) for source in range(count)])


def core_partner(value):
    count = lax.axis_size("blk")
    return lax.ppermute(value, "blk", [(source, source ^ 1) for source in range(count)])


def split_two(values):
    high = values.astype(jnp.bfloat16)
    low = (values - high.astype(jnp.float32)).astype(jnp.bfloat16)
    return high, low


def split_kernel(tiles_ref, own_ref, straight_ref, turned_ref, own_out):
    slots = tiles_ref.shape[0]
    own_out[...] = own_ref[...]

    def visit(t):
        tile = tiles_ref[t]
        straight_ref[t, 0], straight_ref[t, 1] = split_two(tile)
        turned_ref[t, 0], turned_ref[t, 1] = split_two(tile.T)

    if slots <= 32:
        for t in range(slots):
            visit(t)
    else:
        lax.fori_loop(0, slots, lambda t, c: (visit(t), c)[1], 0)


def steps_ahead(chip, mask, chips):
    return ((chip ^ mask) - chip) & (chips - 1)


def product_kernel(planes, chips, pairs_ref, where_ref, own_ref, *refs):
    window = 2 * chips
    far = refs[: planes - 1]
    even = refs[planes - 1 : planes + chips - 2]
    odd_ref, straight_ref, turned_ref, message_ref, kept_ref = refs[planes + chips - 2 : planes + chips + 3]
    far_out = refs[planes + chips + 3 : -3]
    whole, parts, total = refs[-3:]
    rows, cols = own_ref.shape
    chip, core = where_ref[0], where_ref[1]
    spare = jnp.where(core == 0, 1, window - 1)

    def put(place, values):
        whole[place] = values
        high, low = split_two(values)
        parts[place, :, :cols] = high
        parts[place, :, cols:] = low

    put(0, own_ref[...])
    for k in range(1, planes):
        put(window - 1 + k, far[k - 1][...])
    for m in range(1, chips):
        ahead = 2 * steps_ahead(chip, m, chips)
        put(ahead, even[m - 1][...])
        put(ahead + 1 - 2 * core, odd_ref[m])
    put(spare, odd_ref[0])

    total[...] = jnp.zeros_like(total)
    slots = straight_ref.shape[0]

    def product(split_ref, t, place):
        both = jnp.dot(split_ref[t, 0], parts[place], preferred_element_type=jnp.float32)
        rest = jnp.dot(split_ref[t, 1], parts[place, :, :cols], preferred_element_type=jnp.float32)
        return both[:, :cols] + (both[:, cols:] + rest)

    def visit(t, mirrored):
        row_place, col_place = pairs_ref[0, t], pairs_ref[1, t]
        total[row_place] += product(straight_ref, t, col_place)
        if mirrored:
            total[col_place] += product(turned_ref, t, row_place)

    visit(0, False)
    if slots <= 32:
        for t in range(1, slots - 1):
            visit(t, True)
    else:
        lax.fori_loop(1, slots - 1, lambda t, c: (visit(t, True), c)[1], 0)
    visit(slots - 1, False)

    dots = jnp.zeros((1, cols), jnp.float32)
    for place in range(whole.shape[0]):
        dots = dots + jnp.sum(whole[place] * total[place], axis=0, keepdims=True)
    own = own_ref[...]
    norm = jnp.sum(own * own, axis=0, keepdims=True)
    sums = jnp.concatenate([norm, dots, jnp.zeros((EXTRA - 2, cols), jnp.float32)], axis=0)
    message_ref[:rows, :] = total[spare]
    kept_ref[0] = total[0]
    for m in range(1, chips):
        ahead = 2 * steps_ahead(chip, m, chips)
        message_ref[m * rows : (m + 1) * rows, :] = total[ahead + 1 - 2 * core]
        kept_ref[m] = total[ahead]
    message_ref[chips * rows :, :] = sums
    kept_ref[chips] = total[window]
    for k in range(2, planes):
        far_out[k - 2][...] = total[window - 1 + k]


def pair_kernel(chips, where_ref, sent_ref, kept_ref, got_ref, *outs):
    messages = outs[: chips - 1]
    near_ref, next_ref, sums_ref = outs[chips - 1 :]
    rows = kept_ref.shape[1]
    core = where_ref[1]
    sums = sent_ref[chips * rows :, :] + got_ref[chips * rows :, :]
    for m in range(1, chips):
        messages[m - 1][:rows, :] = kept_ref[m] + got_ref[m * rows : (m + 1) * rows, :]
        messages[m - 1][rows:, :] = sums
    spare = got_ref[:rows, :]
    near_ref[...] = kept_ref[0] + jnp.where(core == 1, spare, 0.0)
    next_ref[...] = kept_ref[chips] + jnp.where(core == 0, spare, 0.0)
    sums_ref[...] = sums


def plane_kernel(chips, where_ref, near_ref, next_ref, sums_ref, *refs):
    got = refs[: chips - 1]
    far = refs[chips - 1 : -3]
    near_out, message, sums_out = refs[-3:]
    rows = near_ref.shape[0]
    chip = where_ref[0]
    near, ahead, sums = near_ref[...], next_ref[...], sums_ref[...]
    for m in range(1, chips):
        block = got[m - 1][:rows, :]
        same = (chip ^ m) < chip
        near = near + jnp.where(same, block, 0.0)
        ahead = ahead + jnp.where(same, 0.0, block)
        sums = sums + got[m - 1][rows:, :]
    for block in far:
        near = near + block[...]
    near_out[...] = near
    sums_out[...] = sums
    message[:rows, :] = ahead
    message[rows:, :] = sums


def final_kernel(right_ref, near_ref, sums_ref, got_ref, *refs):
    solution_ref, residual_ref = refs[-2:]
    rows = near_ref.shape[0]
    image = near_ref[...] + got_ref[:rows, :]
    sums = sums_ref[...] + got_ref[rows:, :]
    for more in refs[:-2]:
        sums = sums + more[...]
    step_len = sums[0:1, :] / sums[1:2, :]
    right = right_ref[...]
    solution_ref[...] = step_len * right
    residual_ref[...] = right - step_len * image


def call(kernel, smem, operands, outs, scratch=()):
    vmem = pl.BlockSpec(memory_space=pltpu.VMEM)
    return pl.pallas_call(
        kernel,
        in_specs=[pl.BlockSpec(memory_space=pltpu.SMEM)] * len(smem) + [vmem] * len(operands),
        out_specs=[vmem] * len(outs),
        out_shape=[jax.ShapeDtypeStruct(shape, kind) for shape, kind in outs],
        scratch_shapes=list(scratch),
        compiler_params=pltpu.CompilerParams(vmem_limit_bytes=VMEM_BYTES),
    )(*smem, *operands)


def per_device(right_side, kernel_tiles, route_pairs):
    count = lax.axis_size("blk")
    window = max(8, min(16, count // 8))
    planes, chips = count // window, window // 2
    rows, cols = right_side.shape
    slots = kernel_tiles.shape[1]
    cover_len = window + planes - 1
    place = lax.axis_index("blk").astype(jnp.int32)
    chip, core = place % window // 2, place % 2
    where = jnp.stack([chip, core])
    single, half = jnp.float32, jnp.bfloat16

    straight, turned, own = call(
        split_kernel,
        (),
        (kernel_tiles[0], right_side),
        [((slots, 2, rows, cols), half), ((slots, 2, cols, rows), half), ((rows, cols), single)],
    )
    far = [shifted(right_side, -k * window) for k in range(1, planes)]
    even = [chip_partner(jnp.where((chip ^ m) < chip, own, far[0]), m) for m in range(1, chips)]
    odd = jnp.stack([jnp.where(core == 0, far[0], own)] + even)
    odd, *rest = lax.optimization_barrier((odd, *far[1:]))
    far = far[:1] + rest
    odd = core_partner(odd)

    block, marked, extra = ((rows, cols), single), ((rows + EXTRA, cols), single), ((EXTRA, cols), single)
    sent, kept, *far_out = call(
        functools.partial(product_kernel, planes, chips),
        (route_pairs.T, where),
        (own, *far, *even, odd, straight, turned),
        [((chips * rows + EXTRA, cols), single), ((chips + 1, rows, cols), single)] + [block] * (planes - 2),
        (
            pltpu.VMEM((cover_len, rows, cols), single),
            pltpu.VMEM((cover_len, rows, 2 * cols), half),
            pltpu.VMEM((cover_len, rows, cols), single),
        ),
    )
    far_got = [shifted(value, k * window) for k, value in enumerate(far_out, 2)]
    got = core_partner(sent)
    *messages, near, ahead, sums = call(
        functools.partial(pair_kernel, chips), (where,), (sent, kept, got), [marked] * (chips - 1) + [block, block, extra]
    )
    got = [chip_partner(value, m) for m, value in enumerate(messages, 1)]
    near, message, sums = call(
        functools.partial(plane_kernel, chips), (where,), (near, ahead, sums, *got, *far_got), [block, marked, extra]
    )
    got = shifted(message, window)
    more = [shifted(sums, k * window) for k in range(2, planes)]
    return call(final_kernel, (), (own, near, sums, got, *more), [block, block])


def solution(mesh):
    def run(*args):
        return tuple(per_device(*args))

    return jax.shard_map(
        run,
        mesh=mesh,
        in_specs=(P("blk", None), P("blk", None, None, None), P()),
        out_specs=(P("blk", None), P("blk", None)),
        check_vma=False,
    )
```

```python
import functools

import jax
import jax.numpy as jnp
from jax import lax
from jax.experimental import pallas as pl
from jax.experimental.pallas import tpu as pltpu
from jax.sharding import PartitionSpec as P

EXTRA = 8
VMEM_BYTES = 48 * 1024 * 1024
EVEN, ODD = 0, 1


def plane_steps(steps, count):
    return lambda source: (source + steps) % count


def chip_steps(mask):
    return lambda source: source ^ (2 * mask)


def send(value, even=None, odd=None):
    count = lax.axis_size("blk")
    ways = (even, odd)
    return lax.ppermute(value, "blk", [(source, ways[source % 2](source)) for source in range(count) if ways[source % 2]])


def core_partner(value):
    swap = lambda source: source ^ 1
    return send(value, swap, swap)


def place_of(place_ref, chips):
    place = place_ref[0]
    return (place // 2) % chips, place % 2


def split_two(values):
    high = values.astype(jnp.bfloat16)
    low = (values - high.astype(jnp.float32)).astype(jnp.bfloat16)
    return high, low


def split_kernel(tiles_ref, straight_ref, turned_ref):
    slots = tiles_ref.shape[0]

    def visit(t):
        tile = tiles_ref[t]
        straight_ref[t, 0], straight_ref[t, 1] = split_two(tile)
        turned_ref[t, 0], turned_ref[t, 1] = split_two(tile.T)

    if slots <= 32:
        for t in range(slots):
            visit(t)
    else:
        lax.fori_loop(0, slots, lambda t, c: (visit(t), c)[1], 0)


def fetch_kernel(own_ref, out_ref, done):
    copy = pltpu.make_async_copy(own_ref, out_ref, done)
    copy.start()
    copy.wait()


def steps_ahead(chip, mask, chips):
    return ((chip ^ mask) - chip) & (chips - 1)


def product_kernel(planes, chips, pairs_ref, place_ref, own_ref, pair_ref, swapped_ref, first_ref, *refs):
    window = 2 * chips
    later = refs[: planes - 3]
    plane = refs[planes - 3 : planes + chips - 4]
    straight_ref, turned_ref, message_ref, total, whole, parts = refs[planes + chips - 4 :]
    rows, cols = own_ref.shape
    chip, core = place_of(place_ref, chips)
    even = core == EVEN

    def put(place, values):
        whole[place] = values
        high, low = split_two(values)
        parts[place, :, :cols] = high
        parts[place, :, cols:] = low

    put(0, own_ref[...])
    put(jnp.where(even, 1, window - 1), jnp.where(even, pair_ref[1], first_ref[0]))
    put(window, jnp.where(even, swapped_ref[2 * chips - 2], first_ref[1]))
    for m in range(1, chips):
        ahead = 2 * steps_ahead(chip, m, chips) - core
        for column in range(2):
            slot = 2 * (m - 1) + column
            put(ahead + column, jnp.where(even, swapped_ref[slot], plane[m - 1][column]))
    for k in range(2, planes):
        held = first_ref if k == 2 else later[k - 3]
        put(window - 1 + k, jnp.where(even, held[0], swapped_ref[k - 2]))

    total[...] = jnp.zeros_like(total)
    slots = straight_ref.shape[0]

    def product(split_ref, t, place):
        both = jnp.dot(split_ref[t, 0], parts[place], preferred_element_type=jnp.float32)
        rest = jnp.dot(split_ref[t, 1], parts[place, :, :cols], preferred_element_type=jnp.float32)
        return both[:, :cols] + (both[:, cols:] + rest)

    def visit(t, mirrored):
        row_place, col_place = pairs_ref[0, t], pairs_ref[1, t]
        total[row_place] += product(straight_ref, t, col_place)
        if mirrored:
            total[col_place] += product(turned_ref, t, row_place)

    visit(0, False)
    if slots <= 32:
        for t in range(1, slots - 1):
            visit(t, True)
    else:
        lax.fori_loop(1, slots - 1, lambda t, c: (visit(t, True), c)[1], 0)
    visit(slots - 1, False)

    dots = jnp.zeros((1, cols), jnp.float32)
    for place in range(whole.shape[0]):
        dots = dots + jnp.sum(whole[place] * total[place], axis=0, keepdims=True)
    own = own_ref[...]
    norm = jnp.sum(own * own, axis=0, keepdims=True)
    count = message_ref.shape[0] // rows
    wanted = []
    for m in range(1, chips):
        ahead = 2 * steps_ahead(chip, m, chips)
        wanted += [ahead, ahead + 1]
    wanted += [window, 1]
    for slot in range(count):
        from_even = wanted[slot] if slot < len(wanted) else 0
        from_odd = window + 1 + slot if slot < planes - 2 else 0
        message_ref[slot * rows : (slot + 1) * rows, :] = total[jnp.where(even, from_even, from_odd)]
    sums = jnp.concatenate([norm, dots, jnp.zeros((EXTRA - 2, cols), jnp.float32)], axis=0)
    message_ref[count * rows :, :] = sums


def pair_kernel(planes, chips, place_ref, sent_ref, total_ref, got_ref, *outs):
    messages = outs[:-3]
    near_ref, next_ref, sums_ref = outs[-3:]
    window = 2 * chips
    rows = near_ref.shape[0]
    chip, core = place_of(place_ref, chips)
    even = core == EVEN
    tail = got_ref.shape[0] - EXTRA
    sums = sent_ref[tail:, :] + got_ref[tail:, :]

    def got(slot):
        return got_ref[slot * rows : (slot + 1) * rows, :]

    for i, message in enumerate(messages):
        for column in range(2):
            part = None
            if i < planes - 2:
                part = total_ref[window + 1 + i] if column == 0 else got(i)
            if i < chips - 1:
                ahead = 2 * steps_ahead(chip, i + 1, chips)
                plane = total_ref[jnp.where(even, 0, ahead - 1 + column)] + got(2 * i + column)
                part = plane if part is None else jnp.where(even, part, plane)
            message[column * rows : (column + 1) * rows, :] = part
        message[2 * rows :, :] = sums
    near_ref[...] = total_ref[0] + jnp.where(even, 0.0, got(2 * chips - 1))
    next_ref[:rows, :] = total_ref[window - 1] + got(2 * chips - 2)
    next_ref[rows:, :] = total_ref[window]
    sums_ref[...] = sums


def apart_kernel(planes, *refs):
    out_ref = refs[-1]
    rows = refs[0].shape[0] - EXTRA
    sums = refs[0][rows:, :]
    for more in refs[1:-1]:
        sums = sums + more[rows:, :]
    out_ref[...] = sums


def plane_kernel(planes, chips, place_ref, near_ref, next_ref, sums_ref, *refs):
    got = refs[:-2]
    pair_out, message = refs[-2:]
    rows = near_ref.shape[0]
    chip, core = place_of(place_ref, chips)
    even = core == EVEN
    sums = sums_ref[...]
    near = [jnp.where(even, near_ref[...], 0.0), jnp.where(even, 0.0, near_ref[...])]
    ahead = [next_ref[:rows, :], next_ref[rows:, :]]
    for i, value in enumerate(got):
        in_plane = i < chips - 1
        same = (chip ^ (i + 1)) < chip
        mine = even if i < planes - 2 else False
        if in_plane:
            mine = jnp.logical_or(mine, jnp.logical_and(core == ODD, same))
            sums = sums + value[2 * rows :, :]
        for column in range(2):
            block = value[column * rows : (column + 1) * rows, :]
            near[column] = near[column] + jnp.where(mine, block, 0.0)
            if in_plane:
                ahead[column] = ahead[column] + jnp.where(same, 0.0, block)
    for column in range(2):
        pair_out[column * rows : (column + 1) * rows, :] = near[column]
        message[column * rows : (column + 1) * rows, :] = ahead[column]
    message[2 * rows :, :] = sums


def last_kernel(place_ref, pair_ref, sent_ref, got_ref, apart_ref, mine_ref, message_ref):
    rows = mine_ref.shape[0]
    even = place_ref[0] % 2 == EVEN
    first = pair_ref[:rows, :] + got_ref[:rows, :]
    second = pair_ref[rows:, :] + got_ref[rows : 2 * rows, :]
    mine_ref[...] = jnp.where(even, first, second)
    message_ref[:rows, :] = jnp.where(even, second, first)
    message_ref[rows:, :] = jnp.where(even, apart_ref[...], sent_ref[2 * rows :, :] + got_ref[2 * rows :, :])


def final_kernel(right_ref, mine_ref, sent_ref, got_ref, solution_ref, residual_ref):
    rows = mine_ref.shape[0]
    image = mine_ref[...] + got_ref[:rows, :]
    sums = sent_ref[rows:, :] + got_ref[rows:, :]
    step_len = sums[0:1, :] / sums[1:2, :]
    right = right_ref[...]
    solution_ref[...] = step_len * right
    residual_ref[...] = right - step_len * image


def call(kernel, smem, operands, outs, scratch=(), space=pltpu.VMEM):
    vmem = pl.BlockSpec(memory_space=pltpu.VMEM)
    return pl.pallas_call(
        kernel,
        in_specs=[pl.BlockSpec(memory_space=pltpu.SMEM)] * len(smem) + [pl.BlockSpec(memory_space=space)] * len(operands),
        out_specs=[vmem] * len(outs),
        out_shape=[jax.ShapeDtypeStruct(shape, kind) for shape, kind in outs],
        scratch_shapes=list(scratch),
        compiler_params=pltpu.CompilerParams(vmem_limit_bytes=VMEM_BYTES),
    )(*smem, *operands)


def per_device(right_side, kernel_tiles, route_pairs):
    count = lax.axis_size("blk")
    window = max(8, min(16, count // 8))
    planes, chips = count // window, window // 2
    rows, cols = right_side.shape
    slots = kernel_tiles.shape[1]
    cover_len = window + planes - 1
    place = lax.axis_index("blk").astype(jnp.int32)
    chip, core = place // 2 % chips, place % 2
    where = place[None]
    even = core == EVEN
    single, half = jnp.float32, jnp.bfloat16

    (own,) = call(fetch_kernel, (), (right_side,), [((rows, cols), single)], [pltpu.SemaphoreType.DMA], pl.ANY)
    straight, turned = call(
        split_kernel, (), (kernel_tiles[0],), [((slots, 2, rows, cols), half), ((slots, 2, cols, rows), half)]
    )
    partner = core_partner(right_side)
    pair = jnp.where(even, jnp.stack([own, partner]), jnp.stack([partner, own]))
    first = send(pair, plane_steps(-2 * window, count), plane_steps(-window, count))
    later = [send(pair, even=plane_steps(-k * window, count)) for k in range(3, planes)]
    ahead, *later = lax.optimization_barrier((first, *later))
    plane = [
        send(jnp.where((chip ^ m) < chip, pair, ahead), odd=chip_steps(m)) for m in range(1, chips)
    ]
    to_even = [value[column] for value in plane for column in range(2)] + [ahead[0]]
    to_odd = [value[1] for value in [ahead, *later]]
    swapped = core_partner(
        jnp.stack([jnp.where(even, to_odd[i], value) if i < len(to_odd) else value for i, value in enumerate(to_even)])
    )

    block, extra = ((rows, cols), single), ((EXTRA, cols), single)
    two, marked = ((2 * rows, cols), single), ((2 * rows + EXTRA, cols), single)
    sent, total = call(
        functools.partial(product_kernel, planes, chips),
        (route_pairs.T, where),
        (own, pair, swapped, ahead, *later, *plane, straight, turned),
        [((max(2 * chips, planes - 2) * rows + EXTRA, cols), single), ((cover_len, rows, cols), single)],
        (pltpu.VMEM((cover_len, rows, cols), single), pltpu.VMEM((cover_len, rows, 2 * cols), half)),
    )
    got = core_partner(sent)
    *messages, near, ahead, sums = call(
        functools.partial(pair_kernel, planes, chips),
        (where,),
        (sent, total, got),
        [marked] * max(chips - 1, planes - 2) + [block, two, extra],
    )
    got = [
        send(
            value,
            even=plane_steps((i + 2) * window, count) if i < planes - 2 else None,
            odd=chip_steps(i + 1) if i < chips - 1 else None,
        )
        for i, value in enumerate(messages)
    ]
    (apart,) = call(functools.partial(apart_kernel, planes), (), got[: planes - 2], [extra])
    mask = 1
    while mask < chips:
        apart = apart + send(apart, even=chip_steps(mask))
        mask *= 2
    pair, message = call(
        functools.partial(plane_kernel, planes, chips), (where,), (near, ahead, sums, *got), [two, marked]
    )
    got = send(message, odd=plane_steps(window, count))
    mine, sent = call(last_kernel, (where,), (pair, message, got, apart), [block, ((rows + EXTRA, cols), single)])
    got = core_partner(sent)
    return call(final_kernel, (), (own, mine, sent, got), [block, block])


def solution(mesh):
    def run(*args):
        return tuple(per_device(*args))

    return jax.shard_map(
        run,
        mesh=mesh,
        in_specs=(P("blk", None), P("blk", None, None, None), P()),
        out_specs=(P("blk", None), P("blk", None)),
        check_vma=False,
    )
```

```python
import functools

import jax
import jax.numpy as jnp
from jax import lax
from jax.experimental import pallas as pl
from jax.experimental.pallas import tpu as pltpu
from jax.sharding import PartitionSpec as P

EXTRA = 8
VMEM_BYTES = 48 * 1024 * 1024
EVEN, ODD = 0, 1


def plane_steps(steps, count):
    return lambda source: (source + steps) % count


def chip_steps(mask):
    return lambda source: source ^ (2 * mask)


def send(value, even=None, odd=None):
    count = lax.axis_size("blk")
    ways = [way or (lambda source: source) for way in (even, odd)]
    return lax.ppermute(value, "blk", [(source, ways[source % 2](source)) for source in range(count)])


def core_partner(value):
    swap = lambda source: source ^ 1
    return send(value, swap, swap)


def place_of(place_ref, chips):
    place = place_ref[0]
    return (place // 2) % chips, place % 2


def split_two(values):
    high = values.astype(jnp.bfloat16)
    low = (values - high.astype(jnp.float32)).astype(jnp.bfloat16)
    return high, low


def split_kernel(tiles_ref, straight_ref, turned_ref):
    slots = tiles_ref.shape[0]

    def visit(t):
        tile = tiles_ref[t]
        straight_ref[t, 0], straight_ref[t, 1] = split_two(tile)
        turned_ref[t, 0], turned_ref[t, 1] = split_two(tile.T)

    if slots <= 32:
        for t in range(slots):
            visit(t)
    else:
        lax.fori_loop(0, slots, lambda t, c: (visit(t), c)[1], 0)


def fetch_kernel(own_ref, out_ref, done):
    copy = pltpu.make_async_copy(own_ref, out_ref, done)
    copy.start()
    copy.wait()


def steps_ahead(chip, mask, chips):
    return ((chip ^ mask) - chip) & (chips - 1)


def product_kernel(planes, chips, pairs_ref, place_ref, own_ref, pair_ref, swapped_ref, first_ref, *refs):
    window = 2 * chips
    later = refs[: planes - 3]
    plane = refs[planes - 3 : planes + chips - 4]
    straight_ref, turned_ref, message_ref, total, whole, parts = refs[planes + chips - 4 :]
    rows, cols = own_ref.shape
    chip, core = place_of(place_ref, chips)
    even = core == EVEN

    def put(place, values):
        whole[place] = values
        high, low = split_two(values)
        parts[place, :, :cols] = high
        parts[place, :, cols:] = low

    put(0, own_ref[...])
    put(jnp.where(even, 1, window - 1), jnp.where(even, pair_ref[1], first_ref[0]))
    put(window, jnp.where(even, swapped_ref[2 * chips - 2], first_ref[1]))
    for m in range(1, chips):
        ahead = 2 * steps_ahead(chip, m, chips) - core
        for column in range(2):
            slot = 2 * (m - 1) + column
            put(ahead + column, jnp.where(even, swapped_ref[slot], plane[m - 1][column]))
    for k in range(2, planes):
        held = first_ref if k == 2 else later[k - 3]
        put(window - 1 + k, jnp.where(even, held[0], swapped_ref[k - 2]))

    total[...] = jnp.zeros_like(total)
    slots = straight_ref.shape[0]

    def product(split_ref, t, place):
        both = jnp.dot(split_ref[t, 0], parts[place], preferred_element_type=jnp.float32)
        rest = jnp.dot(split_ref[t, 1], parts[place, :, :cols], preferred_element_type=jnp.float32)
        return both[:, :cols] + (both[:, cols:] + rest)

    def visit(t, mirrored):
        row_place, col_place = pairs_ref[0, t], pairs_ref[1, t]
        total[row_place] += product(straight_ref, t, col_place)
        if mirrored:
            total[col_place] += product(turned_ref, t, row_place)

    visit(0, False)
    if slots <= 32:
        for t in range(1, slots - 1):
            visit(t, True)
    else:
        lax.fori_loop(1, slots - 1, lambda t, c: (visit(t, True), c)[1], 0)
    visit(slots - 1, False)

    dots = jnp.zeros((1, cols), jnp.float32)
    for place in range(whole.shape[0]):
        dots = dots + jnp.sum(whole[place] * total[place], axis=0, keepdims=True)
    own = own_ref[...]
    norm = jnp.sum(own * own, axis=0, keepdims=True)
    count = message_ref.shape[0] // rows
    wanted = []
    for m in range(1, chips):
        ahead = 2 * steps_ahead(chip, m, chips)
        wanted += [ahead, ahead + 1]
    wanted += [window, 1]
    for slot in range(count):
        from_even = wanted[slot] if slot < len(wanted) else 0
        from_odd = window + 1 + slot if slot < planes - 2 else 0
        message_ref[slot * rows : (slot + 1) * rows, :] = total[jnp.where(even, from_even, from_odd)]
    sums = jnp.concatenate([norm, dots, jnp.zeros((EXTRA - 2, cols), jnp.float32)], axis=0)
    message_ref[count * rows :, :] = sums


def pair_kernel(planes, chips, place_ref, sent_ref, total_ref, got_ref, *outs):
    messages = outs[:-3]
    near_ref, next_ref, sums_ref = outs[-3:]
    window = 2 * chips
    rows = near_ref.shape[0]
    chip, core = place_of(place_ref, chips)
    even = core == EVEN
    tail = got_ref.shape[0] - EXTRA
    sums = sent_ref[tail:, :] + got_ref[tail:, :]

    def got(slot):
        return got_ref[slot * rows : (slot + 1) * rows, :]

    for i, message in enumerate(messages):
        for column in range(2):
            part = None
            if i < planes - 2:
                part = total_ref[window + 1 + i] if column == 0 else got(i)
            if i < chips - 1:
                ahead = 2 * steps_ahead(chip, i + 1, chips)
                plane = total_ref[jnp.where(even, 0, ahead - 1 + column)] + got(2 * i + column)
                part = plane if part is None else jnp.where(even, part, plane)
            message[column * rows : (column + 1) * rows, :] = part
        message[2 * rows :, :] = sums
    near_ref[...] = total_ref[0] + jnp.where(even, 0.0, got(2 * chips - 1))
    next_ref[:rows, :] = total_ref[window - 1] + got(2 * chips - 2)
    next_ref[rows:, :] = total_ref[window]
    sums_ref[...] = sums


def apart_kernel(planes, *refs):
    out_ref = refs[-1]
    rows = refs[0].shape[0] - EXTRA
    sums = refs[0][rows:, :]
    for more in refs[1:-1]:
        sums = sums + more[rows:, :]
    out_ref[...] = sums


def plane_kernel(planes, chips, place_ref, near_ref, next_ref, sums_ref, *refs):
    got = refs[:-2]
    pair_out, message = refs[-2:]
    rows = near_ref.shape[0]
    chip, core = place_of(place_ref, chips)
    even = core == EVEN
    sums = sums_ref[...]
    near = [jnp.where(even, near_ref[...], 0.0), jnp.where(even, 0.0, near_ref[...])]
    ahead = [next_ref[:rows, :], next_ref[rows:, :]]
    for i, value in enumerate(got):
        in_plane = i < chips - 1
        same = (chip ^ (i + 1)) < chip
        mine = even if i < planes - 2 else False
        if in_plane:
            mine = jnp.logical_or(mine, jnp.logical_and(core == ODD, same))
            sums = sums + value[2 * rows :, :]
        for column in range(2):
            block = value[column * rows : (column + 1) * rows, :]
            near[column] = near[column] + jnp.where(mine, block, 0.0)
            if in_plane:
                ahead[column] = ahead[column] + jnp.where(same, 0.0, block)
    for column in range(2):
        pair_out[column * rows : (column + 1) * rows, :] = near[column]
        message[column * rows : (column + 1) * rows, :] = ahead[column]
    message[2 * rows :, :] = sums


def last_kernel(place_ref, pair_ref, sent_ref, got_ref, apart_ref, mine_ref, message_ref):
    rows = mine_ref.shape[0]
    even = place_ref[0] % 2 == EVEN
    first = pair_ref[:rows, :] + jnp.where(even, 0.0, got_ref[:rows, :])
    second = pair_ref[rows:, :] + jnp.where(even, 0.0, got_ref[rows : 2 * rows, :])
    mine_ref[...] = jnp.where(even, first, second)
    message_ref[:rows, :] = jnp.where(even, second, first)
    message_ref[rows:, :] = jnp.where(even, apart_ref[...], sent_ref[2 * rows :, :] + got_ref[2 * rows :, :])


def final_kernel(right_ref, mine_ref, sent_ref, got_ref, solution_ref, residual_ref):
    rows = mine_ref.shape[0]
    image = mine_ref[...] + got_ref[:rows, :]
    sums = sent_ref[rows:, :] + got_ref[rows:, :]
    step_len = sums[0:1, :] / sums[1:2, :]
    right = right_ref[...]
    solution_ref[...] = step_len * right
    residual_ref[...] = right - step_len * image


def call(kernel, smem, operands, outs, scratch=(), space=pltpu.VMEM):
    vmem = pl.BlockSpec(memory_space=pltpu.VMEM)
    return pl.pallas_call(
        kernel,
        in_specs=[pl.BlockSpec(memory_space=pltpu.SMEM)] * len(smem) + [pl.BlockSpec(memory_space=space)] * len(operands),
        out_specs=[vmem] * len(outs),
        out_shape=[jax.ShapeDtypeStruct(shape, kind) for shape, kind in outs],
        scratch_shapes=list(scratch),
        compiler_params=pltpu.CompilerParams(vmem_limit_bytes=VMEM_BYTES),
    )(*smem, *operands)


def per_device(right_side, kernel_tiles, route_pairs):
    count = lax.axis_size("blk")
    window = max(8, min(16, count // 8))
    planes, chips = count // window, window // 2
    rows, cols = right_side.shape
    slots = kernel_tiles.shape[1]
    cover_len = window + planes - 1
    place = lax.axis_index("blk").astype(jnp.int32)
    chip, core = place // 2 % chips, place % 2
    where = place[None]
    even = core == EVEN
    single, half = jnp.float32, jnp.bfloat16

    (own,) = call(fetch_kernel, (), (right_side,), [((rows, cols), single)], [pltpu.SemaphoreType.DMA], pl.ANY)
    straight, turned = call(
        split_kernel, (), (kernel_tiles[0],), [((slots, 2, rows, cols), half), ((slots, 2, cols, rows), half)]
    )
    partner = core_partner(right_side)
    pair = jnp.where(even, jnp.stack([own, partner]), jnp.stack([partner, own]))
    first = send(pair, plane_steps(-2 * window, count), plane_steps(-window, count))
    later = [send(pair, even=plane_steps(-k * window, count)) for k in range(3, planes)]
    ahead, *later = lax.optimization_barrier((first, *later))
    plane = [
        send(jnp.where((chip ^ m) < chip, pair, ahead), odd=chip_steps(m)) for m in range(1, chips)
    ]
    to_even = [value[column] for value in plane for column in range(2)] + [ahead[0]]
    to_odd = [value[1] for value in [ahead, *later]]
    swapped = core_partner(
        jnp.stack([jnp.where(even, to_odd[i], value) if i < len(to_odd) else value for i, value in enumerate(to_even)])
    )

    block, extra = ((rows, cols), single), ((EXTRA, cols), single)
    two, marked = ((2 * rows, cols), single), ((2 * rows + EXTRA, cols), single)
    sent, total = call(
        functools.partial(product_kernel, planes, chips),
        (route_pairs.T, where),
        (own, pair, swapped, ahead, *later, *plane, straight, turned),
        [((max(2 * chips, planes - 2) * rows + EXTRA, cols), single), ((cover_len, rows, cols), single)],
        (pltpu.VMEM((cover_len, rows, cols), single), pltpu.VMEM((cover_len, rows, 2 * cols), half)),
    )
    got = core_partner(sent)
    *messages, near, ahead, sums = call(
        functools.partial(pair_kernel, planes, chips),
        (where,),
        (sent, total, got),
        [marked] * max(chips - 1, planes - 2) + [block, two, extra],
    )
    got = [
        send(
            value,
            even=plane_steps((i + 2) * window, count) if i < planes - 2 else None,
            odd=chip_steps(i + 1) if i < chips - 1 else None,
        )
        for i, value in enumerate(messages)
    ]
    (apart,) = call(functools.partial(apart_kernel, planes), (), got[: planes - 2], [extra])
    mask = 1
    while mask < chips:
        apart = apart + send(apart, even=chip_steps(mask))
        mask *= 2
    pair, message = call(
        functools.partial(plane_kernel, planes, chips), (where,), (near, ahead, sums, *got), [two, marked]
    )
    got = send(message, odd=plane_steps(window, count))
    mine, sent = call(last_kernel, (where,), (pair, message, got, apart), [block, ((rows + EXTRA, cols), single)])
    got = core_partner(sent)
    return call(final_kernel, (), (own, mine, sent, got), [block, block])


def solution(mesh):
    def run(*args):
        return tuple(per_device(*args))

    return jax.shard_map(
        run,
        mesh=mesh,
        in_specs=(P("blk", None), P("blk", None, None, None), P()),
        out_specs=(P("blk", None), P("blk", None)),
        check_vma=False,
    )
```

```python
import functools

import jax
import jax.numpy as jnp
from jax import lax
from jax.experimental import pallas as pl
from jax.experimental.pallas import tpu as pltpu
from jax.sharding import PartitionSpec as P

EXTRA = 8
VMEM_BYTES = 48 * 1024 * 1024


def shifted(value, steps):
    count = lax.axis_size("blk")
    pairs = [(source, (source + steps) % count) for source in range(count)]
    return lax.ppermute(value, "blk", pairs)


def chip_partner(value, mask):
    count = lax.axis_size("blk")
    return lax.ppermute(value, "blk", [(source, source ^ (2 * mask)) for source in range(count)])


def core_partner(value):
    count = lax.axis_size("blk")
    return lax.ppermute(value, "blk", [(source, source ^ 1) for source in range(count)])


def split_two(values):
    high = values.astype(jnp.bfloat16)
    low = (values - high.astype(jnp.float32)).astype(jnp.bfloat16)
    return high, low


def place_of(place_ref, chips):
    place = place_ref[0]
    return (place // 2) & (chips - 1), place & 1


def fetch_kernel(own_ref, out_ref, done):
    copy = pltpu.make_async_copy(own_ref, out_ref, done)
    copy.start()
    copy.wait()


def split_kernel(tiles_ref, straight_ref, turned_ref):
    slots = tiles_ref.shape[0]

    def visit(t):
        tile = tiles_ref[t]
        straight_ref[t, 0], straight_ref[t, 1] = split_two(tile)
        turned_ref[t, 0], turned_ref[t, 1] = split_two(tile.T)

    if slots <= 32:
        for t in range(slots):
            visit(t)
    else:
        lax.fori_loop(0, slots, lambda t, c: (visit(t), c)[1], 0)


def steps_ahead(chip, mask, chips):
    return ((chip ^ mask) - chip) & (chips - 1)


def product_kernel(planes, chips, pairs_ref, place_ref, own_ref, *refs):
    window = 2 * chips
    far = refs[: planes - 1]
    even = refs[planes - 1 : planes + chips - 2]
    odd_ref, straight_ref, turned_ref, message_ref, kept_ref = refs[planes + chips - 2 : planes + chips + 3]
    far_out = refs[planes + chips + 3 : -3]
    whole, parts, total = refs[-3:]
    rows, cols = own_ref.shape
    chip, core = place_of(place_ref, chips)
    spare = jnp.where(core == 0, 1, window - 1)

    def put(place, values):
        whole[place] = values
        high, low = split_two(values)
        parts[place, :, :cols] = high
        parts[place, :, cols:] = low

    put(0, own_ref[...])
    for k in range(1, planes):
        put(window - 1 + k, far[k - 1][...])
    for m in range(1, chips):
        ahead = 2 * steps_ahead(chip, m, chips)
        put(ahead, even[m - 1][...])
        put(ahead + 1 - 2 * core, odd_ref[m])
    put(spare, odd_ref[0])

    total[...] = jnp.zeros_like(total)
    slots = straight_ref.shape[0]

    def product(split_ref, t, place):
        both = jnp.dot(split_ref[t, 0], parts[place], preferred_element_type=jnp.float32)
        rest = jnp.dot(split_ref[t, 1], parts[place, :, :cols], preferred_element_type=jnp.float32)
        return both[:, :cols] + (both[:, cols:] + rest)

    def visit(t, mirrored):
        row_place, col_place = pairs_ref[0, t], pairs_ref[1, t]
        total[row_place] += product(straight_ref, t, col_place)
        if mirrored:
            total[col_place] += product(turned_ref, t, row_place)

    visit(0, False)
    if slots <= 32:
        for t in range(1, slots - 1):
            visit(t, True)
    else:
        lax.fori_loop(1, slots - 1, lambda t, c: (visit(t, True), c)[1], 0)
    visit(slots - 1, False)

    dots = jnp.zeros((1, cols), jnp.float32)
    for place in range(whole.shape[0]):
        dots = dots + jnp.sum(whole[place] * total[place], axis=0, keepdims=True)
    own = own_ref[...]
    norm = jnp.sum(own * own, axis=0, keepdims=True)
    sums = jnp.concatenate([norm, dots, jnp.zeros((EXTRA - 2, cols), jnp.float32)], axis=0)
    message_ref[:rows, :] = total[spare]
    kept_ref[0] = total[0]
    for m in range(1, chips):
        ahead = 2 * steps_ahead(chip, m, chips)
        message_ref[m * rows : (m + 1) * rows, :] = total[ahead + 1 - 2 * core]
        kept_ref[m] = total[ahead]
    message_ref[chips * rows :, :] = sums
    kept_ref[chips] = total[window]
    for k in range(2, planes):
        far_out[k - 2][...] = total[window - 1 + k]


def pair_kernel(chips, place_ref, sent_ref, kept_ref, got_ref, *outs):
    messages = outs[: chips - 1]
    near_ref, next_ref, sums_ref = outs[chips - 1 :]
    rows = kept_ref.shape[1]
    core = place_of(place_ref, chips)[1]
    sums = sent_ref[chips * rows :, :] + got_ref[chips * rows :, :]
    for m in range(1, chips):
        messages[m - 1][:rows, :] = kept_ref[m] + got_ref[m * rows : (m + 1) * rows, :]
        messages[m - 1][rows:, :] = sums
    spare = got_ref[:rows, :]
    near_ref[...] = kept_ref[0] + jnp.where(core == 1, spare, 0.0)
    next_ref[...] = kept_ref[chips] + jnp.where(core == 0, spare, 0.0)
    sums_ref[...] = sums


def plane_kernel(planes, chips, place_ref, near_ref, next_ref, sums_ref, *refs):
    got = refs[: chips - 1]
    far = refs[chips - 1 : chips + planes - 3]
    messages = refs[chips + planes - 3 : -2]
    near_out, sums_out = refs[-2:]
    rows = near_ref.shape[0]
    chip = place_of(place_ref, chips)[0]
    near, ahead, sums = near_ref[...], next_ref[...], sums_ref[...]
    for m in range(1, chips):
        block = got[m - 1][:rows, :]
        same = (chip ^ m) < chip
        near = near + jnp.where(same, block, 0.0)
        ahead = ahead + jnp.where(same, 0.0, block)
        sums = sums + got[m - 1][rows:, :]
    near_out[...] = near
    sums_out[...] = sums
    messages[0][:rows, :] = ahead
    for k in range(2, planes):
        messages[k - 1][:rows, :] = far[k - 2][...]
    for message in messages:
        message[rows:, :] = sums


def final_kernel(right_ref, near_ref, sums_ref, *refs):
    solution_ref, residual_ref = refs[-2:]
    rows = near_ref.shape[0]
    image, sums = near_ref[...], sums_ref[...]
    for got in refs[:-2]:
        image = image + got[:rows, :]
        sums = sums + got[rows:, :]
    step_len = sums[0:1, :] / sums[1:2, :]
    right = right_ref[...]
    solution_ref[...] = step_len * right
    residual_ref[...] = right - step_len * image


def call(kernel, smem, operands, outs, scratch=(), space=pltpu.VMEM):
    vmem = pl.BlockSpec(memory_space=pltpu.VMEM)
    return pl.pallas_call(
        kernel,
        in_specs=[pl.BlockSpec(memory_space=pltpu.SMEM)] * len(smem) + [pl.BlockSpec(memory_space=space)] * len(operands),
        out_specs=[vmem] * len(outs),
        out_shape=[jax.ShapeDtypeStruct(shape, kind) for shape, kind in outs],
        scratch_shapes=list(scratch),
        compiler_params=pltpu.CompilerParams(vmem_limit_bytes=VMEM_BYTES),
    )(*smem, *operands)


def per_device(right_side, kernel_tiles, route_pairs):
    count = lax.axis_size("blk")
    window = max(8, min(16, count // 8))
    planes, chips = count // window, window // 2
    rows, cols = right_side.shape
    slots = kernel_tiles.shape[1]
    cover_len = window + planes - 1
    place = lax.axis_index("blk").astype(jnp.int32)
    chip, core = place % window // 2, place % 2
    where = place[None]
    single, half = jnp.float32, jnp.bfloat16

    (own,) = call(fetch_kernel, (), (right_side,), [((rows, cols), single)], [pltpu.SemaphoreType.DMA], pl.ANY)
    straight, turned = call(
        split_kernel, (), (kernel_tiles[0],), [((slots, 2, rows, cols), half), ((slots, 2, cols, rows), half)]
    )
    far = [shifted(right_side, -k * window) for k in range(1, planes)]
    sent = [jnp.where((chip ^ m) < chip, own, far[0]) for m in range(1, chips)]
    sent[-1], *rest = lax.optimization_barrier((sent[-1], *far[1:]))
    far = far[:1] + rest
    even = [chip_partner(value, m) for m, value in enumerate(sent, 1)]
    odd = core_partner(jnp.stack([jnp.where(core == 0, far[0], own)] + even))

    block, marked, extra = ((rows, cols), single), ((rows + EXTRA, cols), single), ((EXTRA, cols), single)
    sent, kept, *far_out = call(
        functools.partial(product_kernel, planes, chips),
        (route_pairs.T, where),
        (own, *far, *even, odd, straight, turned),
        [((chips * rows + EXTRA, cols), single), ((chips + 1, rows, cols), single)] + [block] * (planes - 2),
        (
            pltpu.VMEM((cover_len, rows, cols), single),
            pltpu.VMEM((cover_len, rows, 2 * cols), half),
            pltpu.VMEM((cover_len, rows, cols), single),
        ),
    )
    got = core_partner(sent)
    *messages, near, ahead, sums = call(
        functools.partial(pair_kernel, chips), (where,), (sent, kept, got), [marked] * (chips - 1) + [block, block, extra]
    )
    got = [chip_partner(value, m) for m, value in enumerate(messages, 1)]
    *messages, near, sums = call(
        functools.partial(plane_kernel, planes, chips),
        (where,),
        (near, ahead, sums, *got, *far_out),
        [marked] * (planes - 1) + [block, extra],
    )
    got = [shifted(value, k * window) for k, value in enumerate(messages, 1)]
    return call(final_kernel, (), (own, near, sums, *got), [block, block])


def solution(mesh):
    def run(*args):
        return tuple(per_device(*args))

    return jax.shard_map(
        run,
        mesh=mesh,
        in_specs=(P("blk", None), P("blk", None, None, None), P()),
        out_specs=(P("blk", None), P("blk", None)),
        check_vma=False,
    )
```

```python
import functools

import jax
import jax.numpy as jnp
from jax import lax
from jax.experimental import pallas as pl
from jax.experimental.pallas import tpu as pltpu
from jax.sharding import PartitionSpec as P

EXTRA = 8
VMEM_BYTES = 48 * 1024 * 1024


def shifted(value, window, planes_on):
    count = lax.axis_size("blk")
    pairs = [(source, (source + planes_on[source % 2] * window) % count) for source in range(count)]
    return lax.ppermute(value, "blk", pairs)


def chip_partner(value, masks):
    count = lax.axis_size("blk")
    return lax.ppermute(value, "blk", [(source, source ^ (2 * masks[source % 2])) for source in range(count)])


def mask_order(chips):
    bits = chips.bit_length() - 1
    return [(m, sum(1 << (bits - 1 - b) for b in range(bits) if m >> b & 1)) for m in range(1, chips)]


def plane_order(planes):
    return [(1, 1)] + [(k, planes + 1 - k) for k in range(2, planes)]


def of_core(core, pair):
    return pair[0] if pair[0] == pair[1] else jnp.where(core == 0, *pair)


def core_partner(value):
    count = lax.axis_size("blk")
    return lax.ppermute(value, "blk", [(source, source ^ 1) for source in range(count)])


def split_two(values):
    high = values.astype(jnp.bfloat16)
    low = (values - high.astype(jnp.float32)).astype(jnp.bfloat16)
    return high, low


def place_of(place_ref, chips):
    place = place_ref[0]
    return (place // 2) & (chips - 1), place & 1


def fetch_kernel(own_ref, out_ref, done):
    copy = pltpu.make_async_copy(own_ref, out_ref, done)
    copy.start()
    copy.wait()


def split_kernel(tiles_ref, straight_ref, turned_ref):
    slots = tiles_ref.shape[0]

    def visit(t):
        tile = tiles_ref[t]
        straight_ref[t, 0], straight_ref[t, 1] = split_two(tile)
        turned_ref[t, 0], turned_ref[t, 1] = split_two(tile.T)

    if slots <= 32:
        for t in range(slots):
            visit(t)
    else:
        lax.fori_loop(0, slots, lambda t, c: (visit(t), c)[1], 0)


def steps_ahead(chip, mask, chips):
    return ((chip ^ mask) - chip) & (chips - 1)


def product_kernel(planes, chips, pairs_ref, place_ref, own_ref, *refs):
    window = 2 * chips
    far = refs[: planes - 1]
    even = refs[planes - 1 : planes + chips - 2]
    odd_ref, straight_ref, turned_ref, message_ref, kept_ref = refs[planes + chips - 2 : planes + chips + 3]
    far_out = refs[planes + chips + 3 : -3]
    whole, parts, total = refs[-3:]
    rows, cols = own_ref.shape
    chip, core = place_of(place_ref, chips)
    spare = jnp.where(core == 0, 1, window - 1)

    def put(place, values):
        whole[place] = values
        high, low = split_two(values)
        parts[place, :, :cols] = high
        parts[place, :, cols:] = low

    put(0, own_ref[...])
    for i, pair in enumerate(plane_order(planes)):
        put(window - 1 + of_core(core, pair), far[i][...])
    for i, pair in enumerate(mask_order(chips)):
        put(2 * steps_ahead(chip, of_core(core, pair), chips), even[i][...])
        put(2 * steps_ahead(chip, of_core(1 - core, pair), chips) + 1 - 2 * core, odd_ref[i + 1])
    put(spare, odd_ref[0])

    total[...] = jnp.zeros_like(total)
    slots = straight_ref.shape[0]

    def product(split_ref, t, place):
        both = jnp.dot(split_ref[t, 0], parts[place], preferred_element_type=jnp.float32)
        rest = jnp.dot(split_ref[t, 1], parts[place, :, :cols], preferred_element_type=jnp.float32)
        return both[:, :cols] + (both[:, cols:] + rest)

    def visit(t, mirrored):
        row_place, col_place = pairs_ref[0, t], pairs_ref[1, t]
        total[row_place] += product(straight_ref, t, col_place)
        if mirrored:
            total[col_place] += product(turned_ref, t, row_place)

    visit(0, False)
    if slots <= 32:
        for t in range(1, slots - 1):
            visit(t, True)
    else:
        lax.fori_loop(1, slots - 1, lambda t, c: (visit(t, True), c)[1], 0)
    visit(slots - 1, False)

    dots = jnp.zeros((1, cols), jnp.float32)
    for place in range(whole.shape[0]):
        dots = dots + jnp.sum(whole[place] * total[place], axis=0, keepdims=True)
    own = own_ref[...]
    norm = jnp.sum(own * own, axis=0, keepdims=True)
    sums = jnp.concatenate([norm, dots, jnp.zeros((EXTRA - 2, cols), jnp.float32)], axis=0)
    message_ref[:rows, :] = total[spare]
    kept_ref[0] = total[0]
    for m in range(1, chips):
        ahead = 2 * steps_ahead(chip, m, chips)
        message_ref[m * rows : (m + 1) * rows, :] = total[ahead + 1 - 2 * core]
        kept_ref[m] = total[ahead]
    message_ref[chips * rows :, :] = sums
    kept_ref[chips] = total[window]
    for i, pair in enumerate(plane_order(planes)[1:]):
        far_out[i][...] = total[window - 1 + of_core(core, pair)]


def pair_kernel(chips, place_ref, sent_ref, kept_ref, got_ref, *outs):
    messages = outs[: chips - 1]
    near_ref, next_ref, sums_ref = outs[chips - 1 :]
    rows = kept_ref.shape[1]
    core = place_of(place_ref, chips)[1]
    sums = sent_ref[chips * rows :, :] + got_ref[chips * rows :, :]
    for message, pair in zip(messages, mask_order(chips)):
        mask = of_core(core, pair)
        message[:rows, :] = kept_ref[mask] + got_ref[pl.ds(pl.multiple_of(mask * rows, rows), rows), :]
        message[rows:, :] = sums
    spare = got_ref[:rows, :]
    near_ref[...] = kept_ref[0] + jnp.where(core == 1, spare, 0.0)
    next_ref[...] = kept_ref[chips] + jnp.where(core == 0, spare, 0.0)
    sums_ref[...] = sums


def plane_kernel(planes, chips, place_ref, near_ref, next_ref, sums_ref, *refs):
    got = refs[: chips - 1]
    far = refs[chips - 1 : chips + planes - 3]
    messages = refs[chips + planes - 3 : -2]
    near_out, sums_out = refs[-2:]
    rows = near_ref.shape[0]
    chip, core = place_of(place_ref, chips)
    near, ahead, sums = near_ref[...], next_ref[...], sums_ref[...]
    for i, pair in enumerate(mask_order(chips)):
        block = got[i][:rows, :]
        same = (chip ^ of_core(core, pair)) < chip
        near = near + jnp.where(same, block, 0.0)
        ahead = ahead + jnp.where(same, 0.0, block)
        sums = sums + got[i][rows:, :]
    near_out[...] = near
    sums_out[...] = sums
    messages[0][:rows, :] = ahead
    for k in range(2, planes):
        messages[k - 1][:rows, :] = far[k - 2][...]
    for message in messages:
        message[rows:, :] = sums


def final_kernel(right_ref, near_ref, sums_ref, *refs):
    solution_ref, residual_ref = refs[-2:]
    rows = near_ref.shape[0]
    image, sums = near_ref[...], sums_ref[...]
    for got in refs[:-2]:
        image = image + got[:rows, :]
        sums = sums + got[rows:, :]
    step_len = sums[0:1, :] / sums[1:2, :]
    right = right_ref[...]
    solution_ref[...] = step_len * right
    residual_ref[...] = right - step_len * image


def call(kernel, smem, operands, outs, scratch=(), space=pltpu.VMEM):
    vmem = pl.BlockSpec(memory_space=pltpu.VMEM)
    return pl.pallas_call(
        kernel,
        in_specs=[pl.BlockSpec(memory_space=pltpu.SMEM)] * len(smem) + [pl.BlockSpec(memory_space=space)] * len(operands),
        out_specs=[vmem] * len(outs),
        out_shape=[jax.ShapeDtypeStruct(shape, kind) for shape, kind in outs],
        scratch_shapes=list(scratch),
        compiler_params=pltpu.CompilerParams(vmem_limit_bytes=VMEM_BYTES),
    )(*smem, *operands)


def per_device(right_side, kernel_tiles, route_pairs):
    count = lax.axis_size("blk")
    window = max(8, min(16, count // 8))
    planes, chips = count // window, window // 2
    rows, cols = right_side.shape
    slots = kernel_tiles.shape[1]
    cover_len = window + planes - 1
    place = lax.axis_index("blk").astype(jnp.int32)
    chip, core = place % window // 2, place % 2
    where = place[None]
    single, half = jnp.float32, jnp.bfloat16

    (own,) = call(fetch_kernel, (), (right_side,), [((rows, cols), single)], [pltpu.SemaphoreType.DMA], pl.ANY)
    straight, turned = call(
        split_kernel, (), (kernel_tiles[0],), [((slots, 2, rows, cols), half), ((slots, 2, cols, rows), half)]
    )
    far = [shifted(right_side, window, (-even, -odd)) for even, odd in plane_order(planes)]
    near = []
    for pair in mask_order(chips):
        near.append(chip_partner(jnp.where((chip ^ of_core(core, pair)) < chip, own, far[0]), pair))
    sent = jnp.stack([jnp.where(core == 0, far[0], own)] + near)
    sent, *rest = lax.optimization_barrier((sent, *far[1:]))
    far = far[:1] + rest
    odd = core_partner(sent)

    block, marked, extra = ((rows, cols), single), ((rows + EXTRA, cols), single), ((EXTRA, cols), single)
    sent, kept, *far_out = call(
        functools.partial(product_kernel, planes, chips),
        (route_pairs.T, where),
        (own, *far, *near, odd, straight, turned),
        [((chips * rows + EXTRA, cols), single), ((chips + 1, rows, cols), single)] + [block] * (planes - 2),
        (
            pltpu.VMEM((cover_len, rows, cols), single),
            pltpu.VMEM((cover_len, rows, 2 * cols), half),
            pltpu.VMEM((cover_len, rows, cols), single),
        ),
    )
    got = core_partner(sent)
    *messages, near, ahead, sums = call(
        functools.partial(pair_kernel, chips), (where,), (sent, kept, got), [marked] * (chips - 1) + [block, block, extra]
    )
    got = [chip_partner(value, pair) for value, pair in zip(messages, mask_order(chips))]
    *messages, near, sums = call(
        functools.partial(plane_kernel, planes, chips),
        (where,),
        (near, ahead, sums, *got, *far_out),
        [marked] * (planes - 1) + [block, extra],
    )
    got = [shifted(value, window, pair) for value, pair in zip(messages, plane_order(planes))]
    return call(final_kernel, (), (own, near, sums, *got), [block, block])


def solution(mesh):
    def run(*args):
        return tuple(per_device(*args))

    return jax.shard_map(
        run,
        mesh=mesh,
        in_specs=(P("blk", None), P("blk", None, None, None), P()),
        out_specs=(P("blk", None), P("blk", None)),
        check_vma=False,
    )
```

```python
import functools

import jax
import jax.numpy as jnp
from jax import lax
from jax.experimental import pallas as pl
from jax.experimental.pallas import tpu as pltpu
from jax.sharding import PartitionSpec as P

EXTRA = 8
VMEM_BYTES = 48 * 1024 * 1024


def shifted(value, steps):
    count = lax.axis_size("blk")
    pairs = [(source, (source + steps) % count) for source in range(count)]
    return lax.ppermute(value, "blk", pairs)


def chip_partner(value, mask):
    count = lax.axis_size("blk")
    return lax.ppermute(value, "blk", [(source, source ^ (2 * mask)) for source in range(count)])


def core_partner(value):
    count = lax.axis_size("blk")
    return lax.ppermute(value, "blk", [(source, source ^ 1) for source in range(count)])


def split_two(values):
    high = values.astype(jnp.bfloat16)
    low = (values - high.astype(jnp.float32)).astype(jnp.bfloat16)
    return high, low


def place_of(place_ref, chips):
    place = place_ref[0]
    return (place // 2) & (chips - 1), place & 1


def fetch_kernel(own_ref, out_ref, done):
    copy = pltpu.make_async_copy(own_ref, out_ref, done)
    copy.start()
    copy.wait()


def split_kernel(tiles_ref, straight_ref, turned_ref):
    slots = tiles_ref.shape[0]

    def visit(t):
        tile = tiles_ref[t]
        straight_ref[t, 0], straight_ref[t, 1] = split_two(tile)
        turned_ref[t, 0], turned_ref[t, 1] = split_two(tile.T)

    if slots <= 32:
        for t in range(slots):
            visit(t)
    else:
        lax.fori_loop(0, slots, lambda t, c: (visit(t), c)[1], 0)


def steps_ahead(chip, mask, chips):
    return ((chip ^ mask) - chip) & (chips - 1)


def product_kernel(planes, chips, pairs_ref, place_ref, own_ref, *refs):
    window = 2 * chips
    far = refs[: planes - 1]
    even = refs[planes - 1 : planes + chips - 2]
    odd_ref, straight_ref, turned_ref, message_ref, kept_ref = refs[planes + chips - 2 : planes + chips + 3]
    far_out = refs[planes + chips + 3 : -3]
    whole, parts, total = refs[-3:]
    rows, cols = own_ref.shape
    chip, core = place_of(place_ref, chips)
    spare = jnp.where(core == 0, 1, window - 1)

    def put(place, values):
        whole[place] = values
        high, low = split_two(values)
        parts[place, :, :cols] = high
        parts[place, :, cols:] = low

    put(0, own_ref[...])
    for k in range(1, planes):
        put(window - 1 + k, far[k - 1][...])
    for m in range(1, chips):
        ahead = 2 * steps_ahead(chip, m, chips)
        put(ahead, even[m - 1][...])
        put(ahead + 1 - 2 * core, odd_ref[m])
    put(spare, odd_ref[0])

    total[...] = jnp.zeros_like(total)
    slots = straight_ref.shape[0]

    def product(split_ref, t, place):
        both = jnp.dot(split_ref[t, 0], parts[place], preferred_element_type=jnp.float32)
        rest = jnp.dot(split_ref[t, 1], parts[place, :, :cols], preferred_element_type=jnp.float32)
        return both[:, :cols] + (both[:, cols:] + rest)

    def visit(t, mirrored):
        row_place, col_place = pairs_ref[0, t], pairs_ref[1, t]
        total[row_place] += product(straight_ref, t, col_place)
        if mirrored:
            total[col_place] += product(turned_ref, t, row_place)

    visit(0, False)
    if slots <= 32:
        for t in range(1, slots - 1):
            visit(t, True)
    else:
        lax.fori_loop(1, slots - 1, lambda t, c: (visit(t, True), c)[1], 0)
    visit(slots - 1, False)

    dots = jnp.zeros((1, cols), jnp.float32)
    for place in range(whole.shape[0]):
        dots = dots + jnp.sum(whole[place] * total[place], axis=0, keepdims=True)
    own = own_ref[...]
    norm = jnp.sum(own * own, axis=0, keepdims=True)
    sums = jnp.concatenate([norm, dots, jnp.zeros((EXTRA - 2, cols), jnp.float32)], axis=0)
    message_ref[:rows, :] = total[spare]
    kept_ref[0] = total[0]
    for m in range(1, chips):
        ahead = 2 * steps_ahead(chip, m, chips)
        message_ref[m * rows : (m + 1) * rows, :] = total[ahead + 1 - 2 * core]
        kept_ref[m] = total[ahead]
    message_ref[chips * rows :, :] = sums
    kept_ref[chips] = total[window]
    for k in range(2, planes):
        far_out[k - 2][...] = total[window - 1 + k]


def pair_kernel(chips, place_ref, sent_ref, kept_ref, got_ref, *outs):
    messages = outs[: chips - 1]
    near_ref, next_ref, sums_ref = outs[chips - 1 :]
    rows = kept_ref.shape[1]
    core = place_of(place_ref, chips)[1]
    sums = sent_ref[chips * rows :, :] + got_ref[chips * rows :, :]
    for m in range(1, chips):
        messages[m - 1][:rows, :] = kept_ref[m] + got_ref[m * rows : (m + 1) * rows, :]
        messages[m - 1][rows:, :] = sums
    spare = got_ref[:rows, :]
    near_ref[...] = kept_ref[0] + jnp.where(core == 1, spare, 0.0)
    next_ref[...] = kept_ref[chips] + jnp.where(core == 0, spare, 0.0)
    sums_ref[...] = sums


def plane_kernel(planes, chips, place_ref, near_ref, next_ref, sums_ref, *refs):
    got = refs[: chips - 1]
    far = refs[chips - 1 : chips + planes - 3]
    messages = refs[chips + planes - 3 : -2]
    near_out, sums_out = refs[-2:]
    rows = near_ref.shape[0]
    chip = place_of(place_ref, chips)[0]
    near, ahead, sums = near_ref[...], next_ref[...], sums_ref[...]
    for m in range(1, chips):
        block = got[m - 1][:rows, :]
        same = (chip ^ m) < chip
        near = near + jnp.where(same, block, 0.0)
        ahead = ahead + jnp.where(same, 0.0, block)
        sums = sums + got[m - 1][rows:, :]
    near_out[...] = near
    sums_out[...] = sums
    messages[0][:rows, :] = ahead
    for k in range(2, planes):
        messages[k - 1][:rows, :] = far[k - 2][...]
    for message in messages:
        message[rows:, :] = sums


def final_kernel(right_ref, near_ref, sums_ref, *refs):
    solution_ref, residual_ref = refs[-2:]
    rows = near_ref.shape[0]
    image, sums = near_ref[...], sums_ref[...]
    for got in refs[:-2]:
        image = image + got[:rows, :]
        sums = sums + got[rows:, :]
    step_len = sums[0:1, :] / sums[1:2, :]
    right = right_ref[...]
    solution_ref[...] = step_len * right
    residual_ref[...] = right - step_len * image


def call(kernel, smem, operands, outs, scratch=(), space=pltpu.VMEM):
    vmem = pl.BlockSpec(memory_space=pltpu.VMEM)
    return pl.pallas_call(
        kernel,
        in_specs=[pl.BlockSpec(memory_space=pltpu.SMEM)] * len(smem) + [pl.BlockSpec(memory_space=space)] * len(operands),
        out_specs=[vmem] * len(outs),
        out_shape=[jax.ShapeDtypeStruct(shape, kind) for shape, kind in outs],
        scratch_shapes=list(scratch),
        compiler_params=pltpu.CompilerParams(vmem_limit_bytes=VMEM_BYTES),
    )(*smem, *operands)


def per_device(right_side, kernel_tiles, route_pairs):
    count = lax.axis_size("blk")
    window = max(8, min(16, count // 8))
    planes, chips = count // window, window // 2
    rows, cols = right_side.shape
    slots = kernel_tiles.shape[1]
    cover_len = window + planes - 1
    place = lax.axis_index("blk").astype(jnp.int32)
    chip, core = place % window // 2, place % 2
    where = place[None]
    single, half = jnp.float32, jnp.bfloat16

    (own,) = call(fetch_kernel, (), (right_side,), [((rows, cols), single)], [pltpu.SemaphoreType.DMA], pl.ANY)
    straight, turned = call(
        split_kernel, (), (kernel_tiles[0],), [((slots, 2, rows, cols), half), ((slots, 2, cols, rows), half)]
    )
    order = [planes - 1, *range(1, planes - 1)]
    own, *far = lax.optimization_barrier((own, *[shifted(right_side, -k * window) for k in order]))
    far = [value for _, value in sorted(zip(order, far), key=lambda item: item[0])]
    even = [chip_partner(jnp.where((chip ^ m) < chip, own, far[0]), m) for m in range(1, chips)]
    odd = core_partner(jnp.stack([jnp.where(core == 0, far[0], own)] + even))

    block, marked, extra = ((rows, cols), single), ((rows + EXTRA, cols), single), ((EXTRA, cols), single)
    sent, kept, *far_out = call(
        functools.partial(product_kernel, planes, chips),
        (route_pairs.T, where),
        (own, *far, *even, odd, straight, turned),
        [((chips * rows + EXTRA, cols), single), ((chips + 1, rows, cols), single)] + [block] * (planes - 2),
        (
            pltpu.VMEM((cover_len, rows, cols), single),
            pltpu.VMEM((cover_len, rows, 2 * cols), half),
            pltpu.VMEM((cover_len, rows, cols), single),
        ),
    )
    got = core_partner(sent)
    *messages, near, ahead, sums = call(
        functools.partial(pair_kernel, chips), (where,), (sent, kept, got), [marked] * (chips - 1) + [block, block, extra]
    )
    got = [chip_partner(value, m) for m, value in enumerate(messages, 1)]
    *messages, near, sums = call(
        functools.partial(plane_kernel, planes, chips),
        (where,),
        (near, ahead, sums, *got, *far_out),
        [marked] * (planes - 1) + [block, extra],
    )
    got = [shifted(value, k * window) for k, value in enumerate(messages, 1)]
    return call(final_kernel, (), (own, near, sums, *got), [block, block])


def solution(mesh):
    def run(*args):
        return tuple(per_device(*args))

    return jax.shard_map(
        run,
        mesh=mesh,
        in_specs=(P("blk", None), P("blk", None, None, None), P()),
        out_specs=(P("blk", None), P("blk", None)),
        check_vma=False,
    )
```

```python
import functools

import jax
import jax.numpy as jnp
from jax import lax
from jax.experimental import pallas as pl
from jax.experimental.pallas import tpu as pltpu
from jax.sharding import PartitionSpec as P

EXTRA = 8
VMEM_BYTES = 48 * 1024 * 1024
BESIDE = pl.CostEstimate(flops=10**10, bytes_accessed=0, transcendentals=0)


def shifted(value, steps):
    count = lax.axis_size("blk")
    pairs = [(source, (source + steps) % count) for source in range(count)]
    return lax.ppermute(value, "blk", pairs)


def chip_partner(value, mask):
    count = lax.axis_size("blk")
    return lax.ppermute(value, "blk", [(source, source ^ (2 * mask)) for source in range(count)])


def core_partner(value):
    count = lax.axis_size("blk")
    return lax.ppermute(value, "blk", [(source, source ^ 1) for source in range(count)])


def split_two(values):
    high = values.astype(jnp.bfloat16)
    low = (values - high.astype(jnp.float32)).astype(jnp.bfloat16)
    return high, low


def place_of(place_ref, chips):
    place = place_ref[0]
    return (place // 2) & (chips - 1), place & 1


def fetch_kernel(own_ref, out_ref, done):
    copy = pltpu.make_async_copy(own_ref, out_ref, done)
    copy.start()
    copy.wait()


def split_kernel(tiles_ref, straight_ref, turned_ref):
    slots = tiles_ref.shape[0]

    def visit(t):
        tile = tiles_ref[t]
        straight_ref[t, 0], straight_ref[t, 1] = split_two(tile)
        turned_ref[t, 0], turned_ref[t, 1] = split_two(tile.T)

    if slots <= 32:
        for t in range(slots):
            visit(t)
    else:
        lax.fori_loop(0, slots, lambda t, c: (visit(t), c)[1], 0)


def split_blocks_kernel(*refs):
    out_ref = refs[-1]
    cols = out_ref.shape[2] // 2
    for i, block in enumerate(refs[:-1]):
        out_ref[i, :, :cols], out_ref[i, :, cols:] = split_two(block[...])


def add_kernel(*refs):
    total = refs[0][...]
    for block in refs[1:-1]:
        total = total + block[...]
    refs[-1][...] = total


def steps_ahead(chip, mask, chips):
    return ((chip ^ mask) - chip) & (chips - 1)


def product_kernel(planes, chips, pairs_ref, place_ref, own_ref, *refs):
    window = 2 * chips
    far = refs[: planes - 1]
    even = refs[planes - 1 : planes + chips - 2]
    odd_ref, middle_ref, straight_ref, turned_ref, message_ref, kept_ref = refs[planes + chips - 2 : planes + chips + 4]
    far_out = refs[planes + chips + 4 : -3]
    whole, parts, total = refs[-3:]
    rows, cols = own_ref.shape
    chip, core = place_of(place_ref, chips)
    spare = jnp.where(core == 0, 1, window - 1)

    def put(place, values):
        whole[place] = values
        high, low = split_two(values)
        parts[place, :, :cols] = high
        parts[place, :, cols:] = low

    put(0, own_ref[...])
    for k in (1, planes - 1):
        put(window - 1 + k, far[k - 1][...])
    for k in range(2, planes - 1):
        whole[window - 1 + k] = far[k - 1][...]
        parts[window - 1 + k] = middle_ref[k - 2]
    for m in range(1, chips):
        ahead = 2 * steps_ahead(chip, m, chips)
        put(ahead, even[m - 1][...])
        put(ahead + 1 - 2 * core, odd_ref[m])
    put(spare, odd_ref[0])

    total[...] = jnp.zeros_like(total)
    slots = straight_ref.shape[0]

    def product(split_ref, t, place):
        both = jnp.dot(split_ref[t, 0], parts[place], preferred_element_type=jnp.float32)
        rest = jnp.dot(split_ref[t, 1], parts[place, :, :cols], preferred_element_type=jnp.float32)
        return both[:, :cols] + (both[:, cols:] + rest)

    def visit(t, mirrored):
        row_place, col_place = pairs_ref[0, t], pairs_ref[1, t]
        total[row_place] += product(straight_ref, t, col_place)
        if mirrored:
            total[col_place] += product(turned_ref, t, row_place)

    visit(0, False)
    if slots <= 32:
        for t in range(1, slots - 1):
            visit(t, True)
    else:
        lax.fori_loop(1, slots - 1, lambda t, c: (visit(t, True), c)[1], 0)
    visit(slots - 1, False)

    dots = jnp.zeros((1, cols), jnp.float32)
    for place in range(whole.shape[0]):
        dots = dots + jnp.sum(whole[place] * total[place], axis=0, keepdims=True)
    own = own_ref[...]
    norm = jnp.sum(own * own, axis=0, keepdims=True)
    sums = jnp.concatenate([norm, dots, jnp.zeros((EXTRA - 2, cols), jnp.float32)], axis=0)
    message_ref[:rows, :] = total[spare]
    kept_ref[0] = total[0]
    for m in range(1, chips):
        ahead = 2 * steps_ahead(chip, m, chips)
        message_ref[m * rows : (m + 1) * rows, :] = total[ahead + 1 - 2 * core]
        kept_ref[m] = total[ahead]
    message_ref[chips * rows :, :] = sums
    kept_ref[chips] = total[window]
    for k in range(2, planes):
        far_out[k - 2][...] = total[window - 1 + k]


def pair_kernel(chips, place_ref, sent_ref, kept_ref, got_ref, *outs):
    messages = outs[: chips - 1]
    near_ref, next_ref, sums_ref = outs[chips - 1 :]
    rows = kept_ref.shape[1]
    core = place_of(place_ref, chips)[1]
    sums = sent_ref[chips * rows :, :] + got_ref[chips * rows :, :]
    for m in range(1, chips):
        messages[m - 1][:rows, :] = kept_ref[m] + got_ref[m * rows : (m + 1) * rows, :]
        messages[m - 1][rows:, :] = sums
    spare = got_ref[:rows, :]
    near_ref[...] = kept_ref[0] + jnp.where(core == 1, spare, 0.0)
    next_ref[...] = kept_ref[chips] + jnp.where(core == 0, spare, 0.0)
    sums_ref[...] = sums


def plane_kernel(chips, place_ref, near_ref, next_ref, sums_ref, last_ref, *refs):
    got = refs[: chips - 1]
    next_out, last_out, near_out, sums_out = refs[chips - 1 :]
    rows = near_ref.shape[0]
    chip = place_of(place_ref, chips)[0]
    near, ahead, sums = near_ref[...], next_ref[...], sums_ref[...]
    for m in range(1, chips):
        block = got[m - 1][:rows, :]
        same = (chip ^ m) < chip
        near = near + jnp.where(same, block, 0.0)
        ahead = ahead + jnp.where(same, 0.0, block)
        sums = sums + got[m - 1][rows:, :]
    near_out[...] = near
    sums_out[...] = sums
    next_out[:rows, :] = ahead
    last_out[:rows, :] = last_ref[...]
    for message in (next_out, last_out):
        message[rows:, :] = sums


def final_kernel(right_ref, near_ref, middle_ref, sums_ref, *refs):
    solution_ref, residual_ref = refs[-2:]
    rows = near_ref.shape[0]
    image, sums = near_ref[...] + middle_ref[...], sums_ref[...]
    for got in refs[:2]:
        image = image + got[:rows, :]
        sums = sums + got[rows:, :]
    for got in refs[2:-2]:
        sums = sums + got[...]
    step_len = sums[0:1, :] / sums[1:2, :]
    right = right_ref[...]
    solution_ref[...] = step_len * right
    residual_ref[...] = right - step_len * image


def call(kernel, smem, operands, outs, scratch=(), space=pltpu.VMEM, cost=None):
    vmem = pl.BlockSpec(memory_space=pltpu.VMEM)
    return pl.pallas_call(
        kernel,
        in_specs=[pl.BlockSpec(memory_space=pltpu.SMEM)] * len(smem) + [pl.BlockSpec(memory_space=space)] * len(operands),
        out_specs=[vmem] * len(outs),
        out_shape=[jax.ShapeDtypeStruct(shape, kind) for shape, kind in outs],
        scratch_shapes=list(scratch),
        cost_estimate=cost,
        compiler_params=pltpu.CompilerParams(vmem_limit_bytes=VMEM_BYTES),
    )(*smem, *operands)


def per_device(right_side, kernel_tiles, route_pairs):
    count = lax.axis_size("blk")
    window = max(8, min(16, count // 8))
    planes, chips = count // window, window // 2
    rows, cols = right_side.shape
    slots = kernel_tiles.shape[1]
    cover_len = window + planes - 1
    place = lax.axis_index("blk").astype(jnp.int32)
    chip, core = place % window // 2, place % 2
    where = place[None]
    single, half = jnp.float32, jnp.bfloat16

    (own,) = call(fetch_kernel, (), (right_side,), [((rows, cols), single)], [pltpu.SemaphoreType.DMA], pl.ANY)
    straight, turned = call(
        split_kernel, (), (kernel_tiles[0],), [((slots, 2, rows, cols), half), ((slots, 2, cols, rows), half)]
    )
    far = {k: shifted(right_side, -k * window) for k in (planes - 1, *range(1, planes - 1))}
    own, far[planes - 1], far[1] = lax.optimization_barrier((own, far[planes - 1], far[1]))
    middle = range(2, planes - 1)
    (middle_parts,) = call(
        split_blocks_kernel, (), [far[k] for k in middle], [((len(middle), rows, 2 * cols), half)], cost=BESIDE
    )
    even = [chip_partner(jnp.where((chip ^ m) < chip, own, far[1]), m) for m in range(1, chips)]
    odd = core_partner(jnp.stack([jnp.where(core == 0, far[1], own)] + even))

    block, marked, extra = ((rows, cols), single), ((rows + EXTRA, cols), single), ((EXTRA, cols), single)
    sent, kept, *far_out = call(
        functools.partial(product_kernel, planes, chips),
        (route_pairs.T, where),
        (own, *[far[k] for k in range(1, planes)], *even, odd, middle_parts, straight, turned),
        [((chips * rows + EXTRA, cols), single), ((chips + 1, rows, cols), single)] + [block] * (planes - 2),
        (
            pltpu.VMEM((cover_len, rows, cols), single),
            pltpu.VMEM((cover_len, rows, 2 * cols), half),
            pltpu.VMEM((cover_len, rows, cols), single),
        ),
    )
    got = core_partner(sent)
    *messages, near, ahead, sums = call(
        functools.partial(pair_kernel, chips), (where,), (sent, kept, got), [marked] * (chips - 1) + [block, block, extra]
    )
    middle_got = [shifted(far_out[k - 2], k * window) for k in middle]
    (middle_sum,) = call(add_kernel, (), middle_got, [block], cost=BESIDE)
    got = [chip_partner(value, m) for m, value in enumerate(messages, 1)]
    ahead, last, near, sums = call(
        functools.partial(plane_kernel, chips), (where,), (near, ahead, sums, far_out[-1], *got), [marked, marked, block, extra]
    )
    got = [shifted(ahead, window), *[shifted(sums, k * window) for k in middle], shifted(last, (planes - 1) * window)]
    return call(
        final_kernel, (), (own, near, middle_sum, sums, got[0], got[-1], *got[1:-1]), [block, block]
    )


def solution(mesh):
    def run(*args):
        return tuple(per_device(*args))

    return jax.shard_map(
        run,
        mesh=mesh,
        in_specs=(P("blk", None), P("blk", None, None, None), P()),
        out_specs=(P("blk", None), P("blk", None)),
        check_vma=False,
    )
```

```python
import functools

import jax
import jax.numpy as jnp
from jax import lax
from jax.experimental import pallas as pl
from jax.experimental.pallas import tpu as pltpu
from jax.sharding import PartitionSpec as P

EXTRA = 8
VMEM_BYTES = 48 * 1024 * 1024
BESIDE = pl.CostEstimate(flops=10**10, bytes_accessed=0, transcendentals=0)


def shifted(value, steps):
    count = lax.axis_size("blk")
    pairs = [(source, (source + steps) % count) for source in range(count)]
    return lax.ppermute(value, "blk", pairs)


def chip_partner(value, mask):
    count = lax.axis_size("blk")
    return lax.ppermute(value, "blk", [(source, source ^ (2 * mask)) for source in range(count)])


def core_partner(value):
    count = lax.axis_size("blk")
    return lax.ppermute(value, "blk", [(source, source ^ 1) for source in range(count)])


def split_two(values):
    high = values.astype(jnp.bfloat16)
    low = (values - high.astype(jnp.float32)).astype(jnp.bfloat16)
    return high, low


def place_of(place_ref, chips):
    place = place_ref[0]
    return (place // 2) & (chips - 1), place & 1


def prepare_kernel(own_ref, tiles_ref, own_out, straight_ref, turned_ref):
    own_out[...] = own_ref[...]
    slots, rows, cols = tiles_ref.shape

    def visit(t):
        tile = tiles_ref[t]
        straight_ref[t, :rows, :], straight_ref[t, rows:, :] = split_two(tile)
        turned_ref[t, :cols, :], turned_ref[t, cols:, :] = split_two(tile.T)

    if slots <= 32:
        for t in range(slots):
            visit(t)
    else:
        lax.fori_loop(0, slots, lambda t, c: (visit(t), c)[1], 0)


def split_blocks_kernel(*refs):
    out_ref = refs[-1]
    cols = out_ref.shape[2] // 2
    for i, block in enumerate(refs[:-1]):
        out_ref[i, :, :cols], out_ref[i, :, cols:] = split_two(block[...])


def middle_kernel(sums_ref, *refs):
    total_ref, sums_out = refs[-2:]
    total = refs[0][...]
    for block in refs[1:-2]:
        total = total + block[...]
    total_ref[...] = total
    sums_out[...] = sums_ref[...]


def steps_ahead(chip, mask, chips):
    return ((chip ^ mask) - chip) & (chips - 1)


def product_kernel(planes, chips, pairs_ref, place_ref, own_ref, *refs):
    window = 2 * chips
    far = refs[: planes - 1]
    even = refs[planes - 1 : planes + chips - 2]
    odd_ref, middle_ref, straight_ref, turned_ref, message_ref, kept_ref = refs[planes + chips - 2 : planes + chips + 4]
    far_out = refs[planes + chips + 4 : -3]
    whole, parts, total = refs[-3:]
    rows, cols = own_ref.shape
    chip, core = place_of(place_ref, chips)
    spare = jnp.where(core == 0, 1, window - 1)

    def put(place, values):
        whole[place] = values
        high, low = split_two(values)
        parts[place, :, :cols] = high
        parts[place, :, cols:] = low

    put(0, own_ref[...])
    for k in (1, planes - 1):
        put(window - 1 + k, far[k - 1][...])
    for k in range(2, planes - 1):
        whole[window - 1 + k] = far[k - 1][...]
        parts[window - 1 + k] = middle_ref[k - 2]
    for m in range(1, chips):
        ahead = 2 * steps_ahead(chip, m, chips)
        put(ahead, even[m - 1][...])
        put(ahead + 1 - 2 * core, odd_ref[m])
    put(spare, odd_ref[0])

    total[...] = jnp.zeros_like(total)
    slots = straight_ref.shape[0]

    def product(split_ref, t, place):
        both = jnp.dot(split_ref[t], parts[place], preferred_element_type=jnp.float32)
        high, low = both[:rows], both[rows:]
        return high[:, :cols] + ((high[:, cols:] + low[:, :cols]) + low[:, cols:])

    def visit(t, mirrored):
        row_place, col_place = pairs_ref[0, t], pairs_ref[1, t]
        total[row_place] += product(straight_ref, t, col_place)
        if mirrored:
            total[col_place] += product(turned_ref, t, row_place)

    visit(0, False)
    if slots <= 32:
        for t in range(1, slots - 1):
            visit(t, True)
    else:
        lax.fori_loop(1, slots - 1, lambda t, c: (visit(t, True), c)[1], 0)
    visit(slots - 1, False)

    dots = jnp.zeros((1, cols), jnp.float32)
    for place in range(whole.shape[0]):
        dots = dots + jnp.sum(whole[place] * total[place], axis=0, keepdims=True)
    own = own_ref[...]
    norm = jnp.sum(own * own, axis=0, keepdims=True)
    sums = jnp.concatenate([norm, dots, jnp.zeros((EXTRA - 2, cols), jnp.float32)], axis=0)
    message_ref[:rows, :] = total[spare]
    kept_ref[0] = total[0]
    for m in range(1, chips):
        ahead = 2 * steps_ahead(chip, m, chips)
        message_ref[m * rows : (m + 1) * rows, :] = total[ahead + 1 - 2 * core]
        kept_ref[m] = total[ahead]
    message_ref[chips * rows :, :] = sums
    kept_ref[chips] = total[window]
    for k in range(2, planes):
        far_out[k - 2][...] = total[window - 1 + k]


def pair_kernel(chips, place_ref, sent_ref, kept_ref, got_ref, *outs):
    messages = outs[: chips - 1]
    near_ref, next_ref, sums_ref = outs[chips - 1 :]
    rows = kept_ref.shape[1]
    core = place_of(place_ref, chips)[1]
    sums = sent_ref[chips * rows :, :] + got_ref[chips * rows :, :]
    for m in range(1, chips):
        messages[m - 1][:rows, :] = kept_ref[m] + got_ref[m * rows : (m + 1) * rows, :]
        messages[m - 1][rows:, :] = sums
    spare = got_ref[:rows, :]
    near_ref[...] = kept_ref[0] + jnp.where(core == 1, spare, 0.0)
    next_ref[...] = kept_ref[chips] + jnp.where(core == 0, spare, 0.0)
    sums_ref[...] = sums


def plane_kernel(chips, place_ref, near_ref, next_ref, sums_ref, last_ref, *refs):
    got = refs[: chips - 1]
    next_out, last_out, near_out, sums_out = refs[chips - 1 :]
    rows = near_ref.shape[0]
    chip = place_of(place_ref, chips)[0]
    near, ahead, sums = near_ref[...], next_ref[...], sums_ref[...]
    for m in range(1, chips):
        block = got[m - 1][:rows, :]
        same = (chip ^ m) < chip
        near = near + jnp.where(same, block, 0.0)
        ahead = ahead + jnp.where(same, 0.0, block)
        sums = sums + got[m - 1][rows:, :]
    near_out[...] = near
    sums_out[...] = sums
    next_out[:rows, :] = ahead
    last_out[:rows, :] = last_ref[...]
    for message in (next_out, last_out):
        message[rows:, :] = sums


def final_kernel(right_ref, near_ref, middle_ref, sums_ref, *refs):
    solution_ref, residual_ref = refs[-2:]
    rows = near_ref.shape[0]
    image, sums = near_ref[...] + middle_ref[...], sums_ref[...]
    for got in refs[:2]:
        image = image + got[:rows, :]
        sums = sums + got[rows:, :]
    for got in refs[2:-2]:
        sums = sums + got[...]
    step_len = sums[0:1, :] / sums[1:2, :]
    right = right_ref[...]
    solution_ref[...] = step_len * right
    residual_ref[...] = right - step_len * image


def call(kernel, smem, operands, outs, scratch=(), cost=None):
    vmem = pl.BlockSpec(memory_space=pltpu.VMEM)
    return pl.pallas_call(
        kernel,
        in_specs=[pl.BlockSpec(memory_space=pltpu.SMEM)] * len(smem) + [vmem] * len(operands),
        out_specs=[vmem] * len(outs),
        out_shape=[jax.ShapeDtypeStruct(shape, kind) for shape, kind in outs],
        scratch_shapes=list(scratch),
        cost_estimate=cost,
        compiler_params=pltpu.CompilerParams(vmem_limit_bytes=VMEM_BYTES),
    )(*smem, *operands)


def per_device(right_side, kernel_tiles, route_pairs):
    count = lax.axis_size("blk")
    window = max(8, min(16, count // 8))
    planes, chips = count // window, window // 2
    rows, cols = right_side.shape
    slots = kernel_tiles.shape[1]
    cover_len = window + planes - 1
    place = lax.axis_index("blk").astype(jnp.int32)
    chip, core = place % window // 2, place % 2
    where = place[None]
    single, half = jnp.float32, jnp.bfloat16

    own, straight, turned = call(
        prepare_kernel,
        (),
        (right_side, kernel_tiles[0]),
        [((rows, cols), single), ((slots, 2 * rows, cols), half), ((slots, 2 * cols, rows), half)],
    )
    far = {k: shifted(right_side, -k * window) for k in (planes - 1, *range(1, planes - 1))}
    own, far[planes - 1], far[1] = lax.optimization_barrier((own, far[planes - 1], far[1]))
    middle = range(2, planes - 1)
    (middle_parts,) = call(
        split_blocks_kernel, (), [far[k] for k in middle], [((len(middle), rows, 2 * cols), half)], cost=BESIDE
    )
    even = [chip_partner(jnp.where((chip ^ m) < chip, own, far[1]), m) for m in range(1, chips)]
    odd = core_partner(jnp.stack([jnp.where(core == 0, far[1], own)] + even))

    block, marked, extra = ((rows, cols), single), ((rows + EXTRA, cols), single), ((EXTRA, cols), single)
    sent, kept, *far_out = call(
        functools.partial(product_kernel, planes, chips),
        (route_pairs.T, where),
        (own, *[far[k] for k in range(1, planes)], *even, odd, middle_parts, straight, turned),
        [((chips * rows + EXTRA, cols), single), ((chips + 1, rows, cols), single)] + [block] * (planes - 2),
        (
            pltpu.VMEM((cover_len, rows, cols), single),
            pltpu.VMEM((cover_len, rows, 2 * cols), half),
            pltpu.VMEM((cover_len, rows, cols), single),
        ),
    )
    got = core_partner(sent)
    *messages, near, ahead, sums = call(
        functools.partial(pair_kernel, chips), (where,), (sent, kept, got), [marked] * (chips - 1) + [block, block, extra]
    )
    middle_got = [shifted(far_out[k - 2], k * window) for k in middle]
    got = [chip_partner(value, m) for m, value in enumerate(messages, 1)]
    ahead, last, near, sums = call(
        functools.partial(plane_kernel, chips), (where,), (near, ahead, sums, far_out[-1], *got), [marked, marked, block, extra]
    )
    middle_sum, passed = call(middle_kernel, (), (sums, *middle_got), [block, extra], cost=BESIDE)
    got = [shifted(ahead, window), *[shifted(passed, k * window) for k in middle], shifted(last, (planes - 1) * window)]
    return call(
        final_kernel, (), (own, near, middle_sum, sums, got[0], got[-1], *got[1:-1]), [block, block]
    )


def solution(mesh):
    def run(*args):
        return tuple(per_device(*args))

    return jax.shard_map(
        run,
        mesh=mesh,
        in_specs=(P("blk", None), P("blk", None, None, None), P()),
        out_specs=(P("blk", None), P("blk", None)),
        check_vma=False,
    )
```

```python
import functools

import jax
import jax.numpy as jnp
from jax import lax
from jax.experimental import pallas as pl
from jax.experimental.pallas import tpu as pltpu
from jax.sharding import PartitionSpec as P

EXTRA = 8
VMEM_BYTES = 48 * 1024 * 1024
BESIDE = pl.CostEstimate(flops=10**10, bytes_accessed=0, transcendentals=0)


def shifted(value, steps):
    count = lax.axis_size("blk")
    pairs = [(source, (source + steps) % count) for source in range(count)]
    return lax.ppermute(value, "blk", pairs)


def chip_partner(value, mask):
    count = lax.axis_size("blk")
    return lax.ppermute(value, "blk", [(source, source ^ (2 * mask)) for source in range(count)])


def core_partner(value):
    count = lax.axis_size("blk")
    return lax.ppermute(value, "blk", [(source, source ^ 1) for source in range(count)])


def split_two(values):
    high = values.astype(jnp.bfloat16)
    low = (values - high.astype(jnp.float32)).astype(jnp.bfloat16)
    return high, low


def place_of(place_ref, chips):
    place = place_ref[0]
    return (place // 2) & (chips - 1), place & 1


def prepare_kernel(own_ref, tiles_ref, own_out, straight_ref, turned_ref):
    own_out[...] = own_ref[...]
    slots, rows, cols = tiles_ref.shape

    def visit(t):
        tile = tiles_ref[t]
        straight_ref[t, :rows, :], straight_ref[t, rows:, :] = split_two(tile)
        turned_ref[t, :cols, :], turned_ref[t, cols:, :] = split_two(tile.T)

    if slots <= 32:
        for t in range(slots):
            visit(t)
    else:
        lax.fori_loop(0, slots, lambda t, c: (visit(t), c)[1], 0)


def split_blocks_kernel(*refs):
    out_ref = refs[-1]
    cols = out_ref.shape[2] // 2
    for i, block in enumerate(refs[:-1]):
        out_ref[i, :, :cols], out_ref[i, :, cols:] = split_two(block[...])


def add_kernel(*refs):
    total = refs[0][...]
    for block in refs[1:-1]:
        total = total + block[...]
    refs[-1][...] = total


def near_kernel(near_ref, middle_ref, sums_ref, next_ref, near_out, sums_out):
    rows = near_ref.shape[0]
    near_out[...] = near_ref[...] + middle_ref[...] + next_ref[:rows, :]
    sums_out[...] = sums_ref[...] + next_ref[rows:, :]


def steps_ahead(chip, mask, chips):
    return ((chip ^ mask) - chip) & (chips - 1)


def product_kernel(planes, chips, pairs_ref, place_ref, own_ref, *refs):
    window = 2 * chips
    far = refs[: planes - 1]
    even = refs[planes - 1 : planes + chips - 2]
    odd_ref, middle_ref, straight_ref, turned_ref, message_ref, kept_ref = refs[planes + chips - 2 : planes + chips + 4]
    far_out = refs[planes + chips + 4 : -3]
    whole, parts, total = refs[-3:]
    rows, cols = own_ref.shape
    chip, core = place_of(place_ref, chips)
    spare = jnp.where(core == 0, 1, window - 1)

    def put(place, values):
        whole[place] = values
        high, low = split_two(values)
        parts[place, :, :cols] = high
        parts[place, :, cols:] = low

    put(0, own_ref[...])
    for k in (1, planes - 1):
        put(window - 1 + k, far[k - 1][...])
    for k in range(2, planes - 1):
        whole[window - 1 + k] = far[k - 1][...]
        parts[window - 1 + k] = middle_ref[k - 2]
    for m in range(1, chips):
        ahead = 2 * steps_ahead(chip, m, chips)
        put(ahead, even[m - 1][...])
        put(ahead + 1 - 2 * core, odd_ref[m])
    put(spare, odd_ref[0])

    total[...] = jnp.zeros_like(total)
    slots = straight_ref.shape[0]

    def product(split_ref, t, place):
        high = jnp.dot(split_ref[t, :rows], parts[place], preferred_element_type=jnp.float32)
        low = jnp.dot(split_ref[t, rows:], parts[place, :, :cols], preferred_element_type=jnp.float32)
        return high[:, :cols] + (high[:, cols:] + low)

    def visit(t, mirrored):
        row_place, col_place = pairs_ref[0, t], pairs_ref[1, t]
        total[row_place] += product(straight_ref, t, col_place)
        if mirrored:
            total[col_place] += product(turned_ref, t, row_place)

    visit(0, False)
    if slots <= 32:
        for t in range(1, slots - 1):
            visit(t, True)
    else:
        lax.fori_loop(1, slots - 1, lambda t, c: (visit(t, True), c)[1], 0)
    visit(slots - 1, False)

    dots = jnp.zeros((1, cols), jnp.float32)
    for place in range(whole.shape[0]):
        dots = dots + jnp.sum(whole[place] * total[place], axis=0, keepdims=True)
    own = own_ref[...]
    norm = jnp.sum(own * own, axis=0, keepdims=True)
    sums = jnp.concatenate([norm, dots, jnp.zeros((EXTRA - 2, cols), jnp.float32)], axis=0)
    message_ref[:rows, :] = total[spare]
    kept_ref[0] = total[0]
    for m in range(1, chips):
        ahead = 2 * steps_ahead(chip, m, chips)
        message_ref[m * rows : (m + 1) * rows, :] = total[ahead + 1 - 2 * core]
        kept_ref[m] = total[ahead]
    message_ref[chips * rows :, :] = sums
    kept_ref[chips] = total[window]
    for k in range(2, planes):
        far_out[k - 2][...] = total[window - 1 + k]


def pair_kernel(chips, place_ref, sent_ref, kept_ref, got_ref, *outs):
    messages = outs[: chips - 1]
    near_ref, next_ref, sums_ref = outs[chips - 1 :]
    rows = kept_ref.shape[1]
    core = place_of(place_ref, chips)[1]
    sums = sent_ref[chips * rows :, :] + got_ref[chips * rows :, :]
    for m in range(1, chips):
        messages[m - 1][:rows, :] = kept_ref[m] + got_ref[m * rows : (m + 1) * rows, :]
        messages[m - 1][rows:, :] = sums
    spare = got_ref[:rows, :]
    near_ref[...] = kept_ref[0] + jnp.where(core == 1, spare, 0.0)
    next_ref[...] = kept_ref[chips] + jnp.where(core == 0, spare, 0.0)
    sums_ref[...] = sums


def plane_kernel(chips, place_ref, near_ref, next_ref, sums_ref, last_ref, *refs):
    got = refs[: chips - 1]
    next_out, last_out, near_out, sums_out = refs[chips - 1 :]
    rows = near_ref.shape[0]
    chip = place_of(place_ref, chips)[0]
    near, ahead, sums = near_ref[...], next_ref[...], sums_ref[...]
    for m in range(1, chips):
        block = got[m - 1][:rows, :]
        same = (chip ^ m) < chip
        near = near + jnp.where(same, block, 0.0)
        ahead = ahead + jnp.where(same, 0.0, block)
        sums = sums + got[m - 1][rows:, :]
    near_out[...] = near
    sums_out[...] = sums
    next_out[:rows, :] = ahead
    last_out[:rows, :] = last_ref[...]
    for message in (next_out, last_out):
        message[rows:, :] = sums


def final_kernel(right_ref, near_ref, sums_ref, last_ref, *refs):
    solution_ref, residual_ref = refs[-2:]
    rows = near_ref.shape[0]
    image = near_ref[...] + last_ref[:rows, :]
    sums = sums_ref[...] + last_ref[rows:, :]
    for more in refs[:-2]:
        sums = sums + more[...]
    step_len = sums[0:1, :] / sums[1:2, :]
    right = right_ref[...]
    solution_ref[...] = step_len * right
    residual_ref[...] = right - step_len * image


def call(kernel, smem, operands, outs, scratch=(), cost=None):
    vmem = pl.BlockSpec(memory_space=pltpu.VMEM)
    return pl.pallas_call(
        kernel,
        in_specs=[pl.BlockSpec(memory_space=pltpu.SMEM)] * len(smem) + [vmem] * len(operands),
        out_specs=[vmem] * len(outs),
        out_shape=[jax.ShapeDtypeStruct(shape, kind) for shape, kind in outs],
        scratch_shapes=list(scratch),
        cost_estimate=cost,
        compiler_params=pltpu.CompilerParams(vmem_limit_bytes=VMEM_BYTES),
    )(*smem, *operands)


def per_device(right_side, kernel_tiles, route_pairs):
    count = lax.axis_size("blk")
    window = max(8, min(16, count // 8))
    planes, chips = count // window, window // 2
    rows, cols = right_side.shape
    slots = kernel_tiles.shape[1]
    cover_len = window + planes - 1
    place = lax.axis_index("blk").astype(jnp.int32)
    chip, core = place % window // 2, place % 2
    where = place[None]
    single, half = jnp.float32, jnp.bfloat16

    own, straight, turned = call(
        prepare_kernel,
        (),
        (right_side, kernel_tiles[0]),
        [((rows, cols), single), ((slots, 2 * rows, cols), half), ((slots, 2 * cols, rows), half)],
    )
    far = {k: shifted(right_side, -k * window) for k in (planes - 1, *range(1, planes - 1))}
    own, far[planes - 1], far[1] = lax.optimization_barrier((own, far[planes - 1], far[1]))
    middle = range(2, planes - 1)
    (middle_parts,) = call(
        split_blocks_kernel, (), [far[k] for k in middle], [((len(middle), rows, 2 * cols), half)], cost=BESIDE
    )
    even = [chip_partner(jnp.where((chip ^ m) < chip, own, far[1]), m) for m in range(1, chips)]
    sent = jnp.stack([jnp.where(core == 0, far[1], own)] + even)
    sent, middle_parts = lax.optimization_barrier((sent, middle_parts))
    odd = core_partner(sent)

    block, marked, extra = ((rows, cols), single), ((rows + EXTRA, cols), single), ((EXTRA, cols), single)
    sent, kept, *far_out = call(
        functools.partial(product_kernel, planes, chips),
        (route_pairs.T, where),
        (own, *[far[k] for k in range(1, planes)], *even, odd, middle_parts, straight, turned),
        [((chips * rows + EXTRA, cols), single), ((chips + 1, rows, cols), single)] + [block] * (planes - 2),
        (
            pltpu.VMEM((cover_len, rows, cols), single),
            pltpu.VMEM((cover_len, rows, 2 * cols), half),
            pltpu.VMEM((cover_len, rows, cols), single),
        ),
    )
    got = core_partner(sent)
    *messages, near, ahead, sums = call(
        functools.partial(pair_kernel, chips), (where,), (sent, kept, got), [marked] * (chips - 1) + [block, block, extra]
    )
    middle_got = [shifted(far_out[k - 2], k * window) for k in middle]
    got = [chip_partner(value, m) for m, value in enumerate(messages, 1)]
    ahead, last, near, sums = call(
        functools.partial(plane_kernel, chips),
        (where,),
        (near, ahead, sums, far_out[-1], *got),
        [marked, marked, block, extra],
    )
    got = shifted(ahead, window)
    more = [shifted(sums, k * window) for k in middle]
    last = shifted(last, (planes - 1) * window)
    (middle_sum,) = call(add_kernel, (), middle_got, [block], cost=BESIDE)
    near, sums = call(near_kernel, (), (near, middle_sum, sums, got), [block, extra], cost=BESIDE)
    return call(final_kernel, (), (own, near, sums, last, *more), [block, block])


def solution(mesh):
    def run(*args):
        return tuple(per_device(*args))

    return jax.shard_map(
        run,
        mesh=mesh,
        in_specs=(P("blk", None), P("blk", None, None, None), P()),
        out_specs=(P("blk", None), P("blk", None)),
        check_vma=False,
    )
```

```python
import functools

import jax
import jax.numpy as jnp
from jax import lax
from jax.experimental import pallas as pl
from jax.experimental.pallas import tpu as pltpu
from jax.sharding import PartitionSpec as P

EXTRA = 8
VMEM_BYTES = 48 * 1024 * 1024
BESIDE = pl.CostEstimate(flops=10**10, bytes_accessed=0, transcendentals=0)


def shifted(value, steps):
    count = lax.axis_size("blk")
    pairs = [(source, (source + steps) % count) for source in range(count)]
    return lax.ppermute(value, "blk", pairs)


def chip_partner(value, mask):
    count = lax.axis_size("blk")
    return lax.ppermute(value, "blk", [(source, source ^ (2 * mask)) for source in range(count)])


def core_partner(value):
    count = lax.axis_size("blk")
    return lax.ppermute(value, "blk", [(source, source ^ 1) for source in range(count)])


def split_two(values):
    high = values.astype(jnp.bfloat16)
    low = (values - high.astype(jnp.float32)).astype(jnp.bfloat16)
    return high, low


def place_of(place_ref, chips):
    place = place_ref[0]
    return (place // 2) & (chips - 1), place & 1


def prepare_kernel(own_ref, tiles_ref, own_out, straight_ref, turned_ref):
    own_out[...] = own_ref[...]
    slots, rows, cols = tiles_ref.shape

    def visit(t):
        tile = tiles_ref[t]
        straight_ref[t, :rows, :], straight_ref[t, rows:, :] = split_two(tile)
        turned_ref[t, :cols, :], turned_ref[t, cols:, :] = split_two(tile.T)

    if slots <= 32:
        for t in range(slots):
            visit(t)
    else:
        lax.fori_loop(0, slots, lambda t, c: (visit(t), c)[1], 0)


def split_blocks_kernel(*refs):
    out_ref = refs[-1]
    cols = out_ref.shape[2] // 2
    for i, block in enumerate(refs[:-1]):
        out_ref[i, :, :cols], out_ref[i, :, cols:] = split_two(block[...])


def add_kernel(*refs):
    total = refs[0][...]
    for block in refs[1:-1]:
        total = total + block[...]
    refs[-1][...] = total


def near_kernel(near_ref, sums_ref, next_ref, near_out, sums_out):
    rows = near_ref.shape[0]
    near_out[...] = near_ref[...] + next_ref[:rows, :]
    sums_out[...] = sums_ref[...] + next_ref[rows:, :]


def steps_ahead(chip, mask, chips):
    return ((chip ^ mask) - chip) & (chips - 1)


def product_kernel(planes, chips, pairs_ref, place_ref, own_ref, *refs):
    window = 2 * chips
    far = refs[: planes - 1]
    even = refs[planes - 1 : planes + chips - 2]
    odd_ref, middle_ref, straight_ref, turned_ref, message_ref, kept_ref = refs[planes + chips - 2 : planes + chips + 4]
    far_out = refs[planes + chips + 4 : -3]
    whole, parts, total = refs[-3:]
    rows, cols = own_ref.shape
    chip, core = place_of(place_ref, chips)
    spare = jnp.where(core == 0, 1, window - 1)

    def put(place, values):
        whole[place] = values
        high, low = split_two(values)
        parts[place, :, :cols] = high
        parts[place, :, cols:] = low

    put(0, own_ref[...])
    for k in (1, planes - 1):
        put(window - 1 + k, far[k - 1][...])
    for k in range(2, planes - 1):
        whole[window - 1 + k] = far[k - 1][...]
        parts[window - 1 + k] = middle_ref[k - 2]
    for m in range(1, chips):
        ahead = 2 * steps_ahead(chip, m, chips)
        put(ahead, even[m - 1][...])
        put(ahead + 1 - 2 * core, odd_ref[m])
    put(spare, odd_ref[0])

    total[...] = jnp.zeros_like(total)
    slots = straight_ref.shape[0]

    def product(split_ref, t, place):
        high = jnp.dot(split_ref[t, :rows], parts[place], preferred_element_type=jnp.float32)
        low = jnp.dot(split_ref[t, rows:], parts[place, :, :cols], preferred_element_type=jnp.float32)
        return high[:, :cols] + (high[:, cols:] + low)

    def visit(t, mirrored):
        row_place, col_place = pairs_ref[0, t], pairs_ref[1, t]
        total[row_place] += product(straight_ref, t, col_place)
        if mirrored:
            total[col_place] += product(turned_ref, t, row_place)

    visit(0, False)
    if slots <= 32:
        for t in range(1, slots - 1):
            visit(t, True)
    else:
        lax.fori_loop(1, slots - 1, lambda t, c: (visit(t, True), c)[1], 0)
    visit(slots - 1, False)

    dots = jnp.zeros((1, cols), jnp.float32)
    for place in range(whole.shape[0]):
        dots = dots + jnp.sum(whole[place] * total[place], axis=0, keepdims=True)
    own = own_ref[...]
    norm = jnp.sum(own * own, axis=0, keepdims=True)
    sums = jnp.concatenate([norm, dots, jnp.zeros((EXTRA - 2, cols), jnp.float32)], axis=0)
    message_ref[:rows, :] = total[spare]
    kept_ref[0] = total[0]
    for m in range(1, chips):
        ahead = 2 * steps_ahead(chip, m, chips)
        message_ref[m * rows : (m + 1) * rows, :] = total[ahead + 1 - 2 * core]
        kept_ref[m] = total[ahead]
    message_ref[chips * rows :, :] = sums
    kept_ref[chips] = total[window]
    for k in range(2, planes):
        far_out[k - 2][...] = total[window - 1 + k]


def pair_kernel(chips, place_ref, sent_ref, kept_ref, got_ref, *outs):
    messages = outs[: chips - 1]
    near_ref, next_ref, sums_ref = outs[chips - 1 :]
    rows = kept_ref.shape[1]
    core = place_of(place_ref, chips)[1]
    sums = sent_ref[chips * rows :, :] + got_ref[chips * rows :, :]
    for m in range(1, chips):
        messages[m - 1][:rows, :] = kept_ref[m] + got_ref[m * rows : (m + 1) * rows, :]
        messages[m - 1][rows:, :] = sums
    spare = got_ref[:rows, :]
    near_ref[...] = kept_ref[0] + jnp.where(core == 1, spare, 0.0)
    next_ref[...] = kept_ref[chips] + jnp.where(core == 0, spare, 0.0)
    sums_ref[...] = sums


def plane_kernel(chips, place_ref, near_ref, next_ref, sums_ref, last_ref, *refs):
    got = refs[: chips - 1]
    next_out, last_out, near_out, sums_out = refs[chips - 1 :]
    rows = near_ref.shape[0]
    chip = place_of(place_ref, chips)[0]
    near, ahead, sums = near_ref[...], next_ref[...], sums_ref[...]
    for m in range(1, chips):
        block = got[m - 1][:rows, :]
        same = (chip ^ m) < chip
        near = near + jnp.where(same, block, 0.0)
        ahead = ahead + jnp.where(same, 0.0, block)
        sums = sums + got[m - 1][rows:, :]
    near_out[...] = near
    sums_out[...] = sums
    next_out[:rows, :] = ahead
    last_out[:rows, :] = last_ref[...]
    for message in (next_out, last_out):
        message[rows:, :] = sums


def final_kernel(right_ref, near_ref, middle_ref, sums_ref, last_ref, *refs):
    solution_ref, residual_ref = refs[-2:]
    rows = near_ref.shape[0]
    image = near_ref[...] + middle_ref[...] + last_ref[:rows, :]
    sums = sums_ref[...] + last_ref[rows:, :]
    for more in refs[:-2]:
        sums = sums + more[...]
    step_len = sums[0:1, :] / sums[1:2, :]
    right = right_ref[...]
    solution_ref[...] = step_len * right
    residual_ref[...] = right - step_len * image


def call(kernel, smem, operands, outs, scratch=(), cost=None):
    vmem = pl.BlockSpec(memory_space=pltpu.VMEM)
    return pl.pallas_call(
        kernel,
        in_specs=[pl.BlockSpec(memory_space=pltpu.SMEM)] * len(smem) + [vmem] * len(operands),
        out_specs=[vmem] * len(outs),
        out_shape=[jax.ShapeDtypeStruct(shape, kind) for shape, kind in outs],
        scratch_shapes=list(scratch),
        cost_estimate=cost,
        compiler_params=pltpu.CompilerParams(vmem_limit_bytes=VMEM_BYTES),
    )(*smem, *operands)


def per_device(right_side, kernel_tiles, route_pairs):
    count = lax.axis_size("blk")
    window = max(8, min(16, count // 8))
    planes, chips = count // window, window // 2
    rows, cols = right_side.shape
    slots = kernel_tiles.shape[1]
    cover_len = window + planes - 1
    place = lax.axis_index("blk").astype(jnp.int32)
    chip, core = place % window // 2, place % 2
    where = place[None]
    single, half = jnp.float32, jnp.bfloat16

    own, straight, turned = call(
        prepare_kernel,
        (),
        (right_side, kernel_tiles[0]),
        [((rows, cols), single), ((slots, 2 * rows, cols), half), ((slots, 2 * cols, rows), half)],
    )
    far = {k: shifted(right_side, -k * window) for k in (planes - 1, *range(1, planes - 1))}
    own, far[planes - 1], far[1] = lax.optimization_barrier((own, far[planes - 1], far[1]))
    middle = range(2, planes - 1)
    (middle_parts,) = call(
        split_blocks_kernel, (), [far[k] for k in middle], [((len(middle), rows, 2 * cols), half)], cost=BESIDE
    )
    even = [chip_partner(jnp.where((chip ^ m) < chip, own, far[1]), m) for m in range(1, chips)]
    sent = jnp.stack([jnp.where(core == 0, far[1], own)] + even)
    sent, middle_parts = lax.optimization_barrier((sent, middle_parts))
    odd = core_partner(sent)

    block, marked, extra = ((rows, cols), single), ((rows + EXTRA, cols), single), ((EXTRA, cols), single)
    sent, kept, *far_out = call(
        functools.partial(product_kernel, planes, chips),
        (route_pairs.T, where),
        (own, *[far[k] for k in range(1, planes)], *even, odd, middle_parts, straight, turned),
        [((chips * rows + EXTRA, cols), single), ((chips + 1, rows, cols), single)] + [block] * (planes - 2),
        (
            pltpu.VMEM((cover_len, rows, cols), single),
            pltpu.VMEM((cover_len, rows, 2 * cols), half),
            pltpu.VMEM((cover_len, rows, cols), single),
        ),
    )
    got = core_partner(sent)
    *messages, near, ahead, sums = call(
        functools.partial(pair_kernel, chips), (where,), (sent, kept, got), [marked] * (chips - 1) + [block, block, extra]
    )
    middle_got = [shifted(far_out[k - 2], k * window) for k in middle]
    got = [chip_partner(value, m) for m, value in enumerate(messages, 1)]
    ahead, last, near, sums = call(
        functools.partial(plane_kernel, chips),
        (where,),
        (near, ahead, sums, far_out[-1], *got),
        [marked, marked, block, extra],
    )
    got = shifted(ahead, window)
    more = [shifted(sums, k * window) for k in middle]
    last = shifted(last, (planes - 1) * window)
    (middle_sum,) = call(add_kernel, (), middle_got, [block], cost=BESIDE)
    near, sums = call(near_kernel, (), (near, sums, got), [block, extra])
    return call(final_kernel, (), (own, near, middle_sum, sums, last, *more), [block, block])


def solution(mesh):
    def run(*args):
        return tuple(per_device(*args))

    return jax.shard_map(
        run,
        mesh=mesh,
        in_specs=(P("blk", None), P("blk", None, None, None), P()),
        out_specs=(P("blk", None), P("blk", None)),
        check_vma=False,
    )
```

```python
import functools

import jax
import jax.numpy as jnp
from jax import lax
from jax.experimental import pallas as pl
from jax.experimental.pallas import tpu as pltpu
from jax.sharding import PartitionSpec as P

EXTRA = 8
VMEM_BYTES = 48 * 1024 * 1024
BESIDE = pl.CostEstimate(flops=10**10, bytes_accessed=0, transcendentals=0)


def shifted(value, steps):
    count = lax.axis_size("blk")
    pairs = [(source, (source + steps) % count) for source in range(count)]
    return lax.ppermute(value, "blk", pairs)


def chip_partner(value, mask):
    count = lax.axis_size("blk")
    return lax.ppermute(value, "blk", [(source, source ^ (2 * mask)) for source in range(count)])


def core_partner(value):
    count = lax.axis_size("blk")
    return lax.ppermute(value, "blk", [(source, source ^ 1) for source in range(count)])


def split_two(values):
    high = values.astype(jnp.bfloat16)
    low = (values - high.astype(jnp.float32)).astype(jnp.bfloat16)
    return high, low


def place_of(place_ref, chips):
    place = place_ref[0]
    return (place // 2) & (chips - 1), place & 1


def prepare_kernel(own_ref, tiles_ref, own_out, straight_ref, turned_ref):
    own_out[...] = own_ref[...]
    slots, rows, cols = tiles_ref.shape

    def visit(t):
        tile = tiles_ref[t]
        straight_ref[t, :rows, :], straight_ref[t, rows:, :] = split_two(tile)
        turned_ref[t, :cols, :], turned_ref[t, cols:, :] = split_two(tile.T)

    if slots <= 32:
        for t in range(slots):
            visit(t)
    else:
        lax.fori_loop(0, slots, lambda t, c: (visit(t), c)[1], 0)


def split_blocks_kernel(*refs):
    out_ref = refs[-1]
    cols = out_ref.shape[2] // 2
    for i, block in enumerate(refs[:-1]):
        out_ref[i, :, :cols], out_ref[i, :, cols:] = split_two(block[...])


def add_kernel(*refs):
    total = refs[0][...]
    for block in refs[1:-1]:
        total = total + block[...]
    refs[-1][...] = total


def near_kernel(near_ref, sums_ref, next_ref, near_out, sums_out):
    rows = near_ref.shape[0]
    near_out[...] = near_ref[...] + next_ref[:rows, :]
    sums_out[...] = sums_ref[...] + next_ref[rows:, :]


def steps_ahead(chip, mask, chips):
    return ((chip ^ mask) - chip) & (chips - 1)


def product_kernel(planes, chips, pairs_ref, place_ref, own_ref, *refs):
    window = 2 * chips
    far = refs[: planes - 1]
    even = refs[planes - 1 : planes + chips - 2]
    odd_ref, middle_ref, straight_ref, turned_ref, message_ref, kept_ref = refs[planes + chips - 2 : planes + chips + 4]
    far_out = refs[planes + chips + 4 : -3]
    whole, parts, total = refs[-3:]
    rows, cols = own_ref.shape
    chip, core = place_of(place_ref, chips)
    spare = jnp.where(core == 0, 1, window - 1)

    def put(place, values):
        whole[place] = values
        high, low = split_two(values)
        parts[place, :, :cols] = high
        parts[place, :, cols:] = low

    put(0, own_ref[...])
    for k in (1, planes - 1):
        put(window - 1 + k, far[k - 1][...])
    for k in range(2, planes - 1):
        whole[window - 1 + k] = far[k - 1][...]
        parts[window - 1 + k] = middle_ref[k - 2]
    for m in range(1, chips):
        ahead = 2 * steps_ahead(chip, m, chips)
        put(ahead, even[m - 1][...])
        put(ahead + 1 - 2 * core, odd_ref[m])
    put(spare, odd_ref[0])

    total[...] = jnp.zeros_like(total)
    slots = straight_ref.shape[0]

    def product(split_ref, t, place):
        high = jnp.dot(split_ref[t, :rows], parts[place], preferred_element_type=jnp.float32)
        low = jnp.dot(split_ref[t, rows:], parts[place, :, :cols], preferred_element_type=jnp.float32)
        return high[:, :cols] + (high[:, cols:] + low)

    def visit(t, mirrored):
        row_place, col_place = pairs_ref[0, t], pairs_ref[1, t]
        total[row_place] += product(straight_ref, t, col_place)
        if mirrored:
            total[col_place] += product(turned_ref, t, row_place)

    visit(0, False)
    if slots <= 32:
        for t in range(1, slots - 1):
            visit(t, True)
    else:
        lax.fori_loop(1, slots - 1, lambda t, c: (visit(t, True), c)[1], 0)
    visit(slots - 1, False)

    dots = jnp.zeros((1, cols), jnp.float32)
    for place in range(whole.shape[0]):
        dots = dots + jnp.sum(whole[place] * total[place], axis=0, keepdims=True)
    own = own_ref[...]
    norm = jnp.sum(own * own, axis=0, keepdims=True)
    sums = jnp.concatenate([norm, dots, jnp.zeros((EXTRA - 2, cols), jnp.float32)], axis=0)
    message_ref[:rows, :] = total[spare]
    kept_ref[0] = total[0]
    for m in range(1, chips):
        ahead = 2 * steps_ahead(chip, m, chips)
        message_ref[m * rows : (m + 1) * rows, :] = total[ahead + 1 - 2 * core]
        kept_ref[m] = total[ahead]
    message_ref[chips * rows :, :] = sums
    kept_ref[chips] = total[window]
    for k in range(2, planes):
        far_out[k - 2][...] = total[window - 1 + k]


def pair_kernel(chips, place_ref, sent_ref, kept_ref, got_ref, *outs):
    messages = outs[: chips - 1]
    near_ref, next_ref, sums_ref = outs[chips - 1 :]
    rows = kept_ref.shape[1]
    core = place_of(place_ref, chips)[1]
    sums = sent_ref[chips * rows :, :] + got_ref[chips * rows :, :]
    for m in range(1, chips):
        messages[m - 1][:rows, :] = kept_ref[m] + got_ref[m * rows : (m + 1) * rows, :]
        messages[m - 1][rows:, :] = sums
    spare = got_ref[:rows, :]
    near_ref[...] = kept_ref[0] + jnp.where(core == 1, spare, 0.0)
    next_ref[...] = kept_ref[chips] + jnp.where(core == 0, spare, 0.0)
    sums_ref[...] = sums


def plane_kernel(chips, place_ref, near_ref, middle_ref, next_ref, sums_ref, last_ref, *refs):
    got = refs[: chips - 1]
    next_out, last_out, near_out, sums_out = refs[chips - 1 :]
    rows = near_ref.shape[0]
    chip = place_of(place_ref, chips)[0]
    near, ahead, sums = near_ref[...] + middle_ref[...], next_ref[...], sums_ref[...]
    for m in range(1, chips):
        block = got[m - 1][:rows, :]
        same = (chip ^ m) < chip
        near = near + jnp.where(same, block, 0.0)
        ahead = ahead + jnp.where(same, 0.0, block)
        sums = sums + got[m - 1][rows:, :]
    near_out[...] = near
    sums_out[...] = sums
    next_out[:rows, :] = ahead
    last_out[:rows, :] = last_ref[...]
    for message in (next_out, last_out):
        message[rows:, :] = sums


def final_kernel(right_ref, near_ref, sums_ref, last_ref, *refs):
    solution_ref, residual_ref = refs[-2:]
    rows = near_ref.shape[0]
    image = near_ref[...] + last_ref[:rows, :]
    sums = sums_ref[...] + last_ref[rows:, :]
    for more in refs[:-2]:
        sums = sums + more[...]
    step_len = sums[0:1, :] / sums[1:2, :]
    right = right_ref[...]
    solution_ref[...] = step_len * right
    residual_ref[...] = right - step_len * image


def call(kernel, smem, operands, outs, scratch=(), cost=None):
    vmem = pl.BlockSpec(memory_space=pltpu.VMEM)
    return pl.pallas_call(
        kernel,
        in_specs=[pl.BlockSpec(memory_space=pltpu.SMEM)] * len(smem) + [vmem] * len(operands),
        out_specs=[vmem] * len(outs),
        out_shape=[jax.ShapeDtypeStruct(shape, kind) for shape, kind in outs],
        scratch_shapes=list(scratch),
        cost_estimate=cost,
        compiler_params=pltpu.CompilerParams(vmem_limit_bytes=VMEM_BYTES),
    )(*smem, *operands)


def per_device(right_side, kernel_tiles, route_pairs):
    count = lax.axis_size("blk")
    window = max(8, min(16, count // 8))
    planes, chips = count // window, window // 2
    rows, cols = right_side.shape
    slots = kernel_tiles.shape[1]
    cover_len = window + planes - 1
    place = lax.axis_index("blk").astype(jnp.int32)
    chip, core = place % window // 2, place % 2
    where = place[None]
    single, half = jnp.float32, jnp.bfloat16

    own, straight, turned = call(
        prepare_kernel,
        (),
        (right_side, kernel_tiles[0]),
        [((rows, cols), single), ((slots, 2 * rows, cols), half), ((slots, 2 * cols, rows), half)],
    )
    far = {k: shifted(right_side, -k * window) for k in (planes - 1, *range(1, planes - 1))}
    own, far[planes - 1], far[1] = lax.optimization_barrier((own, far[planes - 1], far[1]))
    middle = range(2, planes - 1)
    (middle_parts,) = call(
        split_blocks_kernel, (), [far[k] for k in middle], [((len(middle), rows, 2 * cols), half)], cost=BESIDE
    )
    even = [chip_partner(jnp.where((chip ^ m) < chip, own, far[1]), m) for m in range(1, chips)]
    sent = jnp.stack([jnp.where(core == 0, far[1], own)] + even)
    sent, middle_parts = lax.optimization_barrier((sent, middle_parts))
    odd = core_partner(sent)

    block, marked, extra = ((rows, cols), single), ((rows + EXTRA, cols), single), ((EXTRA, cols), single)
    sent, kept, *far_out = call(
        functools.partial(product_kernel, planes, chips),
        (route_pairs.T, where),
        (own, *[far[k] for k in range(1, planes)], *even, odd, middle_parts, straight, turned),
        [((chips * rows + EXTRA, cols), single), ((chips + 1, rows, cols), single)] + [block] * (planes - 2),
        (
            pltpu.VMEM((cover_len, rows, cols), single),
            pltpu.VMEM((cover_len, rows, 2 * cols), half),
            pltpu.VMEM((cover_len, rows, cols), single),
        ),
    )
    got = core_partner(sent)
    *messages, near, ahead, sums = call(
        functools.partial(pair_kernel, chips), (where,), (sent, kept, got), [marked] * (chips - 1) + [block, block, extra]
    )
    middle_got = [shifted(far_out[k - 2], k * window) for k in middle]
    got = [chip_partner(value, m) for m, value in enumerate(messages, 1)]
    (middle_sum,) = call(add_kernel, (), middle_got, [block], cost=BESIDE)
    ahead, last, near, sums = call(
        functools.partial(plane_kernel, chips),
        (where,),
        (near, middle_sum, ahead, sums, far_out[-1], *got),
        [marked, marked, block, extra],
    )
    got = shifted(ahead, window)
    more = [shifted(sums, k * window) for k in middle]
    last = shifted(last, (planes - 1) * window)
    near, sums = call(near_kernel, (), (near, sums, got), [block, extra], cost=BESIDE)
    return call(final_kernel, (), (own, near, sums, last, *more), [block, block])


def solution(mesh):
    def run(*args):
        return tuple(per_device(*args))

    return jax.shard_map(
        run,
        mesh=mesh,
        in_specs=(P("blk", None), P("blk", None, None, None), P()),
        out_specs=(P("blk", None), P("blk", None)),
        check_vma=False,
    )
```

```python
import functools

import jax
import jax.numpy as jnp
from jax import lax
from jax.experimental import pallas as pl
from jax.experimental.pallas import tpu as pltpu
from jax.sharding import PartitionSpec as P

EXTRA = 8
VMEM_BYTES = 48 * 1024 * 1024
BESIDE = pl.CostEstimate(flops=10**10, bytes_accessed=0, transcendentals=0)


def shifted(value, steps):
    count = lax.axis_size("blk")
    pairs = [(source, (source + steps) % count) for source in range(count)]
    return lax.ppermute(value, "blk", pairs)


def chip_partner(value, mask):
    count = lax.axis_size("blk")
    return lax.ppermute(value, "blk", [(source, source ^ (2 * mask)) for source in range(count)])


def core_partner(value):
    count = lax.axis_size("blk")
    return lax.ppermute(value, "blk", [(source, source ^ 1) for source in range(count)])


def split_two(values):
    high = values.astype(jnp.bfloat16)
    low = (values - high.astype(jnp.float32)).astype(jnp.bfloat16)
    return high, low


def place_of(place_ref, chips):
    place = place_ref[0]
    return (place // 2) & (chips - 1), place & 1


def keep_kernel(block_ref, out_ref):
    out_ref[...] = block_ref[...]


def split_kernel(tiles_ref, straight_ref, turned_ref):
    slots, rows, cols = tiles_ref.shape

    def visit(t):
        tile = tiles_ref[t]
        straight_ref[t, :, :cols], straight_ref[t, :, cols:] = split_two(tile)
        turned_ref[t, :, :rows], turned_ref[t, :, rows:] = split_two(tile.T)

    if slots <= 32:
        for t in range(slots):
            visit(t)
    else:
        lax.fori_loop(0, slots, lambda t, c: (visit(t), c)[1], 0)


def split_blocks_kernel(*refs):
    out_ref = refs[-1]
    cols = out_ref.shape[2] // 2
    for i, block in enumerate(refs[:-1]):
        out_ref[i, :, :cols], out_ref[i, :, cols:] = split_two(block[...])


def add_kernel(*refs):
    total = refs[0][...]
    for block in refs[1:-1]:
        total = total + block[...]
    refs[-1][...] = total


def near_kernel(near_ref, sums_ref, next_ref, near_out, sums_out):
    rows = near_ref.shape[0]
    near_out[...] = near_ref[...] + next_ref[:rows, :]
    sums_out[...] = sums_ref[...] + next_ref[rows:, :]


def steps_ahead(chip, mask, chips):
    return ((chip ^ mask) - chip) & (chips - 1)


def product_kernel(planes, chips, pairs_ref, place_ref, own_ref, *refs):
    window = 2 * chips
    far = refs[: planes - 1]
    even = refs[planes - 1 : planes + chips - 2]
    odd_ref, middle_ref, straight_ref, turned_ref, message_ref, kept_ref = refs[planes + chips - 2 : planes + chips + 4]
    far_out = refs[planes + chips + 4 : -3]
    whole, parts, total = refs[-3:]
    rows, cols = own_ref.shape
    chip, core = place_of(place_ref, chips)
    spare = jnp.where(core == 0, 1, window - 1)

    def put_parts(place, high, low):
        parts[place, :rows, :cols] = high
        parts[place, :rows, cols:] = low
        parts[place, rows:, :cols] = high
        parts[place, rows:, cols:] = jnp.zeros_like(low)

    def put(place, values):
        whole[place] = values
        put_parts(place, *split_two(values))

    put(0, own_ref[...])
    for k in (1, planes - 1):
        put(window - 1 + k, far[k - 1][...])
    for k in range(2, planes - 1):
        whole[window - 1 + k] = far[k - 1][...]
        put_parts(window - 1 + k, middle_ref[k - 2, :, :cols], middle_ref[k - 2, :, cols:])
    for m in range(1, chips):
        ahead = 2 * steps_ahead(chip, m, chips)
        put(ahead, even[m - 1][...])
        put(ahead + 1 - 2 * core, odd_ref[m])
    put(spare, odd_ref[0])

    total[...] = jnp.zeros_like(total)
    slots = straight_ref.shape[0]

    def product(split_ref, t, place):
        both = jnp.dot(split_ref[t], parts[place], preferred_element_type=jnp.float32)
        return both[:, :cols] + both[:, cols:]

    def visit(t, mirrored):
        row_place, col_place = pairs_ref[0, t], pairs_ref[1, t]
        total[row_place] += product(straight_ref, t, col_place)
        if mirrored:
            total[col_place] += product(turned_ref, t, row_place)

    visit(0, False)
    if slots <= 32:
        for t in range(1, slots - 1):
            visit(t, True)
    else:
        lax.fori_loop(1, slots - 1, lambda t, c: (visit(t, True), c)[1], 0)
    visit(slots - 1, False)

    dots = jnp.zeros((1, cols), jnp.float32)
    for place in range(whole.shape[0]):
        dots = dots + jnp.sum(whole[place] * total[place], axis=0, keepdims=True)
    own = own_ref[...]
    norm = jnp.sum(own * own, axis=0, keepdims=True)
    sums = jnp.concatenate([norm, dots, jnp.zeros((EXTRA - 2, cols), jnp.float32)], axis=0)
    message_ref[:rows, :] = total[spare]
    kept_ref[0] = total[0]
    for m in range(1, chips):
        ahead = 2 * steps_ahead(chip, m, chips)
        message_ref[m * rows : (m + 1) * rows, :] = total[ahead + 1 - 2 * core]
        kept_ref[m] = total[ahead]
    message_ref[chips * rows :, :] = sums
    kept_ref[chips] = total[window]
    for k in range(2, planes):
        far_out[k - 2][...] = total[window - 1 + k]


def pair_kernel(chips, place_ref, sent_ref, kept_ref, got_ref, *outs):
    messages = outs[: chips - 1]
    near_ref, next_ref, sums_ref = outs[chips - 1 :]
    rows = kept_ref.shape[1]
    core = place_of(place_ref, chips)[1]
    sums = sent_ref[chips * rows :, :] + got_ref[chips * rows :, :]
    for m in range(1, chips):
        messages[m - 1][:rows, :] = kept_ref[m] + got_ref[m * rows : (m + 1) * rows, :]
        messages[m - 1][rows:, :] = sums
    spare = got_ref[:rows, :]
    near_ref[...] = kept_ref[0] + jnp.where(core == 1, spare, 0.0)
    next_ref[...] = kept_ref[chips] + jnp.where(core == 0, spare, 0.0)
    sums_ref[...] = sums


def plane_kernel(chips, place_ref, near_ref, middle_ref, next_ref, sums_ref, last_ref, *refs):
    got = refs[: chips - 1]
    next_out, last_out, near_out, sums_out = refs[chips - 1 :]
    rows = near_ref.shape[0]
    chip = place_of(place_ref, chips)[0]
    near, ahead, sums = near_ref[...] + middle_ref[...], next_ref[...], sums_ref[...]
    for m in range(1, chips):
        block = got[m - 1][:rows, :]
        same = (chip ^ m) < chip
        near = near + jnp.where(same, block, 0.0)
        ahead = ahead + jnp.where(same, 0.0, block)
        sums = sums + got[m - 1][rows:, :]
    near_out[...] = near
    sums_out[...] = sums
    next_out[:rows, :] = ahead
    last_out[:rows, :] = last_ref[...]
    for message in (next_out, last_out):
        message[rows:, :] = sums


def final_kernel(right_ref, near_ref, sums_ref, last_ref, *refs):
    solution_ref, residual_ref = refs[-2:]
    rows = near_ref.shape[0]
    image = near_ref[...] + last_ref[:rows, :]
    sums = sums_ref[...] + last_ref[rows:, :]
    for more in refs[:-2]:
        sums = sums + more[...]
    step_len = sums[0:1, :] / sums[1:2, :]
    right = right_ref[...]
    solution_ref[...] = step_len * right
    residual_ref[...] = right - step_len * image


def call(kernel, smem, operands, outs, scratch=(), cost=None):
    vmem = pl.BlockSpec(memory_space=pltpu.VMEM)
    return pl.pallas_call(
        kernel,
        in_specs=[pl.BlockSpec(memory_space=pltpu.SMEM)] * len(smem) + [vmem] * len(operands),
        out_specs=[vmem] * len(outs),
        out_shape=[jax.ShapeDtypeStruct(shape, kind) for shape, kind in outs],
        scratch_shapes=list(scratch),
        cost_estimate=cost,
        compiler_params=pltpu.CompilerParams(vmem_limit_bytes=VMEM_BYTES),
    )(*smem, *operands)


def per_device(right_side, kernel_tiles, route_pairs):
    count = lax.axis_size("blk")
    window = max(8, min(16, count // 8))
    planes, chips = count // window, window // 2
    rows, cols = right_side.shape
    slots = kernel_tiles.shape[1]
    cover_len = window + planes - 1
    place = lax.axis_index("blk").astype(jnp.int32)
    chip, core = place % window // 2, place % 2
    where = place[None]
    single, half = jnp.float32, jnp.bfloat16

    block, marked, extra = ((rows, cols), single), ((rows + EXTRA, cols), single), ((EXTRA, cols), single)
    (own,) = call(keep_kernel, (), (right_side,), [block])
    straight, turned = call(
        split_kernel,
        (),
        (kernel_tiles[0],),
        [((slots, rows, 2 * cols), half), ((slots, cols, 2 * rows), half)],
        cost=BESIDE,
    )
    far = {k: shifted(right_side, -k * window) for k in (planes - 1, *range(1, planes - 1))}
    own, far[planes - 1], far[1] = lax.optimization_barrier((own, far[planes - 1], far[1]))
    middle = range(2, planes - 1)
    (middle_parts,) = call(
        split_blocks_kernel, (), [far[k] for k in middle], [((len(middle), rows, 2 * cols), half)], cost=BESIDE
    )
    even = [chip_partner(jnp.where((chip ^ m) < chip, own, far[1]), m) for m in range(1, chips)]
    sent = jnp.stack([jnp.where(core == 0, far[1], own)] + even)
    sent, middle_parts = lax.optimization_barrier((sent, middle_parts))
    odd = core_partner(sent)

    sent, kept, *far_out = call(
        functools.partial(product_kernel, planes, chips),
        (route_pairs.T, where),
        (own, *[far[k] for k in range(1, planes)], *even, odd, middle_parts, straight, turned),
        [((chips * rows + EXTRA, cols), single), ((chips + 1, rows, cols), single)] + [block] * (planes - 2),
        (
            pltpu.VMEM((cover_len, rows, cols), single),
            pltpu.VMEM((cover_len, 2 * rows, 2 * cols), half),
            pltpu.VMEM((cover_len, rows, cols), single),
        ),
    )
    got = core_partner(sent)
    *messages, near, ahead, sums = call(
        functools.partial(pair_kernel, chips), (where,), (sent, kept, got), [marked] * (chips - 1) + [block, block, extra]
    )
    middle_got = [shifted(far_out[k - 2], k * window) for k in middle]
    got = [chip_partner(value, m) for m, value in enumerate(messages, 1)]
    (middle_sum,) = call(add_kernel, (), middle_got, [block], cost=BESIDE)
    ahead, last, near, sums = call(
        functools.partial(plane_kernel, chips),
        (where,),
        (near, middle_sum, ahead, sums, far_out[-1], *got),
        [marked, marked, block, extra],
    )
    got = shifted(ahead, window)
    more = [shifted(sums, k * window) for k in middle]
    last = shifted(last, (planes - 1) * window)
    near, sums = call(near_kernel, (), (near, sums, got), [block, extra], cost=BESIDE)
    return call(final_kernel, (), (own, near, sums, last, *more), [block, block])


def solution(mesh):
    def run(*args):
        return tuple(per_device(*args))

    return jax.shard_map(
        run,
        mesh=mesh,
        in_specs=(P("blk", None), P("blk", None, None, None), P()),
        out_specs=(P("blk", None), P("blk", None)),
        check_vma=False,
    )
```

```python
import functools

import jax
import jax.numpy as jnp
from jax import lax
from jax.experimental import pallas as pl
from jax.experimental.pallas import tpu as pltpu
from jax.sharding import PartitionSpec as P

EXTRA = 8
VMEM_BYTES = 48 * 1024 * 1024
BESIDE = pl.CostEstimate(flops=10**10, bytes_accessed=0, transcendentals=0)


def shifted(value, steps):
    count = lax.axis_size("blk")
    pairs = [(source, (source + steps) % count) for source in range(count)]
    return lax.ppermute(value, "blk", pairs)


def chip_partner(value, mask):
    count = lax.axis_size("blk")
    return lax.ppermute(value, "blk", [(source, source ^ (2 * mask)) for source in range(count)])


def core_partner(value):
    count = lax.axis_size("blk")
    return lax.ppermute(value, "blk", [(source, source ^ 1) for source in range(count)])


def split_two(values):
    high = values.astype(jnp.bfloat16)
    low = (values - high.astype(jnp.float32)).astype(jnp.bfloat16)
    return high, low


def place_of(place_ref, chips):
    place = place_ref[0]
    return (place // 2) & (chips - 1), place & 1


def keep_kernel(block_ref, out_ref):
    out_ref[...] = block_ref[...]


def split_kernel(tiles_ref, straight_ref, turned_ref):
    slots, rows, cols = tiles_ref.shape

    def visit(t):
        tile = tiles_ref[t]
        straight_ref[t, :, :cols], straight_ref[t, :, cols:] = split_two(tile)
        turned_ref[t, :, :rows], turned_ref[t, :, rows:] = split_two(tile.T)

    if slots <= 32:
        for t in range(slots):
            visit(t)
    else:
        lax.fori_loop(0, slots, lambda t, c: (visit(t), c)[1], 0)


def split_blocks_kernel(*refs):
    out_ref = refs[-1]
    cols = out_ref.shape[2] // 2
    for i, block in enumerate(refs[:-1]):
        out_ref[i, :, :cols], out_ref[i, :, cols:] = split_two(block[...])


def add_kernel(*refs):
    total = refs[0][...]
    for block in refs[1:-1]:
        total = total + block[...]
    refs[-1][...] = total


def near_kernel(near_ref, sums_ref, next_ref, near_out, sums_out):
    rows = near_ref.shape[0]
    near_out[...] = near_ref[...] + next_ref[:rows, :]
    sums_out[...] = sums_ref[...] + next_ref[rows:, :]


def steps_ahead(chip, mask, chips):
    return ((chip ^ mask) - chip) & (chips - 1)


def product_kernel(planes, chips, place_ref, table_ref, own_ref, *refs):
    window = 2 * chips
    far = refs[: planes - 1]
    even = refs[planes - 1 : planes + chips - 2]
    odd_ref, middle_ref, straight_ref, turned_ref, message_ref, kept_ref = refs[planes + chips - 2 : planes + chips + 4]
    far_out = refs[planes + chips + 4 : -4]
    parts, total, pairs_ref, fetched = refs[-4:]
    fetch = pltpu.make_async_copy(table_ref, pairs_ref, fetched)
    fetch.start()
    rows, cols = own_ref.shape
    chip, core = place_of(place_ref, chips)
    spare = jnp.where(core == 0, 1, window - 1)

    def put_parts(place, high, low):
        parts[place, :rows, :cols] = high
        parts[place, :rows, cols:] = low
        parts[place, rows:, :cols] = high
        parts[place, rows:, cols:] = jnp.zeros_like(low)

    blocks = []

    def put(place, block_ref):
        blocks.append((place, block_ref))
        put_parts(place, *split_two(block_ref[...]))

    put(0, own_ref)
    for k in (1, planes - 1):
        put(window - 1 + k, far[k - 1])
    for k in range(2, planes - 1):
        blocks.append((window - 1 + k, far[k - 1]))
        put_parts(window - 1 + k, middle_ref[k - 2, :, :cols], middle_ref[k - 2, :, cols:])
    for m in range(1, chips):
        ahead = 2 * steps_ahead(chip, m, chips)
        put(ahead, even[m - 1])
        put(ahead + 1 - 2 * core, odd_ref.at[m])
    put(spare, odd_ref.at[0])

    total[...] = jnp.zeros_like(total)
    fetch.wait()
    slots = straight_ref.shape[0]

    def product(split_ref, t, place):
        both = jnp.dot(split_ref[t], parts[place], preferred_element_type=jnp.float32)
        return both[:, :cols] + both[:, cols:]

    def visit(t, mirrored):
        row_place, col_place = pairs_ref[0, t], pairs_ref[1, t]
        total[row_place] += product(straight_ref, t, col_place)
        if mirrored:
            total[col_place] += product(turned_ref, t, row_place)

    visit(0, False)
    if slots <= 32:
        for t in range(1, slots - 1):
            visit(t, True)
    else:
        lax.fori_loop(1, slots - 1, lambda t, c: (visit(t, True), c)[1], 0)
    visit(slots - 1, False)

    dots = jnp.zeros((1, cols), jnp.float32)
    for place, block_ref in blocks:
        dots = dots + jnp.sum(block_ref[...] * total[place], axis=0, keepdims=True)
    own = own_ref[...]
    norm = jnp.sum(own * own, axis=0, keepdims=True)
    sums = jnp.concatenate([norm, dots, jnp.zeros((EXTRA - 2, cols), jnp.float32)], axis=0)
    message_ref[:rows, :] = total[spare]
    kept_ref[0] = total[0]
    for m in range(1, chips):
        ahead = 2 * steps_ahead(chip, m, chips)
        message_ref[m * rows : (m + 1) * rows, :] = total[ahead + 1 - 2 * core]
        kept_ref[m] = total[ahead]
    message_ref[chips * rows :, :] = sums
    kept_ref[chips] = total[window]
    for k in range(2, planes):
        far_out[k - 2][...] = total[window - 1 + k]


def pair_kernel(chips, place_ref, sent_ref, kept_ref, got_ref, *outs):
    messages = outs[: chips - 1]
    near_ref, next_ref, sums_ref = outs[chips - 1 :]
    rows = kept_ref.shape[1]
    core = place_of(place_ref, chips)[1]
    sums = sent_ref[chips * rows :, :] + got_ref[chips * rows :, :]
    for m in range(1, chips):
        messages[m - 1][:rows, :] = kept_ref[m] + got_ref[m * rows : (m + 1) * rows, :]
        messages[m - 1][rows:, :] = sums
    spare = got_ref[:rows, :]
    near_ref[...] = kept_ref[0] + jnp.where(core == 1, spare, 0.0)
    next_ref[...] = kept_ref[chips] + jnp.where(core == 0, spare, 0.0)
    sums_ref[...] = sums


def plane_kernel(chips, place_ref, near_ref, middle_ref, next_ref, sums_ref, last_ref, *refs):
    got = refs[: chips - 1]
    next_out, last_out, near_out, sums_out = refs[chips - 1 :]
    rows = near_ref.shape[0]
    chip = place_of(place_ref, chips)[0]
    near, ahead, sums = near_ref[...] + middle_ref[...], next_ref[...], sums_ref[...]
    for m in range(1, chips):
        block = got[m - 1][:rows, :]
        same = (chip ^ m) < chip
        near = near + jnp.where(same, block, 0.0)
        ahead = ahead + jnp.where(same, 0.0, block)
        sums = sums + got[m - 1][rows:, :]
    near_out[...] = near
    sums_out[...] = sums
    next_out[:rows, :] = ahead
    last_out[:rows, :] = last_ref[...]
    for message in (next_out, last_out):
        message[rows:, :] = sums


def final_kernel(right_ref, near_ref, sums_ref, last_ref, *refs):
    solution_ref, residual_ref = refs[-2:]
    rows = near_ref.shape[0]
    image = near_ref[...] + last_ref[:rows, :]
    sums = sums_ref[...] + last_ref[rows:, :]
    for more in refs[:-2]:
        sums = sums + more[...]
    step_len = sums[0:1, :] / sums[1:2, :]
    right = right_ref[...]
    solution_ref[...] = step_len * right
    residual_ref[...] = right - step_len * image


def call(kernel, smem, operands, outs, scratch=(), cost=None):
    vmem = pl.BlockSpec(memory_space=pltpu.VMEM)
    return pl.pallas_call(
        kernel,
        in_specs=[pl.BlockSpec(memory_space=pltpu.SMEM)] * len(smem) + [vmem] * len(operands),
        out_specs=[vmem] * len(outs),
        out_shape=[jax.ShapeDtypeStruct(shape, kind) for shape, kind in outs],
        scratch_shapes=list(scratch),
        cost_estimate=cost,
        compiler_params=pltpu.CompilerParams(vmem_limit_bytes=VMEM_BYTES),
    )(*smem, *operands)


def per_device(right_side, kernel_tiles, route_pairs):
    count = lax.axis_size("blk")
    window = max(8, min(16, count // 8))
    planes, chips = count // window, window // 2
    rows, cols = right_side.shape
    slots = kernel_tiles.shape[1]
    cover_len = window + planes - 1
    place = lax.axis_index("blk").astype(jnp.int32)
    chip, core = place % window // 2, place % 2
    where = place[None]
    single, half = jnp.float32, jnp.bfloat16

    block, marked, extra = ((rows, cols), single), ((rows + EXTRA, cols), single), ((EXTRA, cols), single)
    (own,) = call(keep_kernel, (), (right_side,), [block])
    straight, turned = call(
        split_kernel,
        (),
        (kernel_tiles[0],),
        [((slots, rows, 2 * cols), half), ((slots, cols, 2 * rows), half)],
        cost=BESIDE,
    )
    far = {k: shifted(right_side, -k * window) for k in (planes - 1, *range(1, planes - 1))}
    own, far[planes - 1], far[1] = lax.optimization_barrier((own, far[planes - 1], far[1]))
    middle = range(2, planes - 1)
    (middle_parts,) = call(
        split_blocks_kernel, (), [far[k] for k in middle], [((len(middle), rows, 2 * cols), half)], cost=BESIDE
    )
    even = [chip_partner(jnp.where((chip ^ m) < chip, own, far[1]), m) for m in range(1, chips)]
    sent = jnp.stack([jnp.where(core == 0, far[1], own)] + even)
    sent, middle_parts = lax.optimization_barrier((sent, middle_parts))
    odd = core_partner(sent)

    sent, kept, *far_out = call(
        functools.partial(product_kernel, planes, chips),
        (where,),
        (route_pairs.T, own, *[far[k] for k in range(1, planes)], *even, odd, middle_parts, straight, turned),
        [((chips * rows + EXTRA, cols), single), ((chips + 1, rows, cols), single)] + [block] * (planes - 2),
        (
            pltpu.VMEM((cover_len, 2 * rows, 2 * cols), half),
            pltpu.VMEM((cover_len, rows, cols), single),
            pltpu.SMEM((2, slots), jnp.int32),
            pltpu.SemaphoreType.DMA,
        ),
    )
    got = core_partner(sent)
    *messages, near, ahead, sums = call(
        functools.partial(pair_kernel, chips), (where,), (sent, kept, got), [marked] * (chips - 1) + [block, block, extra]
    )
    middle_got = [shifted(far_out[k - 2], k * window) for k in middle]
    got = [chip_partner(value, m) for m, value in enumerate(messages, 1)]
    (middle_sum,) = call(add_kernel, (), middle_got, [block], cost=BESIDE)
    ahead, last, near, sums = call(
        functools.partial(plane_kernel, chips),
        (where,),
        (near, middle_sum, ahead, sums, far_out[-1], *got),
        [marked, marked, block, extra],
    )
    got = shifted(ahead, window)
    more = [shifted(sums, k * window) for k in middle]
    last = shifted(last, (planes - 1) * window)
    near, sums = call(near_kernel, (), (near, sums, got), [block, extra], cost=BESIDE)
    return call(final_kernel, (), (own, near, sums, last, *more), [block, block])


def solution(mesh):
    def run(*args):
        return tuple(per_device(*args))

    return jax.shard_map(
        run,
        mesh=mesh,
        in_specs=(P("blk", None), P("blk", None, None, None), P()),
        out_specs=(P("blk", None), P("blk", None)),
        check_vma=False,
    )
```

```python
import functools

import jax
import jax.numpy as jnp
from jax import lax
from jax.experimental import pallas as pl
from jax.experimental.pallas import tpu as pltpu
from jax.sharding import PartitionSpec as P

EXTRA = 8
VMEM_BYTES = 48 * 1024 * 1024
STEP = pl.CostEstimate(flops=4 * 10**7, bytes_accessed=0, transcendentals=0)
AFTER = pl.CostEstimate(flops=73 * 10**7, bytes_accessed=0, transcendentals=0)
BESIDE = pl.CostEstimate(flops=10**10, bytes_accessed=0, transcendentals=0)


def shifted(value, steps):
    count = lax.axis_size("blk")
    pairs = [(source, (source + steps) % count) for source in range(count)]
    return lax.ppermute(value, "blk", pairs)


def chip_partner(value, mask):
    count = lax.axis_size("blk")
    return lax.ppermute(value, "blk", [(source, source ^ (2 * mask)) for source in range(count)])


def core_partner(value):
    count = lax.axis_size("blk")
    return lax.ppermute(value, "blk", [(source, source ^ 1) for source in range(count)])


def split_two(values):
    high = values.astype(jnp.bfloat16)
    low = (values - high.astype(jnp.float32)).astype(jnp.bfloat16)
    return high, low


def place_of(place_ref, chips):
    place = place_ref[0]
    return (place // 2) & (chips - 1), place & 1


def keep_kernel(block_ref, out_ref):
    out_ref[...] = block_ref[...]


def split_kernel(tiles_ref, straight_ref, turned_ref):
    slots, rows, cols = tiles_ref.shape

    def visit(t):
        tile = tiles_ref[t]
        straight_ref[t, :, :cols], straight_ref[t, :, cols:] = split_two(tile)
        turned_ref[t, :, :rows], turned_ref[t, :, rows:] = split_two(tile.T)

    if slots <= 32:
        for t in range(slots):
            visit(t)
    else:
        lax.fori_loop(0, slots, lambda t, c: (visit(t), c)[1], 0)


def split_blocks_kernel(*refs):
    out_ref = refs[-1]
    cols = out_ref.shape[2] // 2
    for i, block in enumerate(refs[:-1]):
        out_ref[i, :, :cols], out_ref[i, :, cols:] = split_two(block[...])


def add_kernel(*refs):
    total = refs[0][...]
    for block in refs[1:-1]:
        total = total + block[...]
    refs[-1][...] = total


def near_kernel(near_ref, sums_ref, next_ref, near_out, sums_out):
    rows = near_ref.shape[0]
    near_out[...] = near_ref[...] + next_ref[:rows, :]
    sums_out[...] = sums_ref[...] + next_ref[rows:, :]


def steps_ahead(chip, mask, chips):
    return ((chip ^ mask) - chip) & (chips - 1)


def product_kernel(planes, chips, place_ref, table_ref, own_ref, *refs):
    window = 2 * chips
    far = refs[: planes - 1]
    even = refs[planes - 1 : planes + chips - 2]
    odd_ref, middle_ref, straight_ref, turned_ref, message_ref, kept_ref = refs[planes + chips - 2 : planes + chips + 4]
    far_out = refs[planes + chips + 4 : -4]
    parts, total, pairs_ref, fetched = refs[-4:]
    fetch = pltpu.make_async_copy(table_ref, pairs_ref, fetched)
    fetch.start()
    rows, cols = own_ref.shape
    chip, core = place_of(place_ref, chips)
    spare = jnp.where(core == 0, 1, window - 1)

    def put_parts(place, high, low):
        parts[place, :rows, :cols] = high
        parts[place, :rows, cols:] = low
        parts[place, rows:, :cols] = high
        parts[place, rows:, cols:] = jnp.zeros_like(low)

    blocks = []

    def put(place, block_ref):
        blocks.append((place, block_ref))
        put_parts(place, *split_two(block_ref[...]))

    put(0, own_ref)
    for k in (1, planes - 1):
        put(window - 1 + k, far[k - 1])
    for k in range(2, planes - 1):
        blocks.append((window - 1 + k, far[k - 1]))
        put_parts(window - 1 + k, middle_ref[k - 2, :, :cols], middle_ref[k - 2, :, cols:])
    for m in range(1, chips):
        ahead = 2 * steps_ahead(chip, m, chips)
        put(ahead, even[m - 1])
        put(ahead + 1 - 2 * core, odd_ref.at[m])
    put(spare, odd_ref.at[0])

    total[...] = jnp.zeros_like(total)
    fetch.wait()
    slots = straight_ref.shape[0]

    def product(split_ref, t, place):
        both = jnp.dot(split_ref[t], parts[place], preferred_element_type=jnp.float32)
        return both[:, :cols] + both[:, cols:]

    def visit(t, mirrored):
        row_place, col_place = pairs_ref[0, t], pairs_ref[1, t]
        total[row_place] += product(straight_ref, t, col_place)
        if mirrored:
            total[col_place] += product(turned_ref, t, row_place)

    visit(0, False)
    if slots <= 32:
        for t in range(1, slots - 1):
            visit(t, True)
    else:
        lax.fori_loop(1, slots - 1, lambda t, c: (visit(t, True), c)[1], 0)
    visit(slots - 1, False)

    dots = jnp.zeros((1, cols), jnp.float32)
    for place, block_ref in blocks:
        dots = dots + jnp.sum(block_ref[...] * total[place], axis=0, keepdims=True)
    own = own_ref[...]
    norm = jnp.sum(own * own, axis=0, keepdims=True)
    sums = jnp.concatenate([norm, dots, jnp.zeros((EXTRA - 2, cols), jnp.float32)], axis=0)
    message_ref[:rows, :] = total[spare]
    kept_ref[0] = total[0]
    for m in range(1, chips):
        ahead = 2 * steps_ahead(chip, m, chips)
        message_ref[m * rows : (m + 1) * rows, :] = total[ahead + 1 - 2 * core]
        kept_ref[m] = total[ahead]
    message_ref[chips * rows :, :] = sums
    kept_ref[chips] = total[window]
    for k in range(2, planes):
        far_out[k - 2][...] = total[window - 1 + k]


def pair_kernel(chips, place_ref, sent_ref, kept_ref, got_ref, *outs):
    messages = outs[: chips - 1]
    near_ref, next_ref, sums_ref = outs[chips - 1 :]
    rows = kept_ref.shape[1]
    core = place_of(place_ref, chips)[1]
    sums = sent_ref[chips * rows :, :] + got_ref[chips * rows :, :]
    for m in range(1, chips):
        messages[m - 1][:rows, :] = kept_ref[m] + got_ref[m * rows : (m + 1) * rows, :]
        messages[m - 1][rows:, :] = sums
    spare = got_ref[:rows, :]
    near_ref[...] = kept_ref[0] + jnp.where(core == 1, spare, 0.0)
    next_ref[...] = kept_ref[chips] + jnp.where(core == 0, spare, 0.0)
    sums_ref[...] = sums


def plane_kernel(chips, place_ref, near_ref, next_ref, sums_ref, last_ref, *refs):
    got = refs[: chips - 1]
    next_out, last_out, near_out, sums_out = refs[chips - 1 :]
    rows = near_ref.shape[0]
    chip = place_of(place_ref, chips)[0]
    near, ahead, sums = near_ref[...], next_ref[...], sums_ref[...]
    for m in range(1, chips):
        block = got[m - 1][:rows, :]
        same = (chip ^ m) < chip
        near = near + jnp.where(same, block, 0.0)
        ahead = ahead + jnp.where(same, 0.0, block)
        sums = sums + got[m - 1][rows:, :]
    near_out[...] = near
    sums_out[...] = sums
    next_out[:rows, :] = ahead
    last_out[:rows, :] = last_ref[...]
    for message in (next_out, last_out):
        message[rows:, :] = sums


def final_kernel(right_ref, near_ref, middle_ref, sums_ref, last_ref, *refs):
    solution_ref, residual_ref = refs[-2:]
    rows = near_ref.shape[0]
    image = near_ref[...] + middle_ref[...] + last_ref[:rows, :]
    sums = sums_ref[...] + last_ref[rows:, :]
    for more in refs[:-2]:
        sums = sums + more[...]
    step_len = sums[0:1, :] / sums[1:2, :]
    right = right_ref[...]
    solution_ref[...] = step_len * right
    residual_ref[...] = right - step_len * image


def call(kernel, smem, operands, outs, scratch=(), cost=None):
    vmem = pl.BlockSpec(memory_space=pltpu.VMEM)
    return pl.pallas_call(
        kernel,
        in_specs=[pl.BlockSpec(memory_space=pltpu.SMEM)] * len(smem) + [vmem] * len(operands),
        out_specs=[vmem] * len(outs),
        out_shape=[jax.ShapeDtypeStruct(shape, kind) for shape, kind in outs],
        scratch_shapes=list(scratch),
        cost_estimate=cost,
        compiler_params=pltpu.CompilerParams(vmem_limit_bytes=VMEM_BYTES),
    )(*smem, *operands)


def per_device(right_side, kernel_tiles, route_pairs):
    count = lax.axis_size("blk")
    window = max(8, min(16, count // 8))
    planes, chips = count // window, window // 2
    rows, cols = right_side.shape
    slots = kernel_tiles.shape[1]
    cover_len = window + planes - 1
    place = lax.axis_index("blk").astype(jnp.int32)
    chip, core = place % window // 2, place % 2
    where = place[None]
    single, half = jnp.float32, jnp.bfloat16

    block, marked, extra = ((rows, cols), single), ((rows + EXTRA, cols), single), ((EXTRA, cols), single)
    (own,) = call(keep_kernel, (), (right_side,), [block])
    straight, turned = call(
        split_kernel,
        (),
        (kernel_tiles[0],),
        [((slots, rows, 2 * cols), half), ((slots, cols, 2 * rows), half)],
        cost=BESIDE,
    )
    far = {k: shifted(right_side, -k * window) for k in (planes - 1, *range(1, planes - 1))}
    own, far[planes - 1], far[1] = lax.optimization_barrier((own, far[planes - 1], far[1]))
    middle = range(2, planes - 1)
    (middle_parts,) = call(
        split_blocks_kernel, (), [far[k] for k in middle], [((len(middle), rows, 2 * cols), half)], cost=BESIDE
    )
    even = [chip_partner(jnp.where((chip ^ m) < chip, own, far[1]), m) for m in range(1, chips)]
    sent = jnp.stack([jnp.where(core == 0, far[1], own)] + even)
    sent, middle_parts = lax.optimization_barrier((sent, middle_parts))
    odd = core_partner(sent)

    sent, kept, *far_out = call(
        functools.partial(product_kernel, planes, chips),
        (where,),
        (route_pairs.T, own, *[far[k] for k in range(1, planes)], *even, odd, middle_parts, straight, turned),
        [((chips * rows + EXTRA, cols), single), ((chips + 1, rows, cols), single)] + [block] * (planes - 2),
        (
            pltpu.VMEM((cover_len, 2 * rows, 2 * cols), half),
            pltpu.VMEM((cover_len, rows, cols), single),
            pltpu.SMEM((2, slots), jnp.int32),
            pltpu.SemaphoreType.DMA,
        ),
    )
    got = core_partner(sent)
    *messages, near, ahead, sums = call(
        functools.partial(pair_kernel, chips), (where,), (sent, kept, got), [marked] * (chips - 1) + [block, block, extra]
    )
    middle_got = [shifted(far_out[k - 2], k * window) for k in middle]
    got = [chip_partner(value, m) for m, value in enumerate(messages, 1)]
    (middle_sum,) = call(add_kernel, (), middle_got, [block], cost=AFTER)
    ahead, last, near, sums = call(
        functools.partial(plane_kernel, chips),
        (where,),
        (near, ahead, sums, far_out[-1], *got),
        [marked, marked, block, extra],
    )
    got = shifted(ahead, window)
    more = [shifted(sums, k * window) for k in middle]
    last = shifted(last, (planes - 1) * window)
    near, sums = call(near_kernel, (), (near, sums, got), [block, extra], cost=STEP)
    return call(final_kernel, (), (own, near, middle_sum, sums, last, *more), [block, block])


def solution(mesh):
    def run(*args):
        return tuple(per_device(*args))

    return jax.shard_map(
        run,
        mesh=mesh,
        in_specs=(P("blk", None), P("blk", None, None, None), P()),
        out_specs=(P("blk", None), P("blk", None)),
        check_vma=False,
    )
```

```python
import functools

import jax
import jax.numpy as jnp
from jax import lax
from jax.experimental import pallas as pl
from jax.experimental.pallas import tpu as pltpu
from jax.sharding import PartitionSpec as P

EXTRA = 8
VMEM_BYTES = 48 * 1024 * 1024
BESIDE = pl.CostEstimate(flops=10**10, bytes_accessed=0, transcendentals=0)


def shifted(value, steps):
    count = lax.axis_size("blk")
    pairs = [(source, (source + steps) % count) for source in range(count)]
    return lax.ppermute(value, "blk", pairs)


def chip_partner(value, mask):
    count = lax.axis_size("blk")
    return lax.ppermute(value, "blk", [(source, source ^ (2 * mask)) for source in range(count)])


def core_partner(value):
    count = lax.axis_size("blk")
    return lax.ppermute(value, "blk", [(source, source ^ 1) for source in range(count)])


def split_two(values):
    high = values.astype(jnp.bfloat16)
    low = (values - high.astype(jnp.float32)).astype(jnp.bfloat16)
    return high, low


def place_of(place_ref, chips):
    place = place_ref[0]
    return (place // 2) & (chips - 1), place & 1


def keep_kernel(block_ref, out_ref):
    out_ref[...] = block_ref[...]


def split_kernel(tiles_ref, straight_ref, turned_ref):
    slots, rows, cols = tiles_ref.shape

    def visit(t):
        tile = tiles_ref[t]
        straight_ref[t, :, :cols], straight_ref[t, :, cols:] = split_two(tile)
        turned_ref[t, :, :rows], turned_ref[t, :, rows:] = split_two(tile.T)

    if slots <= 32:
        for t in range(slots):
            visit(t)
    else:
        lax.fori_loop(0, slots, lambda t, c: (visit(t), c)[1], 0)


def split_blocks_kernel(*refs):
    out_ref = refs[-1]
    cols = out_ref.shape[2] // 2
    for i, block in enumerate(refs[:-1]):
        out_ref[i, :, :cols], out_ref[i, :, cols:] = split_two(block[...])


def add_kernel(*refs):
    total = refs[0][...]
    for block in refs[1:-1]:
        total = total + block[...]
    refs[-1][...] = total


def near_kernel(near_ref, sums_ref, next_ref, near_out, sums_out):
    rows = near_ref.shape[0]
    near_out[...] = near_ref[...] + next_ref[:rows, :]
    sums_out[...] = sums_ref[...] + next_ref[rows:, :]


def steps_ahead(chip, mask, chips):
    return ((chip ^ mask) - chip) & (chips - 1)


def product_kernel(planes, chips, place_ref, table_ref, own_ref, *refs):
    window = 2 * chips
    far = refs[: planes - 1]
    even = refs[planes - 1 : planes + chips - 2]
    odd_ref, middle_ref, straight_ref, turned_ref, message_ref, kept_ref = refs[planes + chips - 2 : planes + chips + 4]
    far_out = refs[planes + chips + 4 : -4]
    parts, total, pairs_ref, fetched = refs[-4:]
    fetch = pltpu.make_async_copy(table_ref, pairs_ref, fetched)
    fetch.start()
    rows, cols = own_ref.shape
    chip, core = place_of(place_ref, chips)
    spare = jnp.where(core == 0, 1, window - 1)

    def put_parts(place, high, low):
        parts[place, :rows, :cols] = high
        parts[place, :rows, cols:] = low
        parts[place, rows:, :cols] = high
        parts[place, rows:, cols:] = jnp.zeros_like(low)

    blocks = []

    def put(place, block_ref):
        blocks.append((place, block_ref))
        put_parts(place, *split_two(block_ref[...]))

    put(0, own_ref)
    for k in (1, planes - 1):
        put(window - 1 + k, far[k - 1])
    for k in range(2, planes - 1):
        blocks.append((window - 1 + k, far[k - 1]))
        put_parts(window - 1 + k, middle_ref[k - 2, :, :cols], middle_ref[k - 2, :, cols:])
    for m in range(1, chips):
        ahead = 2 * steps_ahead(chip, m, chips)
        put(ahead, even[m - 1])
        put(ahead + 1 - 2 * core, odd_ref.at[m])
    put(spare, odd_ref.at[0])

    total[...] = jnp.zeros_like(total)
    fetch.wait()
    slots = straight_ref.shape[0]

    def product(split_ref, t, place):
        both = jnp.dot(split_ref[t], parts[place], preferred_element_type=jnp.float32)
        return both[:, :cols] + both[:, cols:]

    def visit(t, mirrored):
        row_place, col_place = pairs_ref[0, t], pairs_ref[1, t]
        total[row_place] += product(straight_ref, t, col_place)
        if mirrored:
            total[col_place] += product(turned_ref, t, row_place)

    visit(0, False)
    if slots <= 32:
        for t in range(1, slots - 1):
            visit(t, True)
    else:
        lax.fori_loop(1, slots - 1, lambda t, c: (visit(t, True), c)[1], 0)
    visit(slots - 1, False)

    dots = jnp.zeros((1, cols), jnp.float32)
    for place, block_ref in blocks:
        dots = dots + jnp.sum(block_ref[...] * total[place], axis=0, keepdims=True)
    own = own_ref[...]
    norm = jnp.sum(own * own, axis=0, keepdims=True)
    sums = jnp.concatenate([norm, dots, jnp.zeros((EXTRA - 2, cols), jnp.float32)], axis=0)
    message_ref[:rows, :] = total[spare]
    kept_ref[0] = total[0]
    for m in range(1, chips):
        ahead = 2 * steps_ahead(chip, m, chips)
        message_ref[m * rows : (m + 1) * rows, :] = total[ahead + 1 - 2 * core]
        kept_ref[m] = total[ahead]
    message_ref[chips * rows :, :] = sums
    kept_ref[chips] = total[window]
    for k in range(2, planes):
        far_out[k - 2][...] = total[window - 1 + k]


def pair_kernel(chips, place_ref, sent_ref, kept_ref, got_ref, *outs):
    messages = outs[: chips - 1]
    near_ref, next_ref, sums_ref = outs[chips - 1 :]
    rows = kept_ref.shape[1]
    core = place_of(place_ref, chips)[1]
    sums = sent_ref[chips * rows :, :] + got_ref[chips * rows :, :]
    for m in range(1, chips):
        messages[m - 1][:rows, :] = kept_ref[m] + got_ref[m * rows : (m + 1) * rows, :]
        messages[m - 1][rows:, :] = sums
    spare = got_ref[:rows, :]
    near_ref[...] = kept_ref[0] + jnp.where(core == 1, spare, 0.0)
    next_ref[...] = kept_ref[chips] + jnp.where(core == 0, spare, 0.0)
    sums_ref[...] = sums


def plane_kernel(chips, place_ref, near_ref, middle_ref, next_ref, sums_ref, last_ref, *refs):
    got = refs[: chips - 1][::-1]
    next_out, last_out, near_out, sums_out = refs[chips - 1 :]
    rows = near_ref.shape[0]
    chip = place_of(place_ref, chips)[0]
    near, ahead, sums = near_ref[...] + middle_ref[...], next_ref[...], sums_ref[...]
    for m in range(1, chips):
        block = got[m - 1][:rows, :]
        same = (chip ^ m) < chip
        near = near + jnp.where(same, block, 0.0)
        ahead = ahead + jnp.where(same, 0.0, block)
        sums = sums + got[m - 1][rows:, :]
    near_out[...] = near
    sums_out[...] = sums
    next_out[:rows, :] = ahead
    last_out[:rows, :] = last_ref[...]
    for message in (next_out, last_out):
        message[rows:, :] = sums


def final_kernel(right_ref, near_ref, sums_ref, last_ref, *refs):
    solution_ref, residual_ref = refs[-2:]
    rows = near_ref.shape[0]
    image = near_ref[...] + last_ref[:rows, :]
    sums = sums_ref[...] + last_ref[rows:, :]
    for more in refs[:-2]:
        sums = sums + more[...]
    step_len = sums[0:1, :] / sums[1:2, :]
    right = right_ref[...]
    solution_ref[...] = step_len * right
    residual_ref[...] = right - step_len * image


def call(kernel, smem, operands, outs, scratch=(), cost=None):
    vmem = pl.BlockSpec(memory_space=pltpu.VMEM)
    return pl.pallas_call(
        kernel,
        in_specs=[pl.BlockSpec(memory_space=pltpu.SMEM)] * len(smem) + [vmem] * len(operands),
        out_specs=[vmem] * len(outs),
        out_shape=[jax.ShapeDtypeStruct(shape, kind) for shape, kind in outs],
        scratch_shapes=list(scratch),
        cost_estimate=cost,
        compiler_params=pltpu.CompilerParams(vmem_limit_bytes=VMEM_BYTES),
    )(*smem, *operands)


def per_device(right_side, kernel_tiles, route_pairs):
    count = lax.axis_size("blk")
    window = max(8, min(16, count // 8))
    planes, chips = count // window, window // 2
    rows, cols = right_side.shape
    slots = kernel_tiles.shape[1]
    cover_len = window + planes - 1
    place = lax.axis_index("blk").astype(jnp.int32)
    chip, core = place % window // 2, place % 2
    where = place[None]
    single, half = jnp.float32, jnp.bfloat16

    block, marked, extra = ((rows, cols), single), ((rows + EXTRA, cols), single), ((EXTRA, cols), single)
    (own,) = call(keep_kernel, (), (right_side,), [block])
    straight, turned = call(
        split_kernel,
        (),
        (kernel_tiles[0],),
        [((slots, rows, 2 * cols), half), ((slots, cols, 2 * rows), half)],
        cost=BESIDE,
    )
    far = {k: shifted(right_side, -k * window) for k in (planes - 1, *range(1, planes - 1))}
    own, far[planes - 1], far[1] = lax.optimization_barrier((own, far[planes - 1], far[1]))
    middle = range(2, planes - 1)
    (middle_parts,) = call(
        split_blocks_kernel, (), [far[k] for k in middle], [((len(middle), rows, 2 * cols), half)], cost=BESIDE
    )
    even = [chip_partner(jnp.where((chip ^ m) < chip, own, far[1]), m) for m in range(1, chips)]
    sent = jnp.stack([jnp.where(core == 0, far[1], own)] + even)
    sent, middle_parts = lax.optimization_barrier((sent, middle_parts))
    odd = core_partner(sent)

    sent, kept, *far_out = call(
        functools.partial(product_kernel, planes, chips),
        (where,),
        (route_pairs.T, own, *[far[k] for k in range(1, planes)], *even, odd, middle_parts, straight, turned),
        [((chips * rows + EXTRA, cols), single), ((chips + 1, rows, cols), single)] + [block] * (planes - 2),
        (
            pltpu.VMEM((cover_len, 2 * rows, 2 * cols), half),
            pltpu.VMEM((cover_len, rows, cols), single),
            pltpu.SMEM((2, slots), jnp.int32),
            pltpu.SemaphoreType.DMA,
        ),
    )
    got = core_partner(sent)
    *messages, near, ahead, sums = call(
        functools.partial(pair_kernel, chips), (where,), (sent, kept, got), [marked] * (chips - 1) + [block, block, extra]
    )
    middle_got = [shifted(far_out[k - 2], k * window) for k in middle]
    got = [chip_partner(value, m) for m, value in enumerate(messages, 1)]
    (middle_sum,) = call(add_kernel, (), middle_got, [block], cost=BESIDE)
    ahead, last, near, sums = call(
        functools.partial(plane_kernel, chips),
        (where,),
        (near, middle_sum, ahead, sums, far_out[-1], *got[::-1]),
        [marked, marked, block, extra],
    )
    got = shifted(ahead, window)
    more = [shifted(sums, k * window) for k in middle]
    last = shifted(last, (planes - 1) * window)
    near, sums = call(near_kernel, (), (near, sums, got), [block, extra], cost=BESIDE)
    return call(final_kernel, (), (own, near, sums, last, *more), [block, block])


def solution(mesh):
    def run(*args):
        return tuple(per_device(*args))

    return jax.shard_map(
        run,
        mesh=mesh,
        in_specs=(P("blk", None), P("blk", None, None, None), P()),
        out_specs=(P("blk", None), P("blk", None)),
        check_vma=False,
    )
```

```python
import functools

import jax
import jax.numpy as jnp
from jax import lax
from jax.experimental import pallas as pl
from jax.experimental.pallas import tpu as pltpu
from jax.sharding import PartitionSpec as P

EXTRA = 8
VMEM_BYTES = 48 * 1024 * 1024
STEP = pl.CostEstimate(flops=4 * 10**7, bytes_accessed=0, transcendentals=0)
AFTER = pl.CostEstimate(flops=73 * 10**7, bytes_accessed=0, transcendentals=0)
BESIDE = pl.CostEstimate(flops=10**10, bytes_accessed=0, transcendentals=0)


def shifted(value, steps):
    count = lax.axis_size("blk")
    pairs = [(source, (source + steps) % count) for source in range(count)]
    return lax.ppermute(value, "blk", pairs)


def chip_partner(value, mask):
    count = lax.axis_size("blk")
    return lax.ppermute(value, "blk", [(source, source ^ (2 * mask)) for source in range(count)])


def core_partner(value):
    count = lax.axis_size("blk")
    return lax.ppermute(value, "blk", [(source, source ^ 1) for source in range(count)])


def split_two(values):
    high = values.astype(jnp.bfloat16)
    low = (values - high.astype(jnp.float32)).astype(jnp.bfloat16)
    return high, low


def place_of(place_ref, chips):
    place = place_ref[0]
    return (place // 2) & (chips - 1), place & 1


def keep_kernel(block_ref, out_ref):
    out_ref[...] = block_ref[...]


def split_kernel(tiles_ref, straight_ref, turned_ref):
    slots, rows, cols = tiles_ref.shape

    def visit(t):
        tile = tiles_ref[t]
        straight_ref[t, :, :cols], straight_ref[t, :, cols:] = split_two(tile)
        turned_ref[t, :, :rows], turned_ref[t, :, rows:] = split_two(tile.T)

    if slots <= 32:
        for t in range(slots):
            visit(t)
    else:
        lax.fori_loop(0, slots, lambda t, c: (visit(t), c)[1], 0)


def split_blocks_kernel(*refs):
    out_ref = refs[-1]
    cols = out_ref.shape[2] // 2
    for i, block in enumerate(refs[:-1]):
        out_ref[i, :, :cols], out_ref[i, :, cols:] = split_two(block[...])


def add_kernel(*refs):
    total = refs[0][...]
    for block in refs[1:-1]:
        total = total + block[...]
    refs[-1][...] = total


def near_kernel(near_ref, sums_ref, next_ref, near_out, sums_out):
    rows = near_ref.shape[0]
    near_out[...] = near_ref[...] + next_ref[:rows, :]
    sums_out[...] = sums_ref[...] + next_ref[rows:, :]


def steps_ahead(chip, mask, chips):
    return ((chip ^ mask) - chip) & (chips - 1)


def product_kernel(planes, chips, place_ref, table_ref, own_ref, *refs):
    window = 2 * chips
    far = refs[: planes - 1]
    even = refs[planes - 1 : planes + chips - 2]
    odd_ref, middle_ref, straight_ref, turned_ref, message_ref, kept_ref = refs[planes + chips - 2 : planes + chips + 4]
    far_out = refs[planes + chips + 4 : -4]
    parts, total, pairs_ref, fetched = refs[-4:]
    fetch = pltpu.make_async_copy(table_ref, pairs_ref, fetched)
    fetch.start()
    rows, cols = own_ref.shape
    chip, core = place_of(place_ref, chips)
    spare = jnp.where(core == 0, 1, window - 1)

    def put_parts(place, high, low):
        parts[place, :rows, :cols] = high
        parts[place, :rows, cols:] = low
        parts[place, rows:, :cols] = high
        parts[place, rows:, cols:] = jnp.zeros_like(low)

    blocks = []

    def put(place, block_ref):
        blocks.append((place, block_ref))
        put_parts(place, *split_two(block_ref[...]))

    put(0, own_ref)
    for k in (1, planes - 1):
        put(window - 1 + k, far[k - 1])
    for k in range(2, planes - 1):
        blocks.append((window - 1 + k, far[k - 1]))
        put_parts(window - 1 + k, middle_ref[k - 2, :, :cols], middle_ref[k - 2, :, cols:])
    for m in range(1, chips):
        ahead = 2 * steps_ahead(chip, m, chips)
        put(ahead, even[m - 1])
        put(ahead + 1 - 2 * core, odd_ref.at[m])
    put(spare, odd_ref.at[0])

    total[...] = jnp.zeros_like(total)
    fetch.wait()
    slots = straight_ref.shape[0]

    def product(split_ref, t, place):
        both = jnp.dot(split_ref[t], parts[place], preferred_element_type=jnp.float32)
        return both[:, :cols] + both[:, cols:]

    def visit(t, mirrored):
        row_place, col_place = pairs_ref[0, t], pairs_ref[1, t]
        total[row_place] += product(straight_ref, t, col_place)
        if mirrored:
            total[col_place] += product(turned_ref, t, row_place)

    visit(0, False)
    if slots <= 32:
        for t in range(1, slots - 1):
            visit(t, True)
    else:
        lax.fori_loop(1, slots - 1, lambda t, c: (visit(t, True), c)[1], 0)
    visit(slots - 1, False)

    dots = jnp.zeros((1, cols), jnp.float32)
    for place, block_ref in blocks:
        dots = dots + jnp.sum(block_ref[...] * total[place], axis=0, keepdims=True)
    own = own_ref[...]
    norm = jnp.sum(own * own, axis=0, keepdims=True)
    sums = jnp.concatenate([norm, dots, jnp.zeros((EXTRA - 2, cols), jnp.float32)], axis=0)
    message_ref[:rows, :] = total[spare]
    kept_ref[0] = total[0]
    for m in range(1, chips):
        ahead = 2 * steps_ahead(chip, m, chips)
        message_ref[m * rows : (m + 1) * rows, :] = total[ahead + 1 - 2 * core]
        kept_ref[m] = total[ahead]
    message_ref[chips * rows :, :] = sums
    kept_ref[chips] = total[window]
    for k in range(2, planes):
        far_out[k - 2][...] = total[window - 1 + k]


def pair_kernel(chips, place_ref, sent_ref, kept_ref, got_ref, *outs):
    messages = outs[: chips - 1]
    near_ref, next_ref, sums_ref = outs[chips - 1 :]
    rows = kept_ref.shape[1]
    core = place_of(place_ref, chips)[1]
    sums = sent_ref[chips * rows :, :] + got_ref[chips * rows :, :]
    for m in range(1, chips):
        messages[m - 1][:rows, :] = kept_ref[m] + got_ref[m * rows : (m + 1) * rows, :]
        messages[m - 1][rows:, :] = sums
    spare = got_ref[:rows, :]
    near_ref[...] = kept_ref[0] + jnp.where(core == 1, spare, 0.0)
    next_ref[...] = kept_ref[chips] + jnp.where(core == 0, spare, 0.0)
    sums_ref[...] = sums


def plane_kernel(chips, place_ref, near_ref, next_ref, sums_ref, last_ref, *refs):
    got = refs[: chips - 1][::-1]
    next_out, last_out, near_out, sums_out = refs[chips - 1 :]
    rows = near_ref.shape[0]
    chip = place_of(place_ref, chips)[0]
    near, ahead, sums = near_ref[...], next_ref[...], sums_ref[...]
    for m in range(1, chips):
        block = got[m - 1][:rows, :]
        same = (chip ^ m) < chip
        near = near + jnp.where(same, block, 0.0)
        ahead = ahead + jnp.where(same, 0.0, block)
        sums = sums + got[m - 1][rows:, :]
    near_out[...] = near
    sums_out[...] = sums
    next_out[:rows, :] = ahead
    last_out[:rows, :] = last_ref[...]
    for message in (next_out, last_out):
        message[rows:, :] = sums


def final_kernel(right_ref, near_ref, middle_ref, sums_ref, last_ref, *refs):
    solution_ref, residual_ref = refs[-2:]
    rows = near_ref.shape[0]
    image = near_ref[...] + middle_ref[...] + last_ref[:rows, :]
    sums = sums_ref[...] + last_ref[rows:, :]
    for more in refs[:-2]:
        sums = sums + more[...]
    step_len = sums[0:1, :] / sums[1:2, :]
    right = right_ref[...]
    solution_ref[...] = step_len * right
    residual_ref[...] = right - step_len * image


def call(kernel, smem, operands, outs, scratch=(), cost=None):
    vmem = pl.BlockSpec(memory_space=pltpu.VMEM)
    return pl.pallas_call(
        kernel,
        in_specs=[pl.BlockSpec(memory_space=pltpu.SMEM)] * len(smem) + [vmem] * len(operands),
        out_specs=[vmem] * len(outs),
        out_shape=[jax.ShapeDtypeStruct(shape, kind) for shape, kind in outs],
        scratch_shapes=list(scratch),
        cost_estimate=cost,
        compiler_params=pltpu.CompilerParams(vmem_limit_bytes=VMEM_BYTES),
    )(*smem, *operands)


def per_device(right_side, kernel_tiles, route_pairs):
    count = lax.axis_size("blk")
    window = max(8, min(16, count // 8))
    planes, chips = count // window, window // 2
    rows, cols = right_side.shape
    slots = kernel_tiles.shape[1]
    cover_len = window + planes - 1
    place = lax.axis_index("blk").astype(jnp.int32)
    chip, core = place % window // 2, place % 2
    where = place[None]
    single, half = jnp.float32, jnp.bfloat16

    block, marked, extra = ((rows, cols), single), ((rows + EXTRA, cols), single), ((EXTRA, cols), single)
    (own,) = call(keep_kernel, (), (right_side,), [block])
    straight, turned = call(
        split_kernel,
        (),
        (kernel_tiles[0],),
        [((slots, rows, 2 * cols), half), ((slots, cols, 2 * rows), half)],
        cost=BESIDE,
    )
    far = {k: shifted(right_side, -k * window) for k in (planes - 1, *range(1, planes - 1))}
    own, far[planes - 1], far[1] = lax.optimization_barrier((own, far[planes - 1], far[1]))
    middle = range(2, planes - 1)
    (middle_parts,) = call(
        split_blocks_kernel, (), [far[k] for k in middle], [((len(middle), rows, 2 * cols), half)], cost=BESIDE
    )
    even = [chip_partner(jnp.where((chip ^ m) < chip, own, far[1]), m) for m in range(1, chips)]
    sent = jnp.stack([jnp.where(core == 0, far[1], own)] + even)
    sent, middle_parts = lax.optimization_barrier((sent, middle_parts))
    odd = core_partner(sent)

    sent, kept, *far_out = call(
        functools.partial(product_kernel, planes, chips),
        (where,),
        (route_pairs.T, own, *[far[k] for k in range(1, planes)], *even, odd, middle_parts, straight, turned),
        [((chips * rows + EXTRA, cols), single), ((chips + 1, rows, cols), single)] + [block] * (planes - 2),
        (
            pltpu.VMEM((cover_len, 2 * rows, 2 * cols), half),
            pltpu.VMEM((cover_len, rows, cols), single),
            pltpu.SMEM((2, slots), jnp.int32),
            pltpu.SemaphoreType.DMA,
        ),
    )
    got = core_partner(sent)
    *messages, near, ahead, sums = call(
        functools.partial(pair_kernel, chips), (where,), (sent, kept, got), [marked] * (chips - 1) + [block, block, extra]
    )
    middle_got = [shifted(far_out[k - 2], k * window) for k in middle]
    got = [chip_partner(value, m) for m, value in enumerate(messages, 1)]
    (middle_sum,) = call(add_kernel, (), middle_got, [block], cost=AFTER)
    ahead, last, near, sums = call(
        functools.partial(plane_kernel, chips),
        (where,),
        (near, ahead, sums, far_out[-1], *got[::-1]),
        [marked, marked, block, extra],
    )
    got = shifted(ahead, window)
    more = [shifted(sums, k * window) for k in middle]
    last = shifted(last, (planes - 1) * window)
    near, sums = call(near_kernel, (), (near, sums, got), [block, extra], cost=STEP)
    return call(final_kernel, (), (own, near, middle_sum, sums, last, *more), [block, block])


def solution(mesh):
    def run(*args):
        return tuple(per_device(*args))

    return jax.shard_map(
        run,
        mesh=mesh,
        in_specs=(P("blk", None), P("blk", None, None, None), P()),
        out_specs=(P("blk", None), P("blk", None)),
        check_vma=False,
    )
```
